32 devices in a mesh: batch: 16 (over z, x, core), blk: 2 (over y).
Axes of the slice: x: 2, y: 2, z: 4, core: 2. Of those that a mesh axis runs over, the one named last changes fastest.
Arguments:
- hidden_in: bfloat16 [32, 2048, 768], P('batch', 'blk'), may hold values from -6 to 6
- lengths: int32 [32], P('batch'), may hold values from 256 to 2048, as said below
- cot_out: bfloat16 [32, 2048, 768], P('batch', 'blk'), may hold values from -6 to 6
- cot_cls: bfloat16 [32, 768], P('batch'), may hold values from -6 to 6
- w_query: bfloat16 [768, 768], P('batch', 'blk'), may hold values from -0.3125 to 0.3125
- w_key: bfloat16 [768, 768], P('batch', 'blk'), may hold values from -0.3125 to 0.3125
- w_value: bfloat16 [768, 768], P('batch', 'blk'), may hold values from -0.21875 to 0.21875
- w_out: bfloat16 [768, 768], P('batch', 'blk'), may hold values from -0.875 to 0.875
- w_inner: bfloat16 [768, 3072], P('batch', 'blk'), may hold values from -0.21875 to 0.21875
- w_outer: bfloat16 [3072, 768], P('batch', 'blk'), may hold values from -0.109375 to 0.109375
- b_query: bfloat16 [768], P('blk'), may hold values from -1 to 1
- b_value: bfloat16 [768], P('blk'), may hold values from -1 to 1
- b_out: bfloat16 [768], P('blk'), may hold values from -1 to 1
- norm1_gain: bfloat16 [768], P('blk'), may hold values from 0.5 to 1.5
- norm1_shift: bfloat16 [768], P('blk'), may hold values from -1 to 1
- b_inner: bfloat16 [3072], P('blk'), may hold values from -1 to 1
- b_outer: bfloat16 [768], P('blk'), may hold values from -1 to 1
- norm2_gain: bfloat16 [768], P('blk'), may hold values from 0.5 to 1.5
- norm2_shift: bfloat16 [768], P('blk'), may hold values from -1 to 1
Outputs:
- layer_out: bfloat16 [32, 2048, 768], P('batch', 'blk')
- cls_embed: bfloat16 [32, 768], P('batch', 'blk')
- grad_input: float32 [32, 2048, 768], P('batch', 'blk')
- grad_w_query: float32 [768, 768], P('batch', 'blk')
- grad_w_key: float32 [768, 768], P('batch', 'blk')
- grad_w_value: float32 [768, 768], P('batch', 'blk')
- grad_w_out: float32 [768, 768], P('batch', 'blk')
- grad_w_inner: float32 [768, 3072], P('batch', 'blk')
- grad_w_outer: float32 [3072, 768], P('batch', 'blk')
- grad_b_query: float32 [768], P('blk')
- grad_b_value: float32 [768], P('blk')
- grad_b_out: float32 [768], P('blk')
- grad_norm1_gain: float32 [768], P('blk')
- grad_norm1_shift: float32 [768], P('blk')
- grad_b_inner: float32 [3072], P('blk')
- grad_b_outer: float32 [768], P('blk')
- grad_norm2_gain: float32 [768], P('blk')
- grad_norm2_shift: float32 [768], P('blk')
The draws below stay inside these ranges and needn't reach their ends.
Inputs may be any that keep to these rules, and one draw needn't show every extreme that they name: Passage p has lengths[p] live tokens, its first ones; the others are padding. In every group of 2 passages that share one index of batch, at least one passage is live at all 2048 positions.
All inputs are finite; a program needn't handle non-finite values.
Results may differ from the reference program's by a relative error of at most 0.024.
Values may be sent and summed in bfloat16 or wider, within the bound.
No kernel may reach another device: no remote copies, remote signals or barrier semaphores. Data moves between devices by JAX's collectives and lax.ppermute only.
A program may use at most 640 MiB of HBM per device.

```python
import jax
import jax.numpy as jnp
from jax import lax

D = 768
HEADS = 12
HDIM = 64
FF = 3072
LENGTH = 2048
SEQ_GRP = 2
NSEQ = 32
QBLK = 512


def draw_lengths(key, part):
    key = jax.random.fold_in(key, 7)
    base_key, pick_key, short_key = jax.random.split(key, 3)
    shortest = max(1, LENGTH // 8)
    group_count = NSEQ // SEQ_GRP
    base_len = jax.random.randint(base_key, (NSEQ,), shortest, LENGTH + 1)
    pick_slot = jax.random.randint(pick_key, (group_count,), 0, SEQ_GRP)
    short_group = jax.random.randint(short_key, (), 0, group_count)
    short_slot = (pick_slot[short_group] + 1) % SEQ_GRP
    short_index = short_group * SEQ_GRP + short_slot
    positions = jnp.arange(NSEQ, dtype=jnp.int32)
    within_group = positions % SEQ_GRP
    chosen_slot = jnp.repeat(pick_slot, SEQ_GRP)
    ragged = jnp.where(positions == short_index, shortest, base_len)
    return jnp.where(within_group == chosen_slot, LENGTH, ragged).astype(jnp.int32)


def shard_levels(stream_key, extent, cuts, low, largest):
    def one(axis_at, shards_of):
        draws = jax.random.uniform(jax.random.fold_in(jax.random.fold_in(stream_key, 6), axis_at), (shards_of,), jnp.float32, low / len(cuts), largest / len(cuts))
        return jnp.repeat(jnp.exp(draws), extent[axis_at] // shards_of).reshape((-1,) + (1,) * (len(extent) - axis_at - 1))

    level = one(*cuts[0])
    for cut in cuts[1:]:
        level = level * one(*cut)
    return level


def gaussian(key, shape, deviation, most, pieces=(), kind=jnp.bfloat16):
    entries = deviation * jax.random.normal(key, shape, jnp.float32)
    if pieces:
        entries = entries * shard_levels(key, shape, pieces, -0.22, 0.18)
    return jnp.clip(entries, -most, most).astype(kind)


def setup_inputs(seed: int = 0) -> dict:
    key_of = jax.random.split(jax.random.key(seed), 20)
    hidden_in = gaussian(key_of[0], (NSEQ, LENGTH, D), 1.0, 6.0, ((0, 16), (1, 2)))
    lengths = draw_lengths(jax.random.fold_in(key_of[19], 71), 0)
    cot_out = gaussian(key_of[2], (NSEQ, LENGTH, D), 1.0, 6.0, ((0, 16), (1, 2)))
    cot_cls = gaussian(key_of[3], (NSEQ, D), 1.0, 6.0, ((0, 16),))
    w_query = gaussian(key_of[4], (D, D), (D // 2) ** -0.5, 0.3125, ((0, 16), (1, 2)))
    w_key = gaussian(key_of[5], (D, D), (D // 2) ** -0.5, 0.3125, ((0, 16), (1, 2)))
    w_value = gaussian(key_of[6], (D, D), D ** -0.5, 0.21875, ((0, 16), (1, 2)))
    w_out = gaussian(key_of[7], (D, D), (D // 16) ** -0.5, 0.875, ((0, 16), (1, 2)))
    w_inner = gaussian(key_of[8], (D, FF), D ** -0.5, 0.21875, ((0, 16), (1, 2)))
    w_outer = gaussian(key_of[9], (FF, D), FF ** -0.5, 0.109375, ((0, 16), (1, 2)))
    b_query = gaussian(key_of[10], (D,), 0.2, 1.0, ((0, 2),))
    b_value = gaussian(key_of[11], (D,), 0.2, 1.0, ((0, 2),))
    b_out = gaussian(key_of[12], (D,), 0.2, 1.0, ((0, 2),))
    norm1_gain = jnp.clip(1.0 + 0.1 * jax.random.normal(key_of[13], (D,), jnp.float32), 0.5, 1.5).astype(jnp.bfloat16)
    norm1_shift = gaussian(key_of[14], (D,), 0.2, 1.0, ((0, 2),))
    b_inner = gaussian(key_of[15], (FF,), 0.2, 1.0, ((0, 2),))
    b_outer = gaussian(key_of[16], (D,), 0.2, 1.0, ((0, 2),))
    norm2_gain = jnp.clip(1.0 + 0.1 * jax.random.normal(key_of[17], (D,), jnp.float32), 0.5, 1.5).astype(jnp.bfloat16)
    norm2_shift = gaussian(key_of[18], (D,), 0.2, 1.0, ((0, 2),))
    return dict(hidden_in=hidden_in, lengths=lengths, cot_out=cot_out, cot_cls=cot_cls, w_query=w_query, w_key=w_key, w_value=w_value, w_out=w_out, w_inner=w_inner, w_outer=w_outer, b_query=b_query, b_value=b_value, b_out=b_out, norm1_gain=norm1_gain, norm1_shift=norm1_shift, b_inner=b_inner, b_outer=b_outer, norm2_gain=norm2_gain, norm2_shift=norm2_shift)


@jax.custom_vjp
def low(v):
    return lax.optimization_barrier(v.astype(jnp.bfloat16)).astype(jnp.float32)

@jax.custom_vjp
def low_back(v):
    return v

def low_keep(v):
    return (low(v), None)

def low_pass(kept, grad):
    return (grad,)

def back_keep(v):
    return (v, None)

def back_low(kept, grad):
    return (low(grad),)
low.defvjp(low_keep, low_pass)
low_back.defvjp(back_keep, back_low)

def layer_norm(values, gain, shift):
    middle = lax.optimization_barrier(jnp.mean(values, axis=-1, keepdims=True))
    centered = values - middle
    spread = lax.optimization_barrier(jnp.mean(centered * centered, axis=-1, keepdims=True))
    return centered * lax.rsqrt(spread + 1e-12) * gain + shift

def matmul(left, right):
    return jnp.dot(left, right, precision=lax.Precision.HIGHEST, preferred_element_type=jnp.float32)

def attend_block(query_block, keys, values, key_live):
    scores = jnp.einsum('qhd,khd->hqk', query_block, keys, precision=lax.Precision.HIGHEST) * HDIM ** (-0.5)
    scores = low_back(scores)
    scores = jnp.where(key_live[None, None, :], scores, -1e+30)
    attn_probs = low(jax.nn.softmax(scores, axis=-1))
    return jnp.einsum('hqk,khd->qhd', attn_probs, values, precision=lax.Precision.HIGHEST)

def passage_forward(params, hidden, length):
    w_query, w_key, w_value, w_out, w_inner, w_outer, b_query, b_value, b_out, norm1_gain, norm1_shift, b_inner, b_outer, norm2_gain, norm2_shift = params
    queries = low(low_back(matmul(hidden, w_query) + b_query)).reshape(LENGTH, HEADS, HDIM)
    keys = low(low_back(matmul(hidden, w_key))).reshape(LENGTH, HEADS, HDIM)
    values = low(low_back(matmul(hidden, w_value) + b_value)).reshape(LENGTH, HEADS, HDIM)
    key_live = jnp.arange(LENGTH, dtype=jnp.int32) < length
    query_blocks = queries.reshape(LENGTH // QBLK, QBLK, HEADS, HDIM)

    def one_block(query_block):
        return attend_block(query_block, keys, values, key_live)
    context = lax.map(jax.checkpoint(one_block), query_blocks)
    context = low(low_back(context.reshape(LENGTH, D)))
    attn_out = low_back(matmul(context, w_out) + b_out)
    normed = layer_norm(hidden + attn_out, norm1_gain, norm1_shift)
    inner = low_back(matmul(low(normed), w_inner) + b_inner)
    outer = low_back(matmul(low(jax.nn.gelu(inner, approximate=False)), w_outer) + b_outer)
    return layer_norm(normed + outer, norm2_gain, norm2_shift)

def reference(hidden_in, lengths, cot_out, cot_cls, w_query, w_key, w_value, w_out, w_inner, w_outer, b_query, b_value, b_out, norm1_gain, norm1_shift, b_inner, b_outer, norm2_gain, norm2_shift):
    params = tuple((weight.astype(jnp.float32) for weight in (w_query, w_key, w_value, w_out, w_inner, w_outer, b_query, b_value, b_out, norm1_gain, norm1_shift, b_inner, b_outer, norm2_gain, norm2_shift)))
    zero_grads = jax.tree.map(jnp.zeros_like, params)

    def one_passage(totals, items):
        hidden, length, cot_rows, cot_first = items

        def forward(weights, rows):
            return passage_forward(weights, rows, length)
        result, back = jax.vjp(forward, params, hidden)
        cotangent = cot_rows.at[0].add(cot_first)
        grad_params, grad_hidden = back(cotangent)
        totals = jax.tree.map(jnp.add, totals, grad_params)
        return (totals, (result.astype(jnp.bfloat16), grad_hidden))
    inputs = (hidden_in.astype(jnp.float32), lengths, cot_out.astype(jnp.float32), cot_cls.astype(jnp.float32))
    totals, (layer_out, grad_input) = lax.scan(one_passage, zero_grads, inputs)
    g_wq, g_wk, g_wv, g_wo, g_wi, g_wu, g_bq, g_bv, g_bo, g_n1, g_s1, g_bi, g_bu, g_n2, g_s2 = totals
    return (layer_out, layer_out[:, 0, :], grad_input, g_wq, g_wk, g_wv, g_wo, g_wi, g_wu, g_bq, g_bv, g_bo, g_n1, g_s1, g_bi, g_bu, g_n2, g_s2)
```

```python
import functools

import jax
import jax.numpy as jnp
from jax import lax
from jax.experimental import pallas as pl
from jax.experimental.pallas import tpu as pltpu
from jax.sharding import PartitionSpec as P

HEADS = 12
HDIM = 64
PAIR = 2 * HDIM
LOG2E = 1.4426950408889634
BF16 = jnp.bfloat16
F32 = jnp.float32


def live_rows(shape, axis, start, length, shift, span):
    row = start + lax.broadcasted_iota(jnp.int32, shape, axis)
    inner = lax.rem(row, span)
    turned = inner + shift
    turned = jnp.where(turned >= span, turned - span, turned)
    return row - inner + turned < length


def attend_kernel(
    info, q_ref, k_ref, v_ref, out_ref, p_ref, sum_ref, keys, vals, ques, bound, turned, *, chunk, span
):
    pos = pl.program_id(1)
    kv = k_ref.shape[0]
    width = p_ref.shape[2]
    factor = HDIM**-0.5 * LOG2E

    @pl.when(pos == 0)
    def prepare():
        live = live_rows((kv, PAIR), 0, 0, info[0], info[1], span)
        kept = jnp.where(live, k_ref[...], jnp.zeros((), BF16))
        keys[...] = kept
        across = live_rows((16, kv), 1, 0, info[0], info[1], span).astype(BF16)
        shown = jnp.where(live, v_ref[...], jnp.zeros((), BF16)).T
        turned_q = q_ref[...].T
        squares = kept.astype(F32)
        squares = (squares * squares).astype(BF16)
        half = lambda axis: lax.broadcasted_iota(jnp.int32, (PAIR, PAIR), axis) // HDIM
        sizes = jnp.dot(squares, (half(0) == half(1)).astype(BF16), preferred_element_type=F32)
        largest = jnp.max(sizes, axis=0, keepdims=True)
        for h in range(2):
            rows = slice(h * HDIM, (h + 1) * HDIM)
            mine = turned_q[rows, :]
            vals[h, 0:HDIM, :] = shown[rows, :]
            vals[h, HDIM:, :] = across
            blank = jnp.zeros_like(mine)
            ques[h] = jnp.concatenate([mine, blank] if h == 0 else [blank, mine], 0)
            sharp = mine.astype(F32)
            reach = jnp.sum(sharp * sharp, axis=0, keepdims=True)
            top = jnp.max(largest[:, rows], axis=1, keepdims=True)
            bound[h : h + 1, :] = jnp.sqrt(reach * top * 1.03) * factor

    cols = pl.ds(pl.multiple_of(pos * width, width), width)

    def weigh(h, peak):
        query = ques[h, :, cols]
        for at in range(0, kv, chunk):
            rows = slice(at, at + chunk)
            scores = jnp.dot(keys[rows, :], query, preferred_element_type=F32)
            p_ref[h, rows, :] = jnp.exp2(scores * factor - peak).astype(BF16)
        total = jnp.dot(vals[h], p_ref[h], preferred_element_type=F32)
        sums = total[HDIM : HDIM + 1, :]
        sum_ref[h] = sums
        turned[h * HDIM : (h + 1) * HDIM, :] = total[0:HDIM, :] / sums
        return jnp.min(sums)

    def exact_peak(h):
        query = ques[h, :, cols]

        def largest(at, peak):
            rows = pl.ds(pl.multiple_of(at * chunk, chunk), chunk)
            scores = jnp.dot(keys[rows, :], query, preferred_element_type=F32)
            live = live_rows((chunk, width), 0, at * chunk, info[0], info[1], span)
            return jnp.maximum(peak, jnp.max(jnp.where(live, scores, -1e30), axis=0, keepdims=True))

        return lax.fori_loop(0, kv // chunk, largest, jnp.full((1, width), -1e30, F32)) * factor

    lowest = [weigh(h, bound[h : h + 1, cols]) for h in range(2)]
    for h in range(2):
        @pl.when(jnp.logical_not(lowest[h] > 2.0**-70))
        def again(h=h):
            weigh(h, exact_peak(h))

    out_ref[...] = turned[...].T.astype(BF16)


def attend(info, q_from, k_from, v_from, span):
    (queries, q_at), (keys, k_at), (values, v_at) = q_from, k_from, v_from
    rows, kv = queries.shape[0], keys.shape[0]
    width = min(512, rows)
    pairs = HEADS // 2
    return pl.pallas_call(
        functools.partial(attend_kernel, chunk=min(256, kv), span=span),
        out_shape=(
            jax.ShapeDtypeStruct((rows, HEADS * HDIM), BF16),
            jax.ShapeDtypeStruct((HEADS, kv, rows), BF16),
            jax.ShapeDtypeStruct((HEADS, 1, rows), F32),
        ),
        grid_spec=pltpu.PrefetchScalarGridSpec(
            num_scalar_prefetch=1,
            grid=(pairs, rows // width),
            in_specs=[
                pl.BlockSpec((rows, PAIR), lambda j, c, s: (0, q_at + j)),
                pl.BlockSpec((kv, PAIR), lambda j, c, s: (0, k_at + j)),
                pl.BlockSpec((kv, PAIR), lambda j, c, s: (0, v_at + j)),
            ],
            out_specs=(
                pl.BlockSpec((width, PAIR), lambda j, c, s: (c, j)),
                pl.BlockSpec((2, kv, width), lambda j, c, s: (j, 0, c)),
                pl.BlockSpec((2, 1, width), lambda j, c, s: (j, 0, c)),
            ),
            scratch_shapes=[
                pltpu.VMEM((kv, PAIR), BF16),
                pltpu.VMEM((2, HDIM + 16, kv), BF16),
                pltpu.VMEM((2, PAIR, rows), BF16),
                pltpu.VMEM((2, rows), F32),
                pltpu.VMEM((PAIR, width), F32),
            ],
        ),
        compiler_params=pltpu.CompilerParams(vmem_limit_bytes=56 * 2**20),
        cost_estimate=pl.CostEstimate(
            flops=2 * 2 * HEADS * rows * kv * 256,
            bytes_accessed=2 * HEADS * rows * kv,
            transcendentals=HEADS * rows * kv,
        ),
        name="attend",
    )(info, queries, keys, values)


def attend_back_kernel(
    info,
    q_ref,
    k_ref,
    v_ref,
    g_ref,
    ctx_ref,
    sum_ref,
    p_ref,
    gq_ref,
    gk_ref,
    gv_ref,
    keys,
    grads,
    grads_up,
    delta,
    low,
    total,
    *,
    width,
    span,
):
    at = pl.program_id(1)
    kv, rows = k_ref.shape[0], q_ref.shape[0]
    block = p_ref.shape[1]
    scale = HDIM**-0.5

    @pl.when(at == 0)
    def prepare():
        live = live_rows((kv, PAIR), 0, 0, info[0], info[1], span)
        keys[...] = jnp.where(live, k_ref[...], jnp.zeros((), BF16)).T
        turned = g_ref[...].T.astype(F32)
        dots = turned * ctx_ref[...].T.astype(F32)
        parts = []
        for h in range(2):
            own = slice(h * HDIM, (h + 1) * HDIM)
            inverse = 1.0 / sum_ref[h]
            delta[h : h + 1, :] = jnp.sum(dots[own, :], axis=0, keepdims=True) * inverse
            parts.append((turned[own, :] * inverse).astype(BF16))
        blank = jnp.zeros((HDIM, rows), BF16)
        grads[0] = jnp.concatenate([parts[0], blank], 0)
        grads[1] = jnp.concatenate([blank, parts[1]], 0)
        grads_up[...] = jnp.concatenate(parts, 0).T
        total[...] = jnp.zeros_like(total)

    here = pl.ds(pl.multiple_of(at * block, block), block)
    values = v_ref[here, :]
    key_parts, value_parts = [], []
    for h in range(2):
        own = slice(h * HDIM, (h + 1) * HDIM)
        for start in range(0, rows, width):
            cols = slice(start, start + width)
            change = jnp.dot(values, grads[h, :, cols], preferred_element_type=F32)
            weight = p_ref[h, :, cols].astype(F32)
            low[h, :, cols] = (weight * (change - delta[h : h + 1, cols])).astype(BF16)
        value_parts.append(jnp.dot(p_ref[h], grads_up[...], preferred_element_type=F32))
        key_parts.append(jnp.dot(low[h], q_ref[...], preferred_element_type=F32))
        total[own, :] += jnp.dot(keys[own, here], low[h], preferred_element_type=F32)
    first = lax.broadcasted_iota(jnp.int32, (block, PAIR), 1) < HDIM
    live = live_rows((block, PAIR), 0, at * block, info[0], info[1], span)
    zero = jnp.zeros((), F32)
    gk_ref[...] = jnp.where(live, jnp.where(first, *key_parts) * scale, zero).astype(BF16)
    gv_ref[...] = jnp.where(live, jnp.where(first, *value_parts), zero).astype(BF16)

    @pl.when(at == kv // block - 1)
    def finish():
        gq_ref[...] = (total[...] * scale).T.astype(BF16)


def attend_back(info, q_from, k_from, v_from, grad, context, sums, probs, span):
    (queries, q_at), (keys, k_at), (values, v_at) = q_from, k_from, v_from
    rows, kv = queries.shape[0], keys.shape[0]
    block = min(512, kv)
    pairs = HEADS // 2
    wide = HEADS * HDIM
    return pl.pallas_call(
        functools.partial(attend_back_kernel, width=min(1024, rows), span=span),
        out_shape=(
            jax.ShapeDtypeStruct((rows, wide), BF16),
            jax.ShapeDtypeStruct((kv, wide), BF16),
            jax.ShapeDtypeStruct((kv, wide), BF16),
        ),
        grid_spec=pltpu.PrefetchScalarGridSpec(
            num_scalar_prefetch=1,
            grid=(pairs, kv // block),
            in_specs=[
                pl.BlockSpec((rows, PAIR), lambda j, c, s: (0, q_at + j)),
                pl.BlockSpec((kv, PAIR), lambda j, c, s: (0, k_at + j)),
                pl.BlockSpec((kv, PAIR), lambda j, c, s: (0, v_at + j)),
                pl.BlockSpec((rows, PAIR), lambda j, c, s: (0, j)),
                pl.BlockSpec((rows, PAIR), lambda j, c, s: (0, j)),
                pl.BlockSpec((2, 1, rows), lambda j, c, s: (j, 0, 0)),
                pl.BlockSpec((2, block, rows), lambda j, c, s: (j, c, 0)),
            ],
            out_specs=(
                pl.BlockSpec((rows, PAIR), lambda j, c, s: (0, j)),
                pl.BlockSpec((block, PAIR), lambda j, c, s: (c, j)),
                pl.BlockSpec((block, PAIR), lambda j, c, s: (c, j)),
            ),
            scratch_shapes=[
                pltpu.VMEM((PAIR, kv), BF16),
                pltpu.VMEM((2, PAIR, rows), BF16),
                pltpu.VMEM((rows, PAIR), BF16),
                pltpu.VMEM((2, rows), F32),
                pltpu.VMEM((2, block, rows), BF16),
                pltpu.VMEM((PAIR, rows), F32),
            ],
        ),
        compiler_params=pltpu.CompilerParams(vmem_limit_bytes=56 * 2**20),
        cost_estimate=pl.CostEstimate(
            flops=4 * 2 * HEADS * rows * kv * 256,
            bytes_accessed=2 * HEADS * rows * kv,
            transcendentals=0,
        ),
        name="attend_back",
    )(info, queries, keys, values, grad, context, sums, probs)


def rows_of(kept_ref, other_ref, step, split):
    return jnp.where(step < split, kept_ref[0], other_ref[...])


def project(rows, weight):
    return jnp.dot(rows, weight, preferred_element_type=F32)


def project_back(grads, weight):
    return lax.dot_general(grads, weight, (((1,), (1,)), ((), ())), preferred_element_type=F32)


def weight_grad(rows, grads):
    return lax.dot_general(rows, grads, (((0,), (0,)), ((), ())), preferred_element_type=F32)


def run_all(copies):
    for copy in copies:
        copy.start()
    return copies


def wait_all(copies):
    for copy in copies:
        copy.wait()


class Pieces:
    def __init__(self, shape, mesh_shape):
        self.m, self.n = mesh_shape
        self.r, self.c = shape

    def copies(self, packed, mats, sems, out):
        found = []
        r, c = self.r, self.c
        for j in range(self.m):
            for i in range(self.n):
                at = 0
                for t, mat in enumerate(mats):
                    tall = mat.shape[0] // (self.m * r)
                    wide = mat.shape[1] // (self.n * c)
                    for w in range(wide):
                        block = packed.at[j * self.n + i, pl.ds(at, tall * r), :]
                        place = mat.at[
                            pl.ds(j * tall * r, tall * r), pl.ds((i * wide + w) * c, c)
                        ]
                        at += tall * r
                        pair = (place, block) if out else (block, place)
                        found.append(pltpu.make_async_copy(*pair, sems.at[len(found)]))
        return found

    def by_mat(self, found, mats):
        counts = [mat.shape[1] // (self.n * self.c) for mat in mats]
        groups = [[] for _ in mats]
        at = 0
        for _ in range(self.m * self.n):
            for t, count in enumerate(counts):
                groups[t] += found[at : at + count]
                at += count
        return groups


def queries_kernel(info, kept_ref, other_ref, packed, bias_ref, out_ref, mat_q, mat_k, mat_v, sems, *, split, grid_of):
    step = pl.program_id(0)
    mats = [mat_q, mat_k, mat_v]

    @pl.when(step == 0)
    def load():
        wait_all(run_all(grid_of.copies(packed, mats, sems, False)))

    rows = rows_of(kept_ref, other_ref, step, split)
    width = mat_q.shape[1]
    for t, mat in enumerate(mats):
        cols = slice(t * width, (t + 1) * width)
        out_ref[:, cols] = (project(rows, mat[...]) + bias_ref[:, cols]).astype(BF16)


def split_specs(kept_at, tile, split, width):
    return [
        pl.BlockSpec((1, tile, width), lambda i, s: (s[kept_at], jnp.minimum(i, split - 1), 0)),
        pl.BlockSpec((tile, width), lambda i, s: (jnp.maximum(i - split, 0), 0)),
    ]


def whole_spec(shape):
    return pl.BlockSpec(shape, lambda i, s: (0,) * len(shape))


def queries_keys_values(info, kept, other, packed, bias, grid_of):
    block_len, width = other.shape
    tile = min(256, block_len)
    split = block_len // tile
    return pl.pallas_call(
        functools.partial(queries_kernel, split=split, grid_of=grid_of),
        out_shape=jax.ShapeDtypeStruct((2 * block_len, 3 * width), BF16),
        grid_spec=pltpu.PrefetchScalarGridSpec(
            num_scalar_prefetch=1,
            grid=(2 * split,),
            in_specs=split_specs(2, tile, split, width)
            + [pl.BlockSpec(memory_space=pl.ANY), whole_spec(bias.shape)],
            out_specs=pl.BlockSpec((tile, 3 * width), lambda i, s: (i, 0)),
            scratch_shapes=[pltpu.VMEM((width, width), BF16)] * 3
            + [pltpu.SemaphoreType.DMA((3 * grid_of.m * grid_of.n,))],
        ),
        compiler_params=pltpu.CompilerParams(vmem_limit_bytes=40 * 2**20),
        cost_estimate=pl.CostEstimate(
            flops=2 * 2 * block_len * width * 3 * width,
            bytes_accessed=2 * 2 * block_len * width * 4,
            transcendentals=0,
        ),
        name="queries",
    )(info, kept, other, packed, bias)


def normal(values):
    middle = jnp.mean(values, axis=-1, keepdims=True)
    centered = values - middle
    spread = jnp.mean(centered * centered, axis=-1, keepdims=True)
    inverse = lax.rsqrt(spread + 1e-12)
    return centered * inverse, inverse


def normal_back(grad, unit, inverse, gain):
    scaled = grad * gain
    mean = jnp.mean(scaled, axis=-1, keepdims=True)
    along = jnp.mean(scaled * unit, axis=-1, keepdims=True)
    return (scaled - mean - unit * along) * inverse


def gelu_pair(u):
    size = jnp.abs(u)
    below = 1.0 + (0.3275911 * 0.7071067811865476) * size
    t = pl.reciprocal(below, approx=True)
    t = t * (2.0 - below * t)
    bell = jnp.exp2((-0.5 * LOG2E) * u * u)
    poly = 0.5 * 1.061405429
    for factor in (-0.5 * 1.453152027, 0.5 * 1.421413741, -0.5 * 0.284496736, 0.5 * 0.254829592):
        poly = poly * t + factor
    tail = poly * t * bell
    phi = jnp.where(u >= 0.0, 1.0 - tail, tail)
    return u * phi, phi + (0.3989422804014327 * u) * bell


def add_rows(total, at, values):
    total[at : at + 1, 0 : values.shape[1]] += jnp.sum(values, axis=0, keepdims=True)


def middle_kernel(
    info,
    hid_kept,
    hid_other,
    cot_kept,
    cot_other,
    ctx_ref,
    cls_ref,
    packed,
    vec_ref,
    inner_bias,
    layer_ref,
    grad_ctx_ref,
    resid_ref,
    sums_ref,
    mat_out,
    mat_inner,
    mat_outer,
    acc_out,
    acc_inner,
    acc_outer,
    totals,
    active,
    slope,
    low,
    vec_low,
    sems,
    vec_sems,
    *,
    split,
    grid_of,
    chunk,
):
    step = pl.program_id(0)
    last = pl.num_programs(0) - 1
    mats = [mat_out, mat_inner, mat_outer]
    tile, width = ctx_ref.shape
    ff = mat_inner.shape[1]
    loads = grid_of.by_mat(grid_of.copies(packed, mats, sems, False), mats)

    @pl.when(step == 0)
    def start():
        for group in loads:
            run_all(group)
        for acc in (acc_out, acc_inner, acc_outer, totals):
            acc[...] = jnp.zeros_like(acc)
        wait_all(loads[0])

    bias_out, gain_one, shift_one, bias_outer, gain_two, shift_two = [
        vec_ref[t : t + 1, :] for t in range(6)
    ]
    hidden = rows_of(hid_kept, hid_other, step, split).astype(F32)
    context = ctx_ref[...]
    unit_one, inverse_one = normal(hidden + project(context, mat_out[...]) + bias_out)
    normed = unit_one * gain_one + shift_one
    normed_low = normed.astype(BF16)

    @pl.when(step == 0)
    def more():
        wait_all(loads[1])
        wait_all(loads[2])

    for at in range(0, ff, chunk):
        cols = slice(at, at + chunk)
        inner = project(normed_low, mat_inner[:, cols]) + inner_bias[:, cols]
        value, change = gelu_pair(inner)
        active[:, cols] = value.astype(BF16)
        slope[:, cols] = change.astype(BF16)
    unit_two, inverse_two = normal(normed + project(active[...], mat_outer[...]) + bias_outer)
    layer_ref[...] = (unit_two * gain_two + shift_two).astype(BF16)

    row = step * tile + lax.broadcasted_iota(jnp.int32, (tile, width), 0)
    grad_result = rows_of(cot_kept, cot_other, step, split).astype(F32)
    grad_result += jnp.where(row == info[4], cls_ref[...], 0.0)
    add_rows(totals, 4, grad_result * unit_two)
    add_rows(totals, 5, grad_result)
    grad_resid_two = normal_back(grad_result, unit_two, inverse_two, gain_two)
    grad_outer = grad_resid_two.astype(BF16)
    add_rows(totals, 3, grad_outer.astype(F32))
    for at in range(0, ff, chunk):
        cols = slice(at, at + chunk)
        grad_inner = project_back(grad_outer, mat_outer[cols, :]) * slope[:, cols].astype(F32)
        low[:, cols] = grad_inner.astype(BF16)
        totals[8:9, cols] += jnp.sum(grad_inner, axis=0, keepdims=True)
        acc_outer[cols, :] += weight_grad(active[:, cols], grad_outer)
    grad_normed = grad_resid_two + project_back(low[...], mat_inner[...])
    for at in range(0, ff, chunk):
        cols = slice(at, at + chunk)
        acc_inner[:, cols] += weight_grad(normed_low, low[:, cols])
    add_rows(totals, 1, grad_normed * unit_one)
    add_rows(totals, 2, grad_normed)
    grad_resid_one = normal_back(grad_normed, unit_one, inverse_one, gain_one)
    resid_ref[...] = grad_resid_one
    grad_attn = grad_resid_one.astype(BF16)
    add_rows(totals, 0, grad_attn.astype(F32))
    acc_out[...] += weight_grad(context, grad_attn)
    grad_ctx_ref[...] = project_back(grad_attn, mat_out[...]).astype(BF16)

    @pl.when(step == last)
    def finish():
        r, c, m, n = grid_of.r, grid_of.c, grid_of.m, grid_of.n
        stores = grid_of.by_mat(grid_of.copies(sums_ref, mats, sems, True), mats)
        for mat, acc, group in zip(mats, (acc_out, acc_inner, acc_outer), stores):
            mat[...] = acc[...].astype(BF16)
            run_all(group)
        vec_low[...] = jnp.zeros_like(vec_low)
        for i in range(n):
            for t in range(6):
                vec_low[i, t : t + 1, :] = totals[t : t + 1, i * c : (i + 1) * c]
            wide = ff // (n * c)
            for t in range(wide):
                at = (i * wide + t) * c
                vec_low[i, 6 + t : 7 + t, :] = totals[8:9, at : at + c]
        tails = []
        vec_bits = vec_low[...].astype(BF16)
        for i in range(n):
            active[16 * i : 16 * i + 16, 0:c] = vec_bits[i]
        for j in range(m):
            for i in range(n):
                tails.append(
                    pltpu.make_async_copy(
                        active.at[pl.ds(16 * i, 16), pl.ds(0, c)],
                        sums_ref.at[j * n + i, pl.ds(9 * r, 16), :],
                        vec_sems.at[j * n + i],
                    )
                )
        run_all(tails)
        for group in stores:
            wait_all(group)
        wait_all(tails)


def middle(info, hidden, cots, context, cls_row, packed, vectors, inner_bias, grid_of):
    block_len, width = hidden[1].shape
    ff = inner_bias.shape[1]
    tile = min(256, block_len)
    split = block_len // tile
    pieces = grid_of.m * grid_of.n
    row_spec = pl.BlockSpec((tile, width), lambda i, s: (i, 0))
    return pl.pallas_call(
        functools.partial(middle_kernel, split=split, grid_of=grid_of, chunk=768),
        out_shape=(
            jax.ShapeDtypeStruct((2 * block_len, width), BF16),
            jax.ShapeDtypeStruct((2 * block_len, width), BF16),
            jax.ShapeDtypeStruct((2 * block_len, width), F32),
            jax.ShapeDtypeStruct((pieces, 9 * grid_of.r + 16, grid_of.c), BF16),
        ),
        grid_spec=pltpu.PrefetchScalarGridSpec(
            num_scalar_prefetch=1,
            grid=(2 * split,),
            in_specs=split_specs(2, tile, split, width)
            + split_specs(3, tile, split, width)
            + [
                row_spec,
                whole_spec(cls_row.shape),
                pl.BlockSpec(memory_space=pl.ANY),
                whole_spec(vectors.shape),
                whole_spec(inner_bias.shape),
            ],
            out_specs=(row_spec, row_spec, row_spec, pl.BlockSpec(memory_space=pl.ANY)),
            scratch_shapes=[
                pltpu.VMEM((width, width), BF16),
                pltpu.VMEM((width, ff), BF16),
                pltpu.VMEM((ff, width), BF16),
                pltpu.VMEM((width, width), F32),
                pltpu.VMEM((width, ff), F32),
                pltpu.VMEM((ff, width), F32),
                pltpu.VMEM((16, ff), F32),
                pltpu.VMEM((tile, ff), BF16),
                pltpu.VMEM((tile, ff), BF16),
                pltpu.VMEM((tile, ff), BF16),
                pltpu.VMEM((grid_of.n, 16, grid_of.c), F32),
                pltpu.SemaphoreType.DMA((6 * pieces,)),
                pltpu.SemaphoreType.DMA((pieces,)),
            ],
        ),
        compiler_params=pltpu.CompilerParams(vmem_limit_bytes=60 * 2**20),
        cost_estimate=pl.CostEstimate(
            flops=2 * 2 * block_len * width * (width + 2 * ff) * 3,
            bytes_accessed=2 * block_len * width * 16 + 40 * width * width,
            transcendentals=2 * 2 * block_len * ff,
        ),
        name="middle",
    )(info, *hidden, *cots, context, cls_row, packed, vectors, inner_bias)


def tail_kernel(info, hid_kept, hid_other, gq_ref, gk_ref, gv_ref, resid_ref, packed, *rest, split, grid_of, full):
    step = pl.program_id(0)
    if full:
        grad_ref, sums_ref, mat_q, mat_k, mat_v, sems, acc, totals, vec_low, vec_sems = rest
    else:
        grad_ref, mat_q, mat_k, mat_v, sems = rest
    mats = [mat_q, mat_k, mat_v]
    grads = [gq_ref[...], gk_ref[...], gv_ref[...]]

    @pl.when(step == 0)
    def load():
        wait_all(run_all(grid_of.copies(packed, mats, sems, False)))

    def into_input():
        total = resid_ref[...]
        for grad, mat in zip(grads, mats):
            total += project_back(grad, mat[...])
        grad_ref[...] = total.astype(grad_ref.dtype)

    if not full:
        into_input()
        return

    pl.when(step < split)(into_input)

    @pl.when(step == 0)
    def clear():
        acc[...] = jnp.zeros_like(acc)
        totals[...] = jnp.zeros_like(totals)

    rows = rows_of(hid_kept, hid_other, step, split)
    for t, grad in enumerate(grads):
        acc[t] += weight_grad(rows, grad)
    add_rows(totals, 0, grads[0].astype(F32))
    add_rows(totals, 1, grads[2].astype(F32))

    @pl.when(step == pl.num_programs(0) - 1)
    def finish():
        r, c, m, n = grid_of.r, grid_of.c, grid_of.m, grid_of.n
        for t, mat in enumerate(mats):
            mat[...] = acc[t].astype(BF16)
        stores = run_all(grid_of.copies(sums_ref, mats, sems, True))
        vec_low[...] = jnp.zeros_like(vec_low)
        for i in range(n):
            part = jnp.concatenate([totals[0:2, i * c : (i + 1) * c], jnp.zeros((14, c), F32)], 0)
            vec_low[i] = part.astype(BF16)
        tails = []
        for j in range(m):
            for i in range(n):
                tails.append(
                    pltpu.make_async_copy(
                        vec_low.at[i],
                        sums_ref.at[j * n + i, pl.ds(3 * r, 16), :],
                        vec_sems.at[j * n + i],
                    )
                )
        run_all(tails)
        wait_all(stores)
        wait_all(tails)


def tail(info, hidden, grads, resid, packed, grid_of, full):
    block_len, width = hidden[1].shape
    tile = min(256, block_len)
    split = block_len // tile
    pieces = grid_of.m * grid_of.n
    steps = 2 * split if full else split
    at = (lambda i: i) if full else (lambda i: i + split)
    row_spec = pl.BlockSpec((tile, width), lambda i, s: (at(i), 0))
    out_spec = pl.BlockSpec((tile, width), lambda i, s: (jnp.minimum(i, split - 1), 0))
    out_shape = [jax.ShapeDtypeStruct((block_len, width), F32 if full else BF16)]
    out_specs = [out_spec]
    scratch = [pltpu.VMEM((width, width), BF16)] * 3 + [pltpu.SemaphoreType.DMA((3 * pieces,))]
    if full:
        out_shape.append(jax.ShapeDtypeStruct((pieces, 3 * grid_of.r + 16, grid_of.c), BF16))
        out_specs.append(pl.BlockSpec(memory_space=pl.ANY))
        scratch += [
            pltpu.VMEM((3, width, width), F32),
            pltpu.VMEM((8, width), F32),
            pltpu.VMEM((grid_of.n, 16, grid_of.c), BF16),
            pltpu.SemaphoreType.DMA((pieces,)),
        ]
    return pl.pallas_call(
        functools.partial(tail_kernel, split=split, grid_of=grid_of, full=full),
        out_shape=tuple(out_shape),
        grid_spec=pltpu.PrefetchScalarGridSpec(
            num_scalar_prefetch=1,
            grid=(steps,),
            in_specs=split_specs(2, tile, split, width)
            + [row_spec] * 4
            + [pl.BlockSpec(memory_space=pl.ANY)],
            out_specs=tuple(out_specs),
            scratch_shapes=scratch,
        ),
        compiler_params=pltpu.CompilerParams(vmem_limit_bytes=48 * 2**20),
        cost_estimate=pl.CostEstimate(
            flops=2 * block_len * width * 3 * width * (3 if full else 1),
            bytes_accessed=block_len * width * 16,
            transcendentals=0,
        ),
        name="tail_all" if full else "tail_other",
    )(info, *hidden, *grads, resid, packed)


def swap(block, axis, route):
    if all(a == b for a, b in route):
        return block
    return lax.ppermute(block, axis, route)


class Regroup:
    def __init__(self):
        self.n = lax.axis_size("blk")
        self.me = lax.axis_index("blk")
        self.per = self.n // 2
        self.passage = self.me // self.per
        self.part = lax.rem(self.me, 2)
        self.first = [(i, (i % 2) * self.per + i // 2) for i in range(self.n)]
        self.second = [(i, (1 - i % 2) * self.per + i // 2) for i in range(self.n)]
        self.stays = all(a == b for a, b in self.first)

    def gather(self, pair):
        other = lax.dynamic_index_in_dim(pair, 1 - self.part, 0, keepdims=False)
        other = swap(other, "blk", self.second)
        if self.stays:
            return (pair, other)
        kept = lax.dynamic_index_in_dim(pair, self.part, 0, keepdims=True)
        return (swap(kept, "blk", self.first), other)

    def kept_index(self):
        return self.part if self.stays else jnp.zeros_like(self.part)

    def back(self, kept, other):
        kept = swap(kept, "blk", [(b, a) for a, b in self.first])
        other = swap(other, "blk", [(b, a) for a, b in self.second])
        return kept, other

    def order(self, kept, other):
        return jnp.where(self.part == 0, jnp.stack([kept, other]), jnp.stack([other, kept]))


def pack(shards):
    c = min(s.shape[1] for s in shards)
    return jnp.concatenate(
        [s[:, at : at + c] for s in shards for at in range(0, s.shape[1], c)], axis=0
    )


def unpack(block, shapes):
    c = block.shape[-1]
    found, at = [], 0
    for rows, cols in shapes:
        parts = []
        for _ in range(cols // c):
            parts.append(block[..., at : at + rows, :])
            at += rows
        found.append(jnp.concatenate(parts, axis=-1) if len(parts) > 1 else parts[0])
    return found


class Weights:
    def __init__(self, shards):
        self.shapes = [s.shape for s in shards]
        self.m, self.n = lax.axis_size("batch"), lax.axis_size("blk")
        r, c = min(s[0] for s in self.shapes), min(s[1] for s in self.shapes)
        self.fits = r % 16 == 0 and c % 128 == 0
        packed = lax.all_gather(pack(shards), ("batch", "blk"), axis=0)
        if self.fits:
            self.grid_of = Pieces((r, c), (self.m, self.n))
            self.packed = packed
        else:
            self.grid_of = Pieces((r * self.m, c * self.n), (1, 1))
            whole = []
            for part in unpack(packed, self.shapes):
                rows, cols = part.shape[1:]
                part = part.reshape(self.m, self.n, rows, cols).transpose(0, 2, 1, 3)
                whole.append(part.reshape(self.m * rows, self.n * cols))
            self.packed = pack(whole)[None]

    def scatter(self, sums):
        extra = 16
        if not self.fits:
            rows = sums.shape[1] - extra
            wide = [(a * self.m, b * self.n) for a, b in self.shapes]
            parts = []
            for part in unpack(sums[0, :rows], wide):
                a, b = part.shape[0] // self.m, part.shape[1] // self.n
                part = part.reshape(self.m, a, self.n, b).transpose(0, 2, 1, 3)
                parts.append(part.reshape(self.m * self.n, a, b))
            c = min(s[1] for s in self.shapes)
            blocks = jnp.stack([pack([p[d] for p in parts]) for d in range(self.m * self.n)])
            vecs = sums[0, rows:].reshape(extra, self.n, c).transpose(1, 0, 2)
            vecs = jnp.broadcast_to(vecs[None], (self.m, self.n, extra, c))
            sums = jnp.concatenate([blocks, vecs.reshape(self.m * self.n, extra, c)], axis=1)
        height, c = sums.shape[1:]
        own = lax.psum_scatter(
            sums.reshape(-1, c), ("batch", "blk"), scatter_dimension=0, tiled=True
        )
        own = own.astype(F32)
        return [*unpack(own[: height - extra], self.shapes), own[height - extra :]]


def on_device(
    hidden_in,
    lengths,
    cot_out,
    cot_cls,
    w_query,
    w_key,
    w_value,
    w_out,
    w_inner,
    w_outer,
    b_query,
    b_value,
    b_out,
    norm1_gain,
    norm1_shift,
    b_inner,
    b_outer,
    norm2_gain,
    norm2_shift,
):
    plan = Regroup()
    groups, block_len, width = hidden_in.shape
    span = groups * block_len
    per = plan.per
    fleets = [[i * per + j for j in range(per)] for i in range(2)]
    first_row = plan.passage * block_len
    owner = lax.rem(plan.me, per) == 0

    length = lax.dynamic_index_in_dim(lengths, plan.passage, 0, keepdims=False)
    info = jnp.stack(
        [
            length,
            first_row,
            plan.kept_index(),
            plan.kept_index(),
            jnp.where(owner, first_row, -1),
        ]
    ).astype(jnp.int32)

    heads = Weights([w_query, w_key, w_value])
    dense = Weights([w_out, w_inner, w_outer])
    narrow = jnp.stack(
        [b_query, b_value, b_out, norm1_gain, norm1_shift, b_outer, norm2_gain, norm2_shift]
    )
    share = width // plan.n
    vec_shard = jnp.concatenate([narrow, b_inner.reshape(-1, share)], 0)
    vec_all = lax.all_gather(vec_shard, "blk", axis=0).astype(F32)
    narrow = vec_all[:, :8].transpose(1, 0, 2).reshape(8, width)
    bias_inner = vec_all[:, 8:].reshape(1, -1)
    bias_heads = jnp.concatenate([narrow[0:1], jnp.zeros_like(narrow[0:1]), narrow[1:2]], 1)

    hidden = plan.gather(hidden_in)
    cots = plan.gather(cot_out)
    qkv = queries_keys_values(info, *hidden, heads.packed, bias_heads, heads.grid_of)
    if per == 1:
        kv, key_at = qkv, width // PAIR
    else:
        kv = lax.all_gather(qkv[:, width:], "blk", axis=0, tiled=True, axis_index_groups=fleets)
        key_at = 0
    sources = ((qkv, 0), (kv, key_at), (kv, key_at + width // PAIR))
    context_low, probs, sums = attend(info, *sources, span)

    own_cls = lax.dynamic_index_in_dim(cot_cls, plan.passage, 0, keepdims=True).astype(F32)
    layer_out, grad_context, grad_resid, dense_sums = middle(
        info, hidden, cots, context_low, own_cls, dense.packed, narrow[2:], bias_inner, dense.grid_of
    )
    part_wo, part_wi, part_wu, dense_vecs = dense.scatter(dense_sums)
    part_bo, part_g1, part_s1, part_bu, part_g2, part_s2 = [dense_vecs[t] for t in range(6)]
    part_bi = dense_vecs[6 : 6 + b_inner.size // share].reshape(-1)

    top = lax.dynamic_slice_in_dim(layer_out, first_row, 1, 0)
    tops = lax.all_gather(top, "blk", axis=0, tiled=True)[::per]
    cls_part = lax.dynamic_slice_in_dim(tops, plan.me * share, share, 1)
    layer_rows = plan.order(*plan.back(layer_out[:block_len], layer_out[block_len:]))

    grad_q, grad_k, grad_v = attend_back(info, *sources, grad_context, context_low, sums, probs, span)
    if per > 1:
        grad_k, grad_v = [
            lax.psum_scatter(g, "blk", scatter_dimension=0, tiled=True, axis_index_groups=fleets)
            for g in (grad_k, grad_v)
        ]
    grads = (grad_q, grad_k, grad_v)
    (other,) = tail(info, hidden, grads, grad_resid, heads.packed, heads.grid_of, False)
    kept, head_sums = tail(info, hidden, grads, grad_resid, heads.packed, heads.grid_of, True)
    kept, other = plan.back(kept, other)
    grad_input = plan.order(kept, other.astype(F32))
    part_wq, part_wk, part_wv, head_vecs = heads.scatter(head_sums)
    part_bq, part_bv = head_vecs[0], head_vecs[1]
    return (
        layer_rows,
        cls_part,
        grad_input,
        part_wq,
        part_wk,
        part_wv,
        part_wo,
        part_wi,
        part_wu,
        part_bq,
        part_bv,
        part_bo,
        part_g1,
        part_s1,
        part_bi,
        part_bu,
        part_g2,
        part_s2,
    )


def solution(mesh):
    rows = P("batch", "blk", None)
    mats = (P("batch", "blk"),) * 6
    vecs = (P("blk"),) * 9
    return jax.shard_map(
        on_device,
        mesh=mesh,
        in_specs=(rows, P("batch"), rows, P("batch", None)) + mats + vecs,
        out_specs=(rows, P("batch", "blk"), rows) + mats + vecs,
        check_vma=False,
    )
```

```python
import functools

import jax
import jax.numpy as jnp
from jax import lax
from jax.experimental import pallas as pl
from jax.experimental.pallas import tpu as pltpu
from jax.sharding import PartitionSpec as P

HEADS = 12
HDIM = 64
PAIR = 2 * HDIM
LOG2E = 1.4426950408889634
BF16 = jnp.bfloat16
F32 = jnp.float32


def live_rows(shape, axis, start, length, shift, span):
    rows = shape[axis]
    step = min(rows, span)
    parts = []
    for at in range(0, rows, step):
        first = start + at
        base = (first // span) * span
        sizes = list(shape)
        sizes[axis] = step
        turned = lax.broadcasted_iota(jnp.int32, tuple(sizes), axis) + (first - base + shift)
        turned = jnp.where(turned >= span, turned - span, turned)
        parts.append(turned < length - base)
    return parts[0] if len(parts) == 1 else jnp.concatenate(parts, axis)


def chunk_of(rows):
    return min(1024, rows // 2)


def segments(rows, size):
    for at in range(0, rows, size):
        for h in range(2):
            yield h, slice(at, at + size), slice(2 * at + h * size, 2 * at + (h + 1) * size)


def beside(part, h):
    blank = jnp.zeros_like(part)
    return jnp.concatenate([part, blank] if h == 0 else [blank, part], 0)


def head_rows(h):
    return slice(h * HDIM, (h + 1) * HDIM)


def attend_kernel(
    info, q_ref, k_ref, v_ref, out_ref, p_ref, sum_ref, keys, vals, ques, bound, turned, *, chunk, across, span
):
    pos = pl.program_id(1)
    kv = k_ref.shape[0]
    size, width = out_ref.shape[0], p_ref.shape[2]
    factor = HDIM**-0.5 * LOG2E

    @pl.when(pos == 0)
    def prepare():
        live = live_rows((kv, PAIR), 0, 0, info[0], info[1], span)
        kept = jnp.where(live, k_ref[...], jnp.zeros((), BF16))
        keys[...] = kept
        vals[0:PAIR, :] = jnp.where(live, v_ref[...], jnp.zeros((), BF16)).T
        vals[PAIR:, :] = live_rows((16, kv), 1, 0, info[0], info[1], span).astype(BF16)
        turned_q = q_ref[...].T
        squares = kept.astype(F32)
        squares = (squares * squares).astype(BF16)
        half = lambda axis: lax.broadcasted_iota(jnp.int32, (PAIR, PAIR), axis) // HDIM
        sizes = jnp.dot(squares, (half(0) == half(1)).astype(BF16), preferred_element_type=F32)
        largest = jnp.max(sizes, axis=0, keepdims=True)
        tops = [jnp.max(largest[:, head_rows(h)], axis=1, keepdims=True) for h in range(2)]
        for h, queries, cols in segments(q_ref.shape[0], size):
            mine = turned_q[head_rows(h), queries]
            ques[:, cols] = beside(mine, h)
            sharp = mine.astype(F32)
            reach = jnp.sum(sharp * sharp, axis=0, keepdims=True)
            bound[:, cols] = jnp.sqrt(reach * tops[h] * 1.03) * factor

    cols = pl.ds(pl.multiple_of(pos * width, width), width)

    def weigh(peak):
        for start in range(0, width, across):
            own = slice(start, start + across)
            query = ques[:, pl.ds(pl.multiple_of(pos * width + start, across), across)]
            for at in range(0, kv, chunk):
                rows = slice(at, at + chunk)
                scores = jnp.dot(keys[rows, :], query, preferred_element_type=F32)
                p_ref[0, rows, own] = jnp.exp2(scores * factor - peak[:, own]).astype(BF16)
        total = jnp.dot(vals[...], p_ref[0], preferred_element_type=F32)
        sums = total[PAIR : PAIR + 1, :]
        sum_ref[0] = sums
        for h in range(2):
            own = slice(h * size, (h + 1) * size)
            turned[head_rows(h), :] = total[head_rows(h), own] / sums[:, own]
        return jnp.min(sums)

    def exact_peak():
        query = ques[:, cols]

        def largest(at, peak):
            rows = pl.ds(pl.multiple_of(at * chunk, chunk), chunk)
            scores = jnp.dot(keys[rows, :], query, preferred_element_type=F32)
            live = live_rows((chunk, width), 0, at * chunk, info[0], info[1], span)
            return jnp.maximum(peak, jnp.max(jnp.where(live, scores, -1e30), axis=0, keepdims=True))

        return lax.fori_loop(0, kv // chunk, largest, jnp.full((1, width), -1e30, F32)) * factor

    lowest = weigh(bound[:, cols])

    @pl.when(jnp.logical_not(lowest > 2.0**-70))
    def again():
        weigh(exact_peak())

    out_ref[...] = turned[...].T.astype(BF16)


def attend(info, q_from, k_from, v_from, span):
    (queries, q_at), (keys, k_at), (values, v_at) = q_from, k_from, v_from
    rows, kv = queries.shape[0], keys.shape[0]
    size = chunk_of(rows)
    pairs = HEADS // 2
    return pl.pallas_call(
        functools.partial(
            attend_kernel, chunk=min(256, kv), across=min(256, 2 * size), span=span
        ),
        out_shape=(
            jax.ShapeDtypeStruct((rows, HEADS * HDIM), BF16),
            jax.ShapeDtypeStruct((pairs, kv, 2 * rows), BF16),
            jax.ShapeDtypeStruct((pairs, 1, 2 * rows), F32),
        ),
        grid_spec=pltpu.PrefetchScalarGridSpec(
            num_scalar_prefetch=1,
            grid=(pairs, rows // size),
            in_specs=[
                pl.BlockSpec((rows, PAIR), lambda j, c, s: (0, q_at + j)),
                pl.BlockSpec((kv, PAIR), lambda j, c, s: (0, k_at + j)),
                pl.BlockSpec((kv, PAIR), lambda j, c, s: (0, v_at + j)),
            ],
            out_specs=(
                pl.BlockSpec((size, PAIR), lambda j, c, s: (c, j)),
                pl.BlockSpec((1, kv, 2 * size), lambda j, c, s: (j, 0, c)),
                pl.BlockSpec((1, 1, 2 * size), lambda j, c, s: (j, 0, c)),
            ),
            scratch_shapes=[
                pltpu.VMEM((kv, PAIR), BF16),
                pltpu.VMEM((PAIR + 16, kv), BF16),
                pltpu.VMEM((PAIR, 2 * rows), BF16),
                pltpu.VMEM((1, 2 * rows), F32),
                pltpu.VMEM((PAIR, size), F32),
            ],
        ),
        compiler_params=pltpu.CompilerParams(vmem_limit_bytes=60 * 2**20),
        name="attend",
    )(info, queries, keys, values)


def attend_back_kernel(
    info,
    units,
    q_ref,
    k_ref,
    v_ref,
    g_ref,
    ctx_ref,
    sum_ref,
    p_ref,
    *rest,
    chunk,
    size,
    span,
    more,
    extra,
):
    before, rest = (rest[:3], rest[3:]) if more else (None, rest)
    rest = rest[extra:]
    gq_ref, gk_ref, gv_ref, keys, grads, grads_up, ques_up, delta, low, total, key_sum, value_sum = rest
    step = pl.program_id(1)
    kv, rows = k_ref.shape[0], q_ref.shape[0]
    block, part = p_ref.shape[1:]
    scale = HDIM**-0.5

    @pl.when(step == 0)
    def prepare():
        live = live_rows((kv, PAIR), 0, 0, info[0], info[1], span)
        keys[...] = jnp.where(live, k_ref[...], jnp.zeros((), BF16)).T
        turned = g_ref[...].T.astype(F32)
        dots = turned * ctx_ref[...].T.astype(F32)
        for h, queries, cols in segments(rows, size):
            inverse = 1.0 / sum_ref[0, :, cols]
            own = head_rows(h)
            delta[:, cols] = jnp.sum(dots[own, queries], axis=0, keepdims=True) * inverse
            shared = beside((turned[own, queries] * inverse).astype(BF16), h)
            grads[:, cols] = shared
            grads_up[cols, :] = shared.T
            lane = lax.broadcasted_iota(jnp.int32, (queries.stop - queries.start, PAIR), 1)
            ques_up[cols, :] = jnp.where(lane // HDIM == h, q_ref[queries, :], jnp.zeros((), BF16))
        for held in (total, key_sum, value_sum):
            held[...] = jnp.zeros_like(held)

    here = pl.ds(pl.multiple_of(units[0, step] * block, block), block)
    there = pl.multiple_of(units[1, step] * part, part)
    cols = pl.ds(there, part)
    values = v_ref[here, :]
    for start in range(0, part, chunk):
        own = slice(start, start + chunk)
        from_all = pl.ds(there + start, chunk)
        change = jnp.dot(values, grads[:, from_all], preferred_element_type=F32)
        low[:, own] = (p_ref[0, :, own].astype(F32) * (change - delta[:, from_all])).astype(BF16)
    value_sum[here, :] += jnp.dot(p_ref[0], grads_up[cols, :], preferred_element_type=F32)
    key_sum[here, :] += jnp.dot(low[...], ques_up[cols, :], preferred_element_type=F32)
    total[:, cols] += jnp.dot(keys[:, here], low[...], preferred_element_type=F32)

    @pl.when(step == pl.num_programs(1) - 1)
    def finish():
        live = live_rows((kv, PAIR), 0, 0, info[0], info[1], span)
        zero = jnp.zeros((), F32)
        found = [jnp.where(live, key_sum[...] * scale, zero), jnp.where(live, value_sum[...], zero)]
        for t, (ref, value) in enumerate(zip((gk_ref, gv_ref), found)):
            if more:
                value += before[t + 1][...].astype(F32)
            ref[...] = value.astype(BF16)
        parts = [[], []]
        for h, queries, cols in segments(rows, size):
            parts[h].append(total[head_rows(h), cols])
        value = (jnp.concatenate([jnp.concatenate(p, 1) for p in parts], 0) * scale).T
        if more:
            value += before[0][...].astype(F32)
        gq_ref[...] = value.astype(BF16)


def attend_back(info, q_from, k_from, v_from, grad, context, sums, probs, span, units, before, events=()):
    (queries, q_at), (keys, k_at), (values, v_at) = q_from, k_from, v_from
    rows, kv = queries.shape[0], keys.shape[0]
    pairs = HEADS // 2
    wide = HEADS * HDIM
    more = before is not None
    block, part, size = min(1024, kv), rows, chunk_of(rows)
    cut = 2 if more else 1
    rows, kv = rows // cut, kv // cut
    out_rows = [rows, kv, kv]
    units = jnp.array(list(zip(*units)), jnp.int32)
    col = lambda height, at=0: pl.BlockSpec((height, PAIR), lambda j, c, s, u: (0, at + j))
    return pl.pallas_call(
        functools.partial(
            attend_back_kernel,
            chunk=min(512, part),
            size=size,
            span=span,
            more=more,
            extra=len(events),
        ),
        out_shape=tuple(jax.ShapeDtypeStruct((height, wide), BF16) for height in out_rows),
        grid_spec=pltpu.PrefetchScalarGridSpec(
            num_scalar_prefetch=2,
            grid=(pairs, units.shape[1]),
            in_specs=[
                col(rows, q_at),
                col(kv, k_at),
                col(kv, v_at),
                col(rows),
                col(rows),
                pl.BlockSpec((1, 1, 2 * rows), lambda j, c, s, u: (j, 0, 0)),
                pl.BlockSpec((1, block, part), lambda j, c, s, u: (j, u[0, c], u[1, c])),
            ]
            + ([col(height) for height in out_rows] if more else [])
            + any_specs(events),
            out_specs=tuple(col(height) for height in out_rows),
            scratch_shapes=[
                pltpu.VMEM((PAIR, kv), BF16),
                pltpu.VMEM((PAIR, 2 * rows), BF16),
                pltpu.VMEM((2 * rows, PAIR), BF16),
                pltpu.VMEM((2 * rows, PAIR), BF16),
                pltpu.VMEM((1, 2 * rows), F32),
                pltpu.VMEM((block, part), BF16),
                pltpu.VMEM((PAIR, 2 * rows), F32),
                pltpu.VMEM((kv, PAIR), F32),
                pltpu.VMEM((kv, PAIR), F32),
            ],
        ),
        compiler_params=pltpu.CompilerParams(vmem_limit_bytes=60 * 2**20),
        name="attend_back_last" if more else "attend_back",
    )(info, units, queries, keys, values, grad, context, sums, probs, *(before or ()), *events)


def rows_of(kept_ref, other_ref, step, split):
    return jnp.where(step < split, kept_ref[0], other_ref[...])


def project(rows, weight):
    return jnp.dot(rows, weight, preferred_element_type=F32)


def project_back(grads, weight):
    return lax.dot_general(grads, weight, (((1,), (1,)), ((), ())), preferred_element_type=F32)


def weight_grad(rows, grads):
    return lax.dot_general(rows, grads, (((0,), (0,)), ((), ())), preferred_element_type=F32)


def run_all(copies):
    for copy in copies:
        copy.start()
    return copies


def wait_all(copies):
    for copy in copies:
        copy.wait()


class Pieces:
    def __init__(self, shape, mesh_shape, bundles):
        self.r, self.c = shape
        self.m, self.n = mesh_shape
        self.bundles = bundles
        self.slots = self.m * self.n

    def place(self, masks, slot, info):
        if masks is None:
            return slot // self.n, lax.rem(slot, self.n)
        return info[5] ^ (masks[slot] // self.n), info[6] ^ (masks[slot] % self.n)

    def copies(self, refs, mats, sems, info, out):
        found = [[] for _ in mats]
        r, c = self.r, self.c
        count = 0
        for (masks, members), ref in zip(self.bundles, refs):
            for slot in range(self.slots if masks is None else len(masks)):
                j, i = self.place(masks, slot, info)
                at = 0
                for t in members:
                    mat = mats[t]
                    tall = mat.shape[0] // (self.m * r)
                    wide = mat.shape[1] // (self.n * c)
                    for w in range(wide):
                        if isinstance(ref, (tuple, list)):
                            each = self.slots // len(ref)
                            block = ref[slot // each].at[slot % each, pl.ds(at, tall * r), :]
                        else:
                            block = ref.at[slot, pl.ds(at, tall * r), :]
                        down = pl.multiple_of(j * (tall * r), tall * r)
                        side = pl.multiple_of((i * wide + w) * c, c)
                        place = mat.at[pl.ds(down, tall * r), pl.ds(side, c)]
                        at += tall * r
                        pair = (place, block) if out else (block, place)
                        found[t].append(pltpu.make_async_copy(*pair, sems.at[count]))
                        count += 1
        return found

    def count(self):
        return 9 * self.slots


def any_specs(arrays):
    return [pl.BlockSpec(memory_space=pl.ANY)] * len(arrays)


def queries_kernel(info, kept_ref, other_ref, bias_ref, *rest, split, grid_of):
    count = len(grid_of.bundles)
    packed, (out_ref, mat_q, mat_k, mat_v, sems) = rest[:count], rest[count:]
    step = pl.program_id(0)
    mats = [mat_q, mat_k, mat_v]

    @pl.when(step == 0)
    def load():
        loads = grid_of.copies(packed, mats, sems, info, False)
        for group in loads:
            run_all(group)
        for group in loads:
            wait_all(group)

    rows = rows_of(kept_ref, other_ref, step, split)
    width = mat_q.shape[1]
    for t, mat in enumerate(mats):
        cols = slice(t * width, (t + 1) * width)
        out_ref[:, cols] = (project(rows, mat[...]) + bias_ref[:, cols]).astype(BF16)


def split_specs(kept_at, tile, split, width):
    return [
        pl.BlockSpec((1, tile, width), lambda i, s: (s[kept_at], jnp.minimum(i, split - 1), 0)),
        pl.BlockSpec((tile, width), lambda i, s: (jnp.maximum(i - split, 0), 0)),
    ]


def whole_spec(shape):
    return pl.BlockSpec(shape, lambda i, s: (0,) * len(shape))


def queries_keys_values(info, kept, other, weights, bias):
    block_len, width = other.shape
    tile = min(512, block_len)
    split = block_len // tile
    mat = jax.ShapeDtypeStruct((width, width), BF16)
    return pl.pallas_call(
        functools.partial(queries_kernel, split=split, grid_of=weights.grid_of),
        out_shape=(jax.ShapeDtypeStruct((2 * block_len, 3 * width), BF16), mat, mat, mat),
        grid_spec=pltpu.PrefetchScalarGridSpec(
            num_scalar_prefetch=1,
            grid=(2 * split,),
            in_specs=split_specs(2, tile, split, width)
            + [whole_spec(bias.shape)]
            + any_specs(weights.packed),
            out_specs=(pl.BlockSpec((tile, 3 * width), lambda i, s: (i, 0)),)
            + (whole_spec(mat.shape),) * 3,
            scratch_shapes=[pltpu.SemaphoreType.DMA((weights.grid_of.count(),))],
        ),
        compiler_params=pltpu.CompilerParams(vmem_limit_bytes=60 * 2**20),
        name="queries",
    )(info, kept, other, bias, *weights.packed)


def normal(values):
    middle = jnp.mean(values, axis=-1, keepdims=True)
    centered = values - middle
    spread = jnp.mean(centered * centered, axis=-1, keepdims=True)
    inverse = lax.rsqrt(spread + 1e-12)
    return centered * inverse, inverse


def normal_back(grad, unit, inverse, gain):
    scaled = grad * gain
    mean = jnp.mean(scaled, axis=-1, keepdims=True)
    along = jnp.mean(scaled * unit, axis=-1, keepdims=True)
    return (scaled - mean - unit * along) * inverse


def gelu_pair(u):
    phi = 0.5 + 0.5 * lax.erf(0.7071067811865476 * u)
    bell = jnp.exp2((-0.5 * LOG2E) * (u * u))
    return u * phi, phi + (0.3989422804014327 * u) * bell


def add_rows(total, at, values):
    total[at : at + 1, 0 : values.shape[1]] += jnp.sum(values, axis=0, keepdims=True)


def middle_kernel(
    info,
    hid_kept,
    hid_other,
    cot_kept,
    cot_other,
    ctx_ref,
    cls_ref,
    vec_ref,
    inner_bias,
    packed,
    layer_kept,
    layer_other,
    top_ref,
    grad_ctx_ref,
    resid_ref,
    sums_ref,
    mat_out,
    mat_inner,
    mat_outer,
    acc_out,
    acc_inner,
    acc_outer,
    totals,
    active,
    slope,
    low,
    vec_low,
    sems,
    vec_sems,
    *,
    split,
    grid_of,
    chunk,
):
    step = pl.program_id(0)
    last = pl.num_programs(0) - 1
    mats = [mat_out, mat_inner, mat_outer]
    tile, width = ctx_ref.shape
    ff = mat_inner.shape[1]
    loads = grid_of.copies([packed], mats, sems, info, False)

    @pl.when(step == 0)
    def start():
        for group in loads:
            run_all(group)
        for acc in (acc_out, acc_inner, acc_outer, totals):
            acc[...] = jnp.zeros_like(acc)
        wait_all(loads[0])

    bias_out, gain_one, shift_one, bias_outer, gain_two, shift_two = [
        vec_ref[t : t + 1, :] for t in range(6)
    ]
    hidden = rows_of(hid_kept, hid_other, step, split).astype(F32)
    context = ctx_ref[...]
    unit_one, inverse_one = normal(hidden + project(context, mat_out[...]) + bias_out)
    normed = unit_one * gain_one + shift_one
    normed_low = normed.astype(BF16)

    @pl.when(step == 0)
    def more():
        wait_all(loads[1])
        wait_all(loads[2])

    for at in range(0, ff, chunk):
        cols = slice(at, at + chunk)
        inner = project(normed_low, mat_inner[:, cols]) + inner_bias[:, cols]
        value, change = gelu_pair(inner)
        active[:, cols] = value.astype(BF16)
        slope[:, cols] = change.astype(BF16)
    unit_two, inverse_two = normal(normed + project(active[...], mat_outer[...]) + bias_outer)
    layer = (unit_two * gain_two + shift_two).astype(BF16)

    @pl.when(step < split)
    def kept():
        layer_kept[0] = layer

    @pl.when(step >= split)
    def other():
        layer_other[...] = layer

    @pl.when(step * tile == info[1])
    def top():
        top_ref[...] = layer[0:16, :]


    row = step * tile + lax.broadcasted_iota(jnp.int32, (tile, width), 0)
    grad_result = rows_of(cot_kept, cot_other, step, split).astype(F32)
    grad_result += jnp.where(row == info[4], cls_ref[...], 0.0)
    add_rows(totals, 4, grad_result * unit_two)
    add_rows(totals, 5, grad_result)
    grad_resid_two = normal_back(grad_result, unit_two, inverse_two, gain_two)
    grad_outer = grad_resid_two.astype(BF16)
    add_rows(totals, 3, grad_outer.astype(F32))
    for at in range(0, ff, chunk):
        cols = slice(at, at + chunk)
        grad_inner = project_back(grad_outer, mat_outer[cols, :]) * slope[:, cols].astype(F32)
        low[:, cols] = grad_inner.astype(BF16)
        totals[8:9, cols] += jnp.sum(grad_inner, axis=0, keepdims=True)
        acc_outer[cols, :] += weight_grad(active[:, cols], grad_outer)
    grad_normed = grad_resid_two + project_back(low[...], mat_inner[...])
    for at in range(0, ff, chunk):
        cols = slice(at, at + chunk)
        acc_inner[:, cols] += weight_grad(normed_low, low[:, cols])
    add_rows(totals, 1, grad_normed * unit_one)
    add_rows(totals, 2, grad_normed)
    grad_resid_one = normal_back(grad_normed, unit_one, inverse_one, gain_one)
    resid_ref[...] = grad_resid_one
    grad_attn = grad_resid_one.astype(BF16)
    add_rows(totals, 0, grad_attn.astype(F32))
    acc_out[...] += weight_grad(context, grad_attn)
    grad_ctx_ref[...] = project_back(grad_attn, mat_out[...]).astype(BF16)

    @pl.when(step == last)
    def finish():
        r, c, m, n = grid_of.r, grid_of.c, grid_of.m, grid_of.n
        stores = grid_of.copies([sums_ref], mats, sems, info, True)
        for mat, acc, group in zip(mats, (acc_out, acc_inner, acc_outer), stores):
            mat[...] = acc[...].astype(BF16)
            run_all(group)
        vec_low[...] = jnp.zeros_like(vec_low)
        for i in range(n):
            for t in range(6):
                vec_low[i, t : t + 1, :] = totals[t : t + 1, i * c : (i + 1) * c]
            wide = ff // (n * c)
            for t in range(wide):
                at = (i * wide + t) * c
                vec_low[i, 6 + t : 7 + t, :] = totals[8:9, at : at + c]
        tails = []
        vec_bits = vec_low[...].astype(BF16)
        for i in range(n):
            active[16 * i : 16 * i + 16, 0:c] = vec_bits[i]
        for j in range(m):
            for i in range(n):
                tails.append(
                    pltpu.make_async_copy(
                        active.at[pl.ds(16 * i, 16), pl.ds(0, c)],
                        sums_ref.at[j * n + i, pl.ds(9 * r, 16), :],
                        vec_sems.at[j * n + i],
                    )
                )
        run_all(tails)
        for group in stores:
            wait_all(group)
        wait_all(tails)


def kept_spec(tile, split, width):
    return pl.BlockSpec((1, tile, width), lambda i, s: (s[2], jnp.minimum(i, split - 1), 0))


def other_spec(tile, split, width):
    return pl.BlockSpec((tile, width), lambda i, s: (jnp.maximum(i - split, 0), 0))


def middle(info, hidden, cots, context, cls_row, weights, vectors, inner_bias):
    block_len, width = hidden[1].shape
    grid_of = weights.grid_of
    ff = inner_bias.shape[1]
    tile = min(256, block_len)
    split = block_len // tile
    row_spec = pl.BlockSpec((tile, width), lambda i, s: (i, 0))
    return pl.pallas_call(
        functools.partial(middle_kernel, split=split, grid_of=grid_of, chunk=768),
        out_shape=(
            jax.ShapeDtypeStruct(hidden[0].shape, BF16),
            jax.ShapeDtypeStruct((block_len, width), BF16),
            jax.ShapeDtypeStruct((16, width), BF16),
            jax.ShapeDtypeStruct((2 * block_len, width), BF16),
            jax.ShapeDtypeStruct((2 * block_len, width), F32),
            jax.ShapeDtypeStruct((grid_of.slots, 9 * grid_of.r + 16, grid_of.c), BF16),
        ),
        grid_spec=pltpu.PrefetchScalarGridSpec(
            num_scalar_prefetch=1,
            grid=(2 * split,),
            in_specs=split_specs(2, tile, split, width)
            + split_specs(2, tile, split, width)
            + [
                row_spec,
                whole_spec(cls_row.shape),
                whole_spec(vectors.shape),
                whole_spec(inner_bias.shape),
                pl.BlockSpec(memory_space=pl.ANY),
            ],
            out_specs=(
                kept_spec(tile, split, width),
                other_spec(tile, split, width),
                whole_spec((16, width)),
                row_spec,
                row_spec,
                pl.BlockSpec(memory_space=pl.ANY),
            ),
            scratch_shapes=[
                pltpu.VMEM((width, width), BF16),
                pltpu.VMEM((width, ff), BF16),
                pltpu.VMEM((ff, width), BF16),
                pltpu.VMEM((width, width), F32),
                pltpu.VMEM((width, ff), F32),
                pltpu.VMEM((ff, width), F32),
                pltpu.VMEM((16, ff), F32),
                pltpu.VMEM((tile, ff), BF16),
                pltpu.VMEM((tile, ff), BF16),
                pltpu.VMEM((tile, ff), BF16),
                pltpu.VMEM((grid_of.n, 16, grid_of.c), F32),
                pltpu.SemaphoreType.DMA((grid_of.count(),)),
                pltpu.SemaphoreType.DMA((grid_of.slots,)),
            ],
        ),
        compiler_params=pltpu.CompilerParams(vmem_limit_bytes=60 * 2**20),
        name="middle",
    )(info, *hidden, *cots, context, cls_row, vectors, inner_bias, *weights.packed)


def input_grad_kernel(info, gq_ref, gk_ref, gv_ref, resid_ref, mat_q, mat_k, mat_v, grad_ref, *, kept):
    total = resid_ref[...]
    for ref, mat in zip((gq_ref, gk_ref, gv_ref), (mat_q, mat_k, mat_v)):
        total += project_back(ref[...], mat[...])
    if kept:
        grad_ref[0] = total.astype(grad_ref.dtype)
    else:
        grad_ref[...] = total.astype(grad_ref.dtype)


def input_grad(info, grads, resid, mats, out_shape, dtype, kept):
    rows, width = resid.shape
    block_len = rows // 2
    tile = min(512, block_len)
    split = block_len // tile
    off = 0 if kept else split
    spec = pl.BlockSpec((tile, width), lambda i, s: (i + off, 0))
    place = kept_spec(tile, split, width) if kept else other_spec(tile, 0, width)
    return pl.pallas_call(
        functools.partial(input_grad_kernel, kept=kept),
        out_shape=jax.ShapeDtypeStruct(out_shape, dtype),
        grid_spec=pltpu.PrefetchScalarGridSpec(
            num_scalar_prefetch=1,
            grid=(split,),
            in_specs=[spec] * 4 + [whole_spec(mat.shape) for mat in mats],
            out_specs=place,
        ),
        compiler_params=pltpu.CompilerParams(vmem_limit_bytes=60 * 2**20),
        name="input_grad_kept" if kept else "input_grad_other",
    )(info, *grads, resid, *mats)


def head_grads_kernel(info, hid_kept, hid_other, *rest, split, grid_of, outs, extra):
    kept, other, rest = rest[:3], rest[3:6], rest[6 + extra :]
    sums, (acc, mat_q, mat_k, mat_v, totals, vec_low, sems, vec_sems) = rest[:outs], rest[outs:]
    mats = [mat_q, mat_k, mat_v]
    step = pl.program_id(0)

    @pl.when(step == 0)
    def clear():
        acc[...] = jnp.zeros_like(acc)
        totals[...] = jnp.zeros_like(totals)

    rows = rows_of(hid_kept, hid_other, step, split)
    grads = [jnp.where(step < split, a[...], b[...]) for a, b in zip(kept, other)]
    for t, grad in enumerate(grads):
        acc[t] += weight_grad(rows, grad)
    add_rows(totals, 0, grads[0].astype(F32))
    add_rows(totals, 1, grads[2].astype(F32))

    @pl.when(step == pl.num_programs(0) - 1)
    def finish():
        r, c, n = grid_of.r, grid_of.c, grid_of.n
        ((masks, _),) = grid_of.bundles
        stores = grid_of.copies([list(sums)], mats, sems, info, True)
        for t, mat in enumerate(mats):
            mat[...] = acc[t].astype(BF16)
            run_all(stores[t])
        for i in range(n):
            part = jnp.concatenate([totals[0:2, i * c : (i + 1) * c], jnp.zeros((14, c), F32)], 0)
            vec_low[i] = part.astype(BF16)
        tails = []
        each = grid_of.slots // outs
        for slot in range(grid_of.slots):
            j, i = grid_of.place(masks, slot, info)
            place = sums[slot // each].at[slot % each, pl.ds(3 * r, 16), :]
            tails.append(pltpu.make_async_copy(vec_low.at[i], place, vec_sems.at[slot]))
        run_all(tails)
        for group in stores:
            wait_all(group)
        wait_all(tails)


def head_grads(info, hidden, kept, other, grid_of, outs, events=()):
    block_len, width = hidden[1].shape
    tile = min(512, block_len)
    split = block_len // tile
    last = other[0].shape[0] // tile - split
    kept_rows = pl.BlockSpec((tile, width), lambda i, s: (jnp.minimum(i, split - 1), 0))
    other_rows = pl.BlockSpec((tile, width), lambda i, s: (jnp.maximum(i, split), 0))
    block = (grid_of.slots // outs, 3 * grid_of.r + 16, grid_of.c)
    return pl.pallas_call(
        functools.partial(
            head_grads_kernel, split=split, grid_of=grid_of, outs=outs, extra=len(events)
        ),
        out_shape=(jax.ShapeDtypeStruct(block, BF16),) * outs,
        grid_spec=pltpu.PrefetchScalarGridSpec(
            num_scalar_prefetch=1,
            grid=(2 * split,),
            in_specs=split_specs(2, tile, split, width) + [kept_rows] * 3 + [other_rows] * 3 + any_specs(events),
            out_specs=(pl.BlockSpec(memory_space=pl.ANY),) * outs,
            scratch_shapes=[pltpu.VMEM((3, width, width), F32)]
            + [pltpu.VMEM((width, width), BF16)] * 3
            + [
                pltpu.VMEM((8, width), F32),
                pltpu.VMEM((grid_of.n, 16, grid_of.c), BF16),
                pltpu.SemaphoreType.DMA((grid_of.count(),)),
                pltpu.SemaphoreType.DMA((grid_of.slots,)),
            ],
        ),
        compiler_params=pltpu.CompilerParams(vmem_limit_bytes=60 * 2**20),
        name="head_grads",
    )(info, *hidden, *kept, *other, *events)


def pick_kernel(info, pair_ref, *rest):
    rest[-1][...] = pair_ref[0]


def pick_other(info, pair, events):
    _, block_len, width = pair.shape
    tile = min(512, block_len)
    return pl.pallas_call(
        pick_kernel,
        out_shape=jax.ShapeDtypeStruct((block_len, width), pair.dtype),
        grid_spec=pltpu.PrefetchScalarGridSpec(
            num_scalar_prefetch=1,
            grid=(block_len // tile,),
            in_specs=[pl.BlockSpec((1, tile, width), lambda i, s: (1 - s[2], i, 0))]
            + any_specs(events),
            out_specs=pl.BlockSpec((tile, width), lambda i, s: (i, 0)),
        ),
        compiler_params=pltpu.CompilerParams(vmem_limit_bytes=60 * 2**20),
        name="pick_other",
    )(info, pair, *events)


def pack_kernel(*refs, count):
    out = refs[-1]
    c = out.shape[1]
    at = 0
    for ref in refs[:count]:
        rows, cols = ref.shape
        for start in range(0, cols, c):
            out[at : at + rows, :] = ref[:, start : start + c]
            at += rows


def pack_after(shards, events):
    c = min(s.shape[1] for s in shards)
    rows = sum(s.size for s in shards) // c
    return pl.pallas_call(
        functools.partial(pack_kernel, count=len(shards)),
        out_shape=jax.ShapeDtypeStruct((rows, c), BF16),
        in_specs=[pl.BlockSpec(memory_space=pltpu.VMEM)] * len(shards) + any_specs(events),
        compiler_params=pltpu.CompilerParams(vmem_limit_bytes=60 * 2**20),
        name="pack",
    )(*shards, *events)


def stack_kernel(*refs, count, outs):
    at = 0
    for out in refs[-outs:]:
        rows = out.shape[1]
        for k, ref in enumerate(refs[:count]):
            out[k] = ref[at : at + rows, :]
        at += rows


def stack_rows(blocks, cuts, events):
    c = blocks[0].shape[1]
    return pl.pallas_call(
        functools.partial(stack_kernel, count=len(blocks), outs=len(cuts)),
        out_shape=tuple(jax.ShapeDtypeStruct((len(blocks), rows, c), BF16) for rows in cuts),
        in_specs=[pl.BlockSpec(memory_space=pltpu.VMEM)] * len(blocks) + any_specs(events),
        compiler_params=pltpu.CompilerParams(vmem_limit_bytes=60 * 2**20),
        name="stack_rows",
    )(*blocks, *events)


def add_kernel(*refs, count, extra):
    parts, outs = refs[:count], refs[count + extra :]
    each = outs[0].shape[0]
    for k, out in enumerate(outs):
        here = slice(k * each, (k + 1) * each)
        out[...] = sum(part[here].astype(F32) for part in parts).astype(BF16)


def add_blocks(parts, groups, events):
    shape = (parts[0].shape[0] // groups,) + parts[0].shape[1:]
    return pl.pallas_call(
        functools.partial(add_kernel, count=len(parts), extra=len(events)),
        out_shape=(jax.ShapeDtypeStruct(shape, BF16),) * groups,
        in_specs=[pl.BlockSpec(memory_space=pltpu.VMEM)] * len(parts) + any_specs(events),
        compiler_params=pltpu.CompilerParams(vmem_limit_bytes=60 * 2**20),
        name="add_blocks",
    )(*parts, *events)


def place_kernel(info, base_ref, other_ref, out_ref):
    out_ref[0] = other_ref[...].astype(out_ref.dtype)


def place_other(info, base, other):
    block_len, width = other.shape
    tile = min(512, block_len)
    return pl.pallas_call(
        place_kernel,
        out_shape=jax.ShapeDtypeStruct(base.shape, base.dtype),
        grid_spec=pltpu.PrefetchScalarGridSpec(
            num_scalar_prefetch=1,
            grid=(block_len // tile,),
            in_specs=[
                pl.BlockSpec(memory_space=pl.ANY),
                pl.BlockSpec((tile, width), lambda i, s: (i, 0)),
            ],
            out_specs=pl.BlockSpec((1, tile, width), lambda i, s: (1 - s[2], i, 0)),
        ),
        input_output_aliases={1: 0},
        compiler_params=pltpu.CompilerParams(vmem_limit_bytes=60 * 2**20),
        name="place_other",
    )(info, base, other)


def swap(block, axis, route):
    if all(a == b for a, b in route):
        return block
    return lax.ppermute(block, axis, route)


class Regroup:
    def __init__(self):
        self.n = lax.axis_size("blk")
        self.me = lax.axis_index("blk")
        self.per = self.n // 2
        self.passage = self.me // self.per
        self.part = lax.rem(self.me, 2)
        self.first = [(i, (i % 2) * self.per + i // 2) for i in range(self.n)]
        self.second = [(i, (1 - i % 2) * self.per + i // 2) for i in range(self.n)]
        self.stays = all(a == b for a, b in self.first)

    def pick(self, info, pair, events=()):
        if self.stays:
            return pick_other(info, pair, events)
        return lax.dynamic_index_in_dim(pair, 1 - self.part, 0, keepdims=False)

    def gather(self, pair, picked):
        other = swap(picked, "blk", self.second)
        if self.stays:
            return (pair, other)
        kept = lax.dynamic_index_in_dim(pair, self.part, 0, keepdims=True)
        return (swap(kept, "blk", self.first), other)

    def kept_index(self):
        return self.part if self.stays else jnp.zeros_like(self.part)

    def all_blocks(self, block):
        if self.n != 2:
            return lax.all_gather(block, "blk", axis=0)
        other = lax.ppermute(block, "blk", [(0, 1), (1, 0)])
        return jnp.where(self.me == 0, jnp.stack([block, other]), jnp.stack([other, block]))

    def send_back(self, other):
        return swap(other, "blk", [(b, a) for a, b in self.second])

    def join(self, info, kept, other):
        if self.stays:
            return place_other(info, kept, other)
        kept = swap(kept[0], "blk", [(b, a) for a, b in self.first])
        other = other.astype(kept.dtype)
        return jnp.where(self.part == 0, jnp.stack([kept, other]), jnp.stack([other, kept]))


def pack(shards):
    c = min(s.shape[1] for s in shards)
    return jnp.concatenate(
        [s[:, at : at + c] for s in shards for at in range(0, s.shape[1], c)], axis=0
    )


def unpack(block, shapes):
    c = block.shape[-1]
    found, at = [], 0
    for rows, cols in shapes:
        parts = []
        for _ in range(cols // c):
            parts.append(block[..., at : at + rows, :])
            at += rows
        found.append(jnp.concatenate(parts, axis=-1) if len(parts) > 1 else parts[0])
    return found


def exchanged(block, mask):
    both = ("batch", "blk")
    places = range(lax.axis_size("batch") * lax.axis_size("blk"))
    return lax.ppermute(block, both, [(i, i ^ mask) for i in places])


def xor_gather(block, stages):
    found, masks = block[None], [0]
    for stage in stages:
        parts = [found] + [exchanged(found, mask) for mask in stage]
        masks = masks + [held ^ mask for mask in stage for held in masks]
        found = jnp.concatenate(parts, 0)
    return found, masks


def xor_masks(stages):
    masks = [0]
    for stage in stages:
        masks = [held ^ mask for held in masks for mask in [0] + stage]
    return masks


def xor_sum(groups, stages, meanwhile):
    for at, stage in enumerate(stages):
        parts = [groups[0]] + [exchanged(g, mask) for mask, g in zip(stage, groups[1:])]
        if at == len(stages) - 1:
            return [part[0] for part in parts]
        events = meanwhile if at == len(stages) - 2 else ()
        groups = add_blocks(parts, len(stages[at + 1]) + 1, events)


class Weights:
    def __init__(self, shards, by_pairs, events=()):
        self.shapes = [s.shape for s in shards]
        self.m, self.n = lax.axis_size("batch"), lax.axis_size("blk")
        m, n = self.m, self.n
        r, c = min(s[0] for s in self.shapes), min(s[1] for s in self.shapes)
        self.fits = r % 16 == 0 and c % 128 == 0
        powers = m & (m - 1) == 0 and n & (n - 1) == 0 and m >= 8
        self.by_pairs = by_pairs and self.fits and powers
        every = list(range(len(shards)))
        if self.by_pairs:
            y, core, x = list(range(1, n)), [n], [2 * n]
            z = list(range(4 * n, m * n, 4 * n))
            near = pack_after(shards, ())
            near = [near] + [exchanged(near, mask) for mask in y]
            cut = sum(s.size for s in shards[:-1]) // c
            cuts = [cut, near[0].shape[0] - cut]
            near = stack_rows(near, cuts, events(near))
            self.packed, bundles, self.half = [], [], []
            for rows, members, order in (
                (near[0], every[:-1], [z, x]),
                (near[1], every[-1:], [x, z]),
            ):
                part, masks = xor_gather(rows, order[:1])
                self.half.append(part)
                part, more = xor_gather(part, order[1:])
                masks = [a ^ b for a in more for b in masks]
                for mask in [0] + core:
                    block = exchanged(part, mask) if mask else part
                    self.packed.append(block.reshape(-1, *rows.shape[1:]))
                    bundles.append(([a ^ b ^ mask for a in masks for b in [0] + y], members))
            self.grid_of = Pieces((r, c), (m, n), bundles)
            self.stages = [core, [a ^ b for a in [0] + x for b in [0] + y][1:], z]
            self.sums_of = Pieces((r, c), (m, n), [(xor_masks(self.stages), every)])
            return
        if callable(events):
            events = ()
        packed = pack_after(shards, events) if self.fits else pack(shards)
        packed = lax.all_gather(packed, ("batch", "blk"), axis=0)
        if self.fits:
            self.grid_of = Pieces((r, c), (m, n), [(None, every)])
            self.packed = [packed]
        else:
            self.grid_of = Pieces((r * m, c * n), (1, 1), [(None, every)])
            whole = []
            for part in unpack(packed, self.shapes):
                rows, cols = part.shape[1:]
                part = part.reshape(m, n, rows, cols).transpose(0, 2, 1, 3)
                whole.append(part.reshape(m * rows, n * cols))
            self.packed = [pack(whole)[None]]
        self.sums_of = self.grid_of

    def halfway(self):
        return tuple(self.half) if self.by_pairs else ()

    def scatter(self, sums, meanwhile=()):
        extra = 16
        if self.by_pairs:
            return finish_sums(xor_sum(sums, self.stages, meanwhile), self.shapes)
        (sums,) = sums
        if not self.fits:
            rows = sums.shape[1] - extra
            wide = [(a * self.m, b * self.n) for a, b in self.shapes]
            parts = []
            for part in unpack(sums[0, :rows], wide):
                a, b = part.shape[0] // self.m, part.shape[1] // self.n
                part = part.reshape(self.m, a, self.n, b).transpose(0, 2, 1, 3)
                parts.append(part.reshape(self.m * self.n, a, b))
            c = min(s[1] for s in self.shapes)
            blocks = jnp.stack([pack([p[d] for p in parts]) for d in range(self.m * self.n)])
            vecs = sums[0, rows:].reshape(extra, self.n, c).transpose(1, 0, 2)
            vecs = jnp.broadcast_to(vecs[None], (self.m, self.n, extra, c))
            sums = jnp.concatenate([blocks, vecs.reshape(self.m * self.n, extra, c)], axis=1)
        height, c = sums.shape[1:]
        own = lax.psum_scatter(
            sums.reshape(-1, c), ("batch", "blk"), scatter_dimension=0, tiled=True
        )
        return finish_sums([own], self.shapes)


def finish_kernel(*refs, count):
    parts, outs = refs[:count], refs[count:]
    at = 0
    for out in outs:
        rows, cols = out.shape
        c = parts[0].shape[1]
        for start in range(0, cols, c):
            here = slice(at, at + rows)
            out[:, start : start + c] = sum(part[here, :].astype(F32) for part in parts)
            at += rows


def finish_sums(parts, shapes):
    height, c = parts[0].shape
    used = sum(a * b for a, b in shapes) // c
    shapes = list(shapes) + [(height - used, c)]
    if used % 16:
        total = sum(part.astype(F32) for part in parts)
        return [*unpack(total[:used], shapes[:-1]), total[used:]]
    return pl.pallas_call(
        functools.partial(finish_kernel, count=len(parts)),
        out_shape=tuple(jax.ShapeDtypeStruct(shape, F32) for shape in shapes),
        compiler_params=pltpu.CompilerParams(vmem_limit_bytes=60 * 2**20),
        name="finish_sums",
    )(*parts)


def on_device(
    hidden_in,
    lengths,
    cot_out,
    cot_cls,
    w_query,
    w_key,
    w_value,
    w_out,
    w_inner,
    w_outer,
    b_query,
    b_value,
    b_out,
    norm1_gain,
    norm1_shift,
    b_inner,
    b_outer,
    norm2_gain,
    norm2_shift,
):
    plan = Regroup()
    groups, block_len, width = hidden_in.shape
    span = groups * block_len
    per = plan.per
    fleets = [[i * per + j for j in range(per)] for i in range(2)]
    first_row = plan.passage * block_len
    owner = lax.rem(plan.me, per) == 0

    length = lax.dynamic_index_in_dim(lengths, plan.passage, 0, keepdims=False)
    info = jnp.stack(
        [
            length,
            first_row,
            plan.kept_index(),
            plan.kept_index(),
            jnp.where(owner, first_row, -1),
            lax.axis_index("batch"),
            plan.me,
        ]
    ).astype(jnp.int32)

    share = width // plan.n
    narrow = jnp.stack(
        [b_query, b_value, b_out, norm1_gain, norm1_shift, b_outer, norm2_gain, norm2_shift]
    )
    vec_all = plan.all_blocks(jnp.concatenate([narrow, b_inner.reshape(-1, share)], 0)).astype(F32)
    narrow = vec_all[:, :8].transpose(1, 0, 2).reshape(8, width)
    bias_inner = vec_all[:, 8:].reshape(1, -1)
    bias_heads = jnp.concatenate([narrow[0:1], jnp.zeros_like(narrow[0:1]), narrow[1:2]], 1)

    picked = []

    def pick_hidden(near):
        picked.append(plan.pick(info, hidden_in, near))
        return picked

    heads = Weights([w_query, w_key, w_value], True, pick_hidden)
    hidden = plan.gather(hidden_in, picked[0] if picked else plan.pick(info, hidden_in))
    dense = Weights([w_out, w_inner, w_outer], False, heads.halfway())
    qkv, *mats = queries_keys_values(info, *hidden, heads, bias_heads)
    cots = plan.gather(cot_out, plan.pick(info, cot_out, (qkv,)))
    if per == 1:
        kv, key_at = qkv, width // PAIR
    else:
        kv = lax.all_gather(qkv[:, width:], "blk", axis=0, tiled=True, axis_index_groups=fleets)
        key_at = 0
    sources = ((qkv, 0), (kv, key_at), (kv, key_at + width // PAIR))
    context_low, probs, sums = attend(info, *sources, span)

    own_cls = lax.dynamic_index_in_dim(cot_cls, plan.passage, 0, keepdims=True).astype(F32)
    layer_kept, layer_other, top, grad_context, grad_resid, dense_sums = middle(
        info, hidden, cots, context_low, own_cls, dense, narrow[2:], bias_inner
    )
    part_wo, part_wi, part_wu, dense_vecs = dense.scatter([dense_sums])
    part_bo, part_g1, part_s1, part_bu, part_g2, part_s2 = [dense_vecs[t] for t in range(6)]
    part_bi = dense_vecs[6 : 6 + b_inner.size // share].reshape(-1)
    layer_rows = plan.join(info, layer_kept, plan.send_back(layer_other))
    tops = plan.all_blocks(top)[::per, 0, :]
    cls_part = lax.dynamic_slice_in_dim(tops, plan.me * share, share, 1)

    back = functools.partial(
        attend_back, info, *sources, grad_context, context_low, sums, probs, span
    )
    give = functools.partial(input_grad, info, resid=grad_resid, mats=mats)
    if per == 1:
        most = back([(1, 1), (1, 0), (0, 1)], None)
        other = give(most, out_shape=(block_len, width), dtype=BF16, kept=False)
        rest = back([(0, 0)], most, (other, layer_rows))
        other = plan.send_back(other)
    else:
        blocks = span * per // min(1024, span * per)
        grad_q, *grad_kv = back([(k, q) for k in range(blocks) for q in range(2)], None)
        most = [grad_q] + [
            lax.psum_scatter(g, "blk", scatter_dimension=0, tiled=True, axis_index_groups=fleets)
            for g in grad_kv
        ]
        other = plan.send_back(give(most, out_shape=(block_len, width), dtype=BF16, kept=False))
        rest = most
    head_sums = head_grads(
        info, hidden, rest, most, heads.sums_of, 2 if heads.by_pairs else 1, (other,)
    )
    kept = give(rest, out_shape=hidden[0].shape, dtype=F32, kept=True)
    grad_input = plan.join(info, kept, other)
    part_wq, part_wk, part_wv, head_vecs = heads.scatter(head_sums, (grad_input,))
    part_bq, part_bv = head_vecs[0], head_vecs[1]
    return (
        layer_rows,
        cls_part,
        grad_input,
        part_wq,
        part_wk,
        part_wv,
        part_wo,
        part_wi,
        part_wu,
        part_bq,
        part_bv,
        part_bo,
        part_g1,
        part_s1,
        part_bi,
        part_bu,
        part_g2,
        part_s2,
    )


def solution(mesh):
    rows = P("batch", "blk", None)
    mats = (P("batch", "blk"),) * 6
    vecs = (P("blk"),) * 9
    return jax.shard_map(
        on_device,
        mesh=mesh,
        in_specs=(rows, P("batch"), rows, P("batch", None)) + mats + vecs,
        out_specs=(rows, P("batch", "blk"), rows) + mats + vecs,
        check_vma=False,
    )
```

```python
import functools

import jax
import jax.numpy as jnp
from jax import lax
from jax.experimental import pallas as pl
from jax.experimental.pallas import tpu as pltpu
from jax.sharding import PartitionSpec as P

HEADS = 12
HDIM = 64
PAIR = 2 * HDIM
LOG2E = 1.4426950408889634
BF16 = jnp.bfloat16
F32 = jnp.float32


def live_rows(shape, axis, start, length, shift, span):
    rows = shape[axis]
    step = min(rows, span)
    parts = []
    for at in range(0, rows, step):
        first = start + at
        base = (first // span) * span
        sizes = list(shape)
        sizes[axis] = step
        turned = lax.broadcasted_iota(jnp.int32, tuple(sizes), axis) + (first - base + shift)
        turned = jnp.where(turned >= span, turned - span, turned)
        parts.append(turned < length - base)
    return parts[0] if len(parts) == 1 else jnp.concatenate(parts, axis)


def chunk_of(rows):
    return min(1024, rows // 2)


def segments(rows, size):
    for at in range(0, rows, size):
        for h in range(2):
            yield h, slice(at, at + size), slice(2 * at + h * size, 2 * at + (h + 1) * size)


def beside(part, h):
    blank = jnp.zeros_like(part)
    return jnp.concatenate([part, blank] if h == 0 else [blank, part], 0)


def head_rows(h):
    return slice(h * HDIM, (h + 1) * HDIM)


def attend_kernel(
    info, q_ref, k_ref, v_ref, *rest, chunk, across, span, extra
):
    out_ref, p_ref, sum_ref, keys, vals, ques, bound, turned = rest[extra:]
    pos = pl.program_id(1)
    kv = k_ref.shape[0]
    size, width = out_ref.shape[0], p_ref.shape[2]
    factor = HDIM**-0.5 * LOG2E

    @pl.when(pos == 0)
    def prepare():
        live = live_rows((kv, PAIR), 0, 0, info[0], info[1], span)
        kept = jnp.where(live, k_ref[...], jnp.zeros((), BF16))
        keys[...] = kept
        vals[0:PAIR, :] = jnp.where(live, v_ref[...], jnp.zeros((), BF16)).T
        vals[PAIR:, :] = live_rows((16, kv), 1, 0, info[0], info[1], span).astype(BF16)
        turned_q = q_ref[...].T
        squares = kept.astype(F32)
        squares = (squares * squares).astype(BF16)
        half = lambda axis: lax.broadcasted_iota(jnp.int32, (PAIR, PAIR), axis) // HDIM
        sizes = jnp.dot(squares, (half(0) == half(1)).astype(BF16), preferred_element_type=F32)
        largest = jnp.max(sizes, axis=0, keepdims=True)
        tops = [jnp.max(largest[:, head_rows(h)], axis=1, keepdims=True) for h in range(2)]
        for h, queries, cols in segments(q_ref.shape[0], size):
            mine = turned_q[head_rows(h), queries]
            ques[:, cols] = beside(mine, h)
            sharp = mine.astype(F32)
            reach = jnp.sum(sharp * sharp, axis=0, keepdims=True)
            bound[:, cols] = jnp.sqrt(reach * tops[h] * 1.03) * factor

    cols = pl.ds(pl.multiple_of(pos * width, width), width)

    def weigh(peak):
        for start in range(0, width, across):
            own = slice(start, start + across)
            query = ques[:, pl.ds(pl.multiple_of(pos * width + start, across), across)]
            for at in range(0, kv, chunk):
                rows = slice(at, at + chunk)
                scores = jnp.dot(keys[rows, :], query, preferred_element_type=F32)
                p_ref[0, rows, own] = jnp.exp2(scores * factor - peak[:, own]).astype(BF16)
        total = jnp.dot(vals[...], p_ref[0], preferred_element_type=F32)
        sums = total[PAIR : PAIR + 1, :]
        sum_ref[0] = sums
        for h in range(2):
            own = slice(h * size, (h + 1) * size)
            turned[head_rows(h), :] = total[head_rows(h), own] / sums[:, own]
        return jnp.min(sums)

    def exact_peak():
        query = ques[:, cols]

        def largest(at, peak):
            rows = pl.ds(pl.multiple_of(at * chunk, chunk), chunk)
            scores = jnp.dot(keys[rows, :], query, preferred_element_type=F32)
            live = live_rows((chunk, width), 0, at * chunk, info[0], info[1], span)
            return jnp.maximum(peak, jnp.max(jnp.where(live, scores, -1e30), axis=0, keepdims=True))

        return lax.fori_loop(0, kv // chunk, largest, jnp.full((1, width), -1e30, F32)) * factor

    lowest = weigh(bound[:, cols])

    @pl.when(jnp.logical_not(lowest > 2.0**-70))
    def again():
        weigh(exact_peak())

    out_ref[...] = turned[...].T.astype(BF16)


def attend(info, sources, span, first, count, before):
    (queries, q_at), (keys, k_at), (values, v_at) = sources
    rows, kv = queries.shape[0], keys.shape[0]
    size = chunk_of(rows)
    pairs = HEADS // 2
    before = before or ()
    return pl.pallas_call(
        functools.partial(
            attend_kernel,
            chunk=min(256, kv),
            across=min(256, 2 * size),
            span=span,
            extra=len(before),
        ),
        out_shape=(
            jax.ShapeDtypeStruct((rows, HEADS * HDIM), BF16),
            jax.ShapeDtypeStruct((pairs, kv, 2 * rows), BF16),
            jax.ShapeDtypeStruct((pairs, 1, 2 * rows), F32),
        ),
        grid_spec=pltpu.PrefetchScalarGridSpec(
            num_scalar_prefetch=1,
            grid=(count, rows // size),
            in_specs=[
                pl.BlockSpec((rows, PAIR), lambda j, c, s: (0, q_at(first + j))),
                pl.BlockSpec((kv, PAIR), lambda j, c, s: (0, k_at(first + j))),
                pl.BlockSpec((kv, PAIR), lambda j, c, s: (0, v_at(first + j))),
            ]
            + any_specs(before),
            out_specs=(
                pl.BlockSpec((size, PAIR), lambda j, c, s: (c, first + j)),
                pl.BlockSpec((1, kv, 2 * size), lambda j, c, s: (first + j, 0, c)),
                pl.BlockSpec((1, 1, 2 * size), lambda j, c, s: (first + j, 0, c)),
            ),
            scratch_shapes=[
                pltpu.VMEM((kv, PAIR), BF16),
                pltpu.VMEM((PAIR + 16, kv), BF16),
                pltpu.VMEM((PAIR, 2 * rows), BF16),
                pltpu.VMEM((1, 2 * rows), F32),
                pltpu.VMEM((PAIR, size), F32),
            ],
        ),
        input_output_aliases={4 + t: t for t in range(len(before))},
        compiler_params=pltpu.CompilerParams(vmem_limit_bytes=60 * 2**20),
        name="attend",
    )(info, queries, keys, values, *before)


def attend_back_kernel(
    info,
    units,
    q_ref,
    k_ref,
    v_ref,
    g_ref,
    ctx_ref,
    sum_ref,
    p_ref,
    *rest,
    chunk,
    size,
    span,
    more,
    extra,
):
    before, rest = (rest[:3], rest[3:]) if more else (None, rest)
    rest = rest[extra:]
    gq_ref, gk_ref, gv_ref, keys, grads, grads_up, ques_up, delta, low, total, key_sum, value_sum = rest
    step = pl.program_id(1)
    kv, rows = k_ref.shape[0], q_ref.shape[0]
    block, part = p_ref.shape[1:]
    scale = HDIM**-0.5

    @pl.when(step == 0)
    def prepare():
        live = live_rows((kv, PAIR), 0, 0, info[0], info[1], span)
        keys[...] = jnp.where(live, k_ref[...], jnp.zeros((), BF16)).T
        turned = g_ref[...].T.astype(F32)
        dots = turned * ctx_ref[...].T.astype(F32)
        for h, queries, cols in segments(rows, size):
            inverse = 1.0 / sum_ref[0, :, cols]
            own = head_rows(h)
            delta[:, cols] = jnp.sum(dots[own, queries], axis=0, keepdims=True) * inverse
            shared = beside((turned[own, queries] * inverse).astype(BF16), h)
            grads[:, cols] = shared
            grads_up[cols, :] = shared.T
            lane = lax.broadcasted_iota(jnp.int32, (queries.stop - queries.start, PAIR), 1)
            ques_up[cols, :] = jnp.where(lane // HDIM == h, q_ref[queries, :], jnp.zeros((), BF16))
        for held in (total, key_sum, value_sum):
            held[...] = jnp.zeros_like(held)

    here = pl.ds(pl.multiple_of(units[0, step] * block, block), block)
    there = pl.multiple_of(units[1, step] * part, part)
    cols = pl.ds(there, part)
    values = v_ref[here, :]
    for start in range(0, part, chunk):
        own = slice(start, start + chunk)
        from_all = pl.ds(there + start, chunk)
        change = jnp.dot(values, grads[:, from_all], preferred_element_type=F32)
        low[:, own] = (p_ref[0, :, own].astype(F32) * (change - delta[:, from_all])).astype(BF16)
    value_sum[here, :] += jnp.dot(p_ref[0], grads_up[cols, :], preferred_element_type=F32)
    key_sum[here, :] += jnp.dot(low[...], ques_up[cols, :], preferred_element_type=F32)
    total[:, cols] += jnp.dot(keys[:, here], low[...], preferred_element_type=F32)

    @pl.when(step == pl.num_programs(1) - 1)
    def finish():
        live = live_rows((kv, PAIR), 0, 0, info[0], info[1], span)
        zero = jnp.zeros((), F32)
        found = [jnp.where(live, key_sum[...] * scale, zero), jnp.where(live, value_sum[...], zero)]
        for t, (ref, value) in enumerate(zip((gk_ref, gv_ref), found)):
            if more:
                value += before[t + 1][...].astype(F32)
            ref[...] = value.astype(BF16)
        parts = [[], []]
        for h, queries, cols in segments(rows, size):
            parts[h].append(total[head_rows(h), cols])
        value = (jnp.concatenate([jnp.concatenate(p, 1) for p in parts], 0) * scale).T
        if more:
            value += before[0][...].astype(F32)
        gq_ref[...] = value.astype(BF16)


def attend_back(info, sources, grad, context, sums, probs, span, units, before, events=()):
    (queries, q_at), (keys, k_at), (values, v_at) = sources
    rows, kv = queries.shape[0], keys.shape[0]
    pairs = HEADS // 2
    wide = HEADS * HDIM
    more = before is not None
    block, part, size = min(1024, kv), rows, chunk_of(rows)
    cut = 2 if more else 1
    rows, kv = rows // cut, kv // cut
    out_rows = [rows, kv, kv]
    units = jnp.array(list(zip(*units)), jnp.int32)
    col = lambda height, at=lambda j: j: pl.BlockSpec(
        (height, PAIR), lambda j, c, s, u: (0, at(j))
    )
    return pl.pallas_call(
        functools.partial(
            attend_back_kernel,
            chunk=min(512, part),
            size=size,
            span=span,
            more=more,
            extra=len(events),
        ),
        out_shape=tuple(jax.ShapeDtypeStruct((height, wide), BF16) for height in out_rows),
        grid_spec=pltpu.PrefetchScalarGridSpec(
            num_scalar_prefetch=2,
            grid=(pairs, units.shape[1]),
            in_specs=[
                col(rows, q_at),
                col(kv, k_at),
                col(kv, v_at),
                col(rows),
                col(rows),
                pl.BlockSpec((1, 1, 2 * rows), lambda j, c, s, u: (j, 0, 0)),
                pl.BlockSpec((1, block, part), lambda j, c, s, u: (j, u[0, c], u[1, c])),
            ]
            + ([col(height) for height in out_rows] if more else [])
            + any_specs(events),
            out_specs=tuple(col(height) for height in out_rows),
            scratch_shapes=[
                pltpu.VMEM((PAIR, kv), BF16),
                pltpu.VMEM((PAIR, 2 * rows), BF16),
                pltpu.VMEM((2 * rows, PAIR), BF16),
                pltpu.VMEM((2 * rows, PAIR), BF16),
                pltpu.VMEM((1, 2 * rows), F32),
                pltpu.VMEM((block, part), BF16),
                pltpu.VMEM((PAIR, 2 * rows), F32),
                pltpu.VMEM((kv, PAIR), F32),
                pltpu.VMEM((kv, PAIR), F32),
            ],
        ),
        compiler_params=pltpu.CompilerParams(vmem_limit_bytes=60 * 2**20),
        name="attend_back_last" if more else "attend_back",
    )(info, units, queries, keys, values, grad, context, sums, probs, *(before or ()), *events)


def rows_of(kept_ref, other_ref, step, split):
    return jnp.where(step < split, kept_ref[0], other_ref[...])


def project(rows, weight):
    return jnp.dot(rows, weight, preferred_element_type=F32)


def project_back(grads, weight):
    return lax.dot_general(grads, weight, (((1,), (1,)), ((), ())), preferred_element_type=F32)


def weight_grad(rows, grads):
    return lax.dot_general(rows, grads, (((0,), (0,)), ((), ())), preferred_element_type=F32)


def run_all(copies):
    for copy in copies:
        copy.start()
    return copies


def wait_all(copies):
    for copy in copies:
        copy.wait()


class Pieces:
    def __init__(self, shape, mesh_shape, bundles, turned=()):
        self.turned = turned
        self.r, self.c = shape
        self.m, self.n = mesh_shape
        self.bundles = bundles
        self.slots = self.m * self.n

    def place(self, masks, slot, info):
        if masks is None:
            return slot // self.n, lax.rem(slot, self.n)
        return info[5] ^ (masks[slot] // self.n), masks[slot] % self.n

    def copies(self, refs, mats, sems, info, out):
        found = [[] for _ in mats]
        r, c = self.r, self.c
        count = 0
        for (masks, members), ref in zip(self.bundles, refs):
            for slot in range(self.slots if masks is None else len(masks)):
                j, i = self.place(masks, slot, info)
                at = 0
                for t in members:
                    mat = mats[t]
                    tall = mat.shape[0] // (self.m * r)
                    wide = max(mat.shape[1] // (self.n * c), 1)
                    for w in range(wide):
                        if isinstance(ref, (tuple, list)):
                            each = self.slots // len(ref)
                            block = ref[slot // each].at[slot % each, pl.ds(at, tall * r), :]
                        else:
                            block = ref.at[slot, pl.ds(at, tall * r), :]
                        row = j ^ (info[6] * (self.m // 2)) if t in self.turned else j
                        down = pl.multiple_of(row * (tall * r), tall * r)
                        side = (i * wide + w) * c if mat.shape[1] > c else 0
                        place = mat.at[pl.ds(down, tall * r), pl.ds(side, c)]
                        at += tall * r
                        pair = (place, block) if out else (block, place)
                        found[t].append(pltpu.make_async_copy(*pair, sems.at[count]))
                        count += 1
        return found

    def count(self):
        return 9 * self.slots


def any_specs(arrays):
    return [pl.BlockSpec(memory_space=pl.ANY)] * len(arrays)


def queries_kernel(info, kept_ref, other_ref, bias_ref, *rest, split, grid_of, extra):
    count = len(grid_of.bundles)
    packed, (out_ref, mat_q, mat_k, mat_v, sems) = rest[:count], rest[count + extra :]
    step = pl.program_id(0)
    mats = [mat_q, mat_k, mat_v]

    @pl.when(step == 0)
    def load():
        loads = grid_of.copies(packed, mats, sems, info, False)
        for group in loads:
            run_all(group)
        for group in loads:
            wait_all(group)

    rows = rows_of(kept_ref, other_ref, step, split)
    width = mat_q.shape[1]
    for t, mat in enumerate(mats):
        cols = slice(t * width, (t + 1) * width)
        out_ref[:, cols] = (project(rows, mat[...]) + bias_ref[:, cols]).astype(BF16)


def split_specs(kept_at, tile, split, width):
    return [
        pl.BlockSpec((1, tile, width), lambda i, s: (s[kept_at], jnp.minimum(i, split - 1), 0)),
        pl.BlockSpec((tile, width), lambda i, s: (jnp.maximum(i - split, 0), 0)),
    ]


def whole_spec(shape):
    return pl.BlockSpec(shape, lambda i, s: (0,) * len(shape))


def queries_keys_values(info, kept, other, packed, grid_of, bias, group, before):
    block_len, width = other.shape
    tile = min(512, block_len)
    split = block_len // tile
    wide = bias.shape[1]
    before = before or ()
    mat = jax.ShapeDtypeStruct((width, width), BF16)
    inputs = [kept, other, bias, *packed]
    return pl.pallas_call(
        functools.partial(queries_kernel, split=split, grid_of=grid_of, extra=len(before)),
        out_shape=(jax.ShapeDtypeStruct((2 * block_len, 3 * width), BF16), mat, mat, mat),
        grid_spec=pltpu.PrefetchScalarGridSpec(
            num_scalar_prefetch=1,
            grid=(2 * split,),
            in_specs=split_specs(2, tile, split, width)
            + [whole_spec(bias.shape)]
            + any_specs(packed)
            + any_specs(before),
            out_specs=(pl.BlockSpec((tile, wide), lambda i, s: (i, group)),)
            + (pl.BlockSpec((width, wide // 3), lambda i, s: (0, group)),) * 3,
            scratch_shapes=[pltpu.SemaphoreType.DMA((grid_of.count(),))],
        ),
        input_output_aliases={1 + len(inputs) + t: t for t in range(len(before))},
        compiler_params=pltpu.CompilerParams(vmem_limit_bytes=60 * 2**20),
        name="queries",
    )(info, *inputs, *before)


def normal(values):
    middle = jnp.mean(values, axis=-1, keepdims=True)
    centered = values - middle
    spread = jnp.mean(centered * centered, axis=-1, keepdims=True)
    inverse = lax.rsqrt(spread + 1e-12)
    return centered * inverse, inverse


def normal_back(grad, unit, inverse, gain):
    scaled = grad * gain
    mean = jnp.mean(scaled, axis=-1, keepdims=True)
    along = jnp.mean(scaled * unit, axis=-1, keepdims=True)
    return (scaled - mean - unit * along) * inverse


def gelu_pair(u):
    phi = 0.5 + 0.5 * lax.erf(0.7071067811865476 * u)
    bell = jnp.exp2((-0.5 * LOG2E) * (u * u))
    return u * phi, phi + (0.3989422804014327 * u) * bell


def add_rows(total, at, values):
    total[at : at + 1, 0 : values.shape[1]] += jnp.sum(values, axis=0, keepdims=True)


def middle_kernel(
    info,
    hid_kept,
    hid_other,
    cot_kept,
    cot_other,
    ctx_ref,
    cls_ref,
    vec_ref,
    inner_bias,
    packed,
    layer_kept,
    layer_other,
    top_ref,
    grad_ctx_ref,
    resid_ref,
    sums_ref,
    mat_out,
    mat_inner,
    mat_outer,
    acc_out,
    acc_inner,
    acc_outer,
    totals,
    active,
    slope,
    low,
    vec_low,
    sems,
    vec_sems,
    *,
    split,
    grid_of,
    chunk,
):
    step = pl.program_id(0)
    last = pl.num_programs(0) - 1
    mats = [mat_out, mat_inner, mat_outer]
    tile, width = ctx_ref.shape
    ff = mat_inner.shape[1]
    loads = grid_of.copies([packed], mats, sems, info, False)

    @pl.when(step == 0)
    def start():
        for group in loads:
            run_all(group)
        for acc in (acc_out, acc_inner, acc_outer, totals):
            acc[...] = jnp.zeros_like(acc)
        wait_all(loads[0])

    bias_out, gain_one, shift_one, bias_outer, gain_two, shift_two = [
        vec_ref[t : t + 1, :] for t in range(6)
    ]
    hidden = rows_of(hid_kept, hid_other, step, split).astype(F32)
    context = ctx_ref[...]
    unit_one, inverse_one = normal(hidden + project(context, mat_out[...]) + bias_out)
    normed = unit_one * gain_one + shift_one
    normed_low = normed.astype(BF16)

    @pl.when(step == 0)
    def more():
        wait_all(loads[1])
        wait_all(loads[2])

    for at in range(0, ff, chunk):
        cols = slice(at, at + chunk)
        inner = project(normed_low, mat_inner[:, cols]) + inner_bias[:, cols]
        value, change = gelu_pair(inner)
        active[:, cols] = value.astype(BF16)
        slope[:, cols] = change.astype(BF16)
    unit_two, inverse_two = normal(normed + project(active[...], mat_outer[...]) + bias_outer)
    layer = (unit_two * gain_two + shift_two).astype(BF16)

    @pl.when(step < split)
    def kept():
        layer_kept[0] = layer

    @pl.when(step >= split)
    def other():
        layer_other[...] = layer

    @pl.when(step * tile == info[1])
    def top():
        top_ref[...] = layer[0:16, :]


    row = step * tile + lax.broadcasted_iota(jnp.int32, (tile, width), 0)
    grad_result = rows_of(cot_kept, cot_other, step, split).astype(F32)
    grad_result += jnp.where(row == info[4], cls_ref[...], 0.0)
    add_rows(totals, 4, grad_result * unit_two)
    add_rows(totals, 5, grad_result)
    grad_resid_two = normal_back(grad_result, unit_two, inverse_two, gain_two)
    grad_outer = grad_resid_two.astype(BF16)
    add_rows(totals, 3, grad_outer.astype(F32))
    for at in range(0, ff, chunk):
        cols = slice(at, at + chunk)
        grad_inner = project_back(grad_outer, mat_outer[cols, :]) * slope[:, cols].astype(F32)
        low[:, cols] = grad_inner.astype(BF16)
        totals[8:9, cols] += jnp.sum(grad_inner, axis=0, keepdims=True)
        acc_outer[cols, :] += weight_grad(active[:, cols], grad_outer)
    grad_normed = grad_resid_two + project_back(low[...], mat_inner[...])
    for at in range(0, ff, chunk):
        cols = slice(at, at + chunk)
        acc_inner[:, cols] += weight_grad(normed_low, low[:, cols])
    add_rows(totals, 1, grad_normed * unit_one)
    add_rows(totals, 2, grad_normed)
    grad_resid_one = normal_back(grad_normed, unit_one, inverse_one, gain_one)
    resid_ref[...] = grad_resid_one
    grad_attn = grad_resid_one.astype(BF16)
    add_rows(totals, 0, grad_attn.astype(F32))
    acc_out[...] += weight_grad(context, grad_attn)
    grad_ctx_ref[...] = project_back(grad_attn, mat_out[...]).astype(BF16)

    @pl.when(step == last)
    def finish():
        r, c, m, n = grid_of.r, grid_of.c, grid_of.m, grid_of.n
        stores = grid_of.copies([sums_ref], mats, sems, info, True)
        for mat, acc, group in zip(mats, (acc_out, acc_inner, acc_outer), stores):
            mat[...] = acc[...].astype(BF16)
            run_all(group)
        vec_low[...] = jnp.zeros_like(vec_low)
        for i in range(n):
            for t in range(6):
                vec_low[i, t : t + 1, :] = totals[t : t + 1, i * c : (i + 1) * c]
            wide = ff // (n * c)
            for t in range(wide):
                at = (i * wide + t) * c
                vec_low[i, 6 + t : 7 + t, :] = totals[8:9, at : at + c]
        tails = []
        vec_bits = vec_low[...].astype(BF16)
        for i in range(n):
            active[16 * i : 16 * i + 16, 0:c] = vec_bits[i]
        for j in range(m):
            for i in range(n):
                tails.append(
                    pltpu.make_async_copy(
                        active.at[pl.ds(16 * i, 16), pl.ds(0, c)],
                        sums_ref.at[j * n + i, pl.ds(9 * r, 16), :],
                        vec_sems.at[j * n + i],
                    )
                )
        run_all(tails)
        for group in stores:
            wait_all(group)
        wait_all(tails)


def kept_spec(tile, split, width):
    return pl.BlockSpec((1, tile, width), lambda i, s: (s[2], jnp.minimum(i, split - 1), 0))


def other_spec(tile, split, width):
    return pl.BlockSpec((tile, width), lambda i, s: (jnp.maximum(i - split, 0), 0))


def middle(info, hidden, cots, context, cls_row, weights, vectors, inner_bias):
    block_len, width = hidden[1].shape
    grid_of = weights.grid_of
    ff = inner_bias.shape[1]
    tile = min(256, block_len)
    split = block_len // tile
    row_spec = pl.BlockSpec((tile, width), lambda i, s: (i, 0))
    return pl.pallas_call(
        functools.partial(middle_kernel, split=split, grid_of=grid_of, chunk=768),
        out_shape=(
            jax.ShapeDtypeStruct(hidden[0].shape, BF16),
            jax.ShapeDtypeStruct((block_len, width), BF16),
            jax.ShapeDtypeStruct((16, width), BF16),
            jax.ShapeDtypeStruct((2 * block_len, width), BF16),
            jax.ShapeDtypeStruct((2 * block_len, width), F32),
            jax.ShapeDtypeStruct((grid_of.slots, 9 * grid_of.r + 16, grid_of.c), BF16),
        ),
        grid_spec=pltpu.PrefetchScalarGridSpec(
            num_scalar_prefetch=1,
            grid=(2 * split,),
            in_specs=split_specs(2, tile, split, width)
            + split_specs(2, tile, split, width)
            + [
                row_spec,
                whole_spec(cls_row.shape),
                whole_spec(vectors.shape),
                whole_spec(inner_bias.shape),
                pl.BlockSpec(memory_space=pl.ANY),
            ],
            out_specs=(
                kept_spec(tile, split, width),
                other_spec(tile, split, width),
                whole_spec((16, width)),
                row_spec,
                row_spec,
                pl.BlockSpec(memory_space=pl.ANY),
            ),
            scratch_shapes=[
                pltpu.VMEM((width, width), BF16),
                pltpu.VMEM((width, ff), BF16),
                pltpu.VMEM((ff, width), BF16),
                pltpu.VMEM((width, width), F32),
                pltpu.VMEM((width, ff), F32),
                pltpu.VMEM((ff, width), F32),
                pltpu.VMEM((16, ff), F32),
                pltpu.VMEM((tile, ff), BF16),
                pltpu.VMEM((tile, ff), BF16),
                pltpu.VMEM((tile, ff), BF16),
                pltpu.VMEM((grid_of.n, 16, grid_of.c), F32),
                pltpu.SemaphoreType.DMA((grid_of.count(),)),
                pltpu.SemaphoreType.DMA((grid_of.slots,)),
            ],
        ),
        compiler_params=pltpu.CompilerParams(vmem_limit_bytes=60 * 2**20),
        name="middle",
    )(info, *hidden, *cots, context, cls_row, vectors, inner_bias, *weights.packed)


def input_grad_kernel(info, gq_ref, gk_ref, gv_ref, resid_ref, mat_q, mat_k, mat_v, *rest, kept):
    grad_ref = rest[-1]
    total = resid_ref[...]
    for ref, mat in zip((gq_ref, gk_ref, gv_ref), (mat_q, mat_k, mat_v)):
        total += project_back(ref[...], mat[...])
    if kept:
        grad_ref[0] = total.astype(grad_ref.dtype)
    else:
        grad_ref[...] = total.astype(grad_ref.dtype)


def input_grad(info, grads, resid, mats, out_shape, dtype, kept, events=()):
    rows, width = resid.shape
    block_len = rows // 2
    tile = min(512, block_len)
    split = block_len // tile
    off = 0 if kept else split
    spec = pl.BlockSpec((tile, width), lambda i, s: (i + off, 0))
    place = kept_spec(tile, split, width) if kept else other_spec(tile, 0, width)
    return pl.pallas_call(
        functools.partial(input_grad_kernel, kept=kept),
        out_shape=jax.ShapeDtypeStruct(out_shape, dtype),
        grid_spec=pltpu.PrefetchScalarGridSpec(
            num_scalar_prefetch=1,
            grid=(split,),
            in_specs=[spec] * 4 + [whole_spec(mat.shape) for mat in mats] + any_specs(events),
            out_specs=place,
        ),
        compiler_params=pltpu.CompilerParams(vmem_limit_bytes=60 * 2**20),
        name="input_grad_kept" if kept else "input_grad_other",
    )(info, *grads, resid, *mats, *events)


def head_grads_kernel(info, hid_kept, hid_other, *rest, split, grid_of, outs, extra):
    kept, other, rest = rest[:3], rest[3:6], rest[6 + extra :]
    sums, (acc, mat_q, mat_k, mat_v, totals, vec_low, sems, vec_sems) = rest[:outs], rest[outs:]
    mats = [mat_q, mat_k, mat_v]
    step = pl.program_id(0)

    @pl.when(step == 0)
    def clear():
        acc[...] = jnp.zeros_like(acc)
        totals[...] = jnp.zeros_like(totals)

    rows = rows_of(hid_kept, hid_other, step, split)
    grads = [jnp.where(step < split, a[...], b[...]) for a, b in zip(kept, other)]
    for t, grad in enumerate(grads):
        acc[t] += weight_grad(rows, grad)
    add_rows(totals, 0, grads[0].astype(F32))
    add_rows(totals, 1, grads[2].astype(F32))

    @pl.when(step == pl.num_programs(0) - 1)
    def finish():
        r, c, n = grid_of.r, grid_of.c, grid_of.n
        ((masks, _),) = grid_of.bundles
        stores = grid_of.copies([list(sums)], mats, sems, info, True)
        for t, mat in enumerate(mats):
            mat[...] = acc[t].astype(BF16)
            run_all(stores[t])
        for i in range(n):
            part = jnp.concatenate([totals[0:2, i * c : (i + 1) * c], jnp.zeros((14, c), F32)], 0)
            vec_low[i] = part.astype(BF16)
        tails = []
        each = grid_of.slots // outs
        for slot in range(grid_of.slots):
            j, i = grid_of.place(masks, slot, info)
            place = sums[slot // each].at[slot % each, pl.ds(3 * r, 16), :]
            tails.append(pltpu.make_async_copy(vec_low.at[i], place, vec_sems.at[slot]))
        run_all(tails)
        for group in stores:
            wait_all(group)
        wait_all(tails)


def head_grads(info, hidden, kept, other, grid_of, outs, events=()):
    block_len, width = hidden[1].shape
    tile = min(512, block_len)
    split = block_len // tile
    last = other[0].shape[0] // tile - split
    kept_rows = pl.BlockSpec((tile, width), lambda i, s: (jnp.minimum(i, split - 1), 0))
    other_rows = pl.BlockSpec((tile, width), lambda i, s: (jnp.maximum(i, split), 0))
    block = (grid_of.slots // outs, 3 * grid_of.r + 16, grid_of.c)
    return pl.pallas_call(
        functools.partial(
            head_grads_kernel, split=split, grid_of=grid_of, outs=outs, extra=len(events)
        ),
        out_shape=(jax.ShapeDtypeStruct(block, BF16),) * outs,
        grid_spec=pltpu.PrefetchScalarGridSpec(
            num_scalar_prefetch=1,
            grid=(2 * split,),
            in_specs=split_specs(2, tile, split, width) + [kept_rows] * 3 + [other_rows] * 3 + any_specs(events),
            out_specs=(pl.BlockSpec(memory_space=pl.ANY),) * outs,
            scratch_shapes=[pltpu.VMEM((3, width, width), F32)]
            + [pltpu.VMEM((width, width), BF16)] * 3
            + [
                pltpu.VMEM((8, width), F32),
                pltpu.VMEM((grid_of.n, 16, grid_of.c), BF16),
                pltpu.SemaphoreType.DMA((grid_of.count(),)),
                pltpu.SemaphoreType.DMA((grid_of.slots,)),
            ],
        ),
        compiler_params=pltpu.CompilerParams(vmem_limit_bytes=60 * 2**20),
        name="head_grads",
    )(info, *hidden, *kept, *other, *events)


def pick_kernel(info, pair_ref, *rest):
    rest[-1][...] = pair_ref[0]


def pick_other(info, pair, events):
    _, block_len, width = pair.shape
    tile = min(256, block_len)
    return pl.pallas_call(
        pick_kernel,
        out_shape=jax.ShapeDtypeStruct((block_len, width), pair.dtype),
        grid_spec=pltpu.PrefetchScalarGridSpec(
            num_scalar_prefetch=1,
            grid=(block_len // tile,),
            in_specs=[pl.BlockSpec((1, tile, width), lambda i, s: (1 - s[2], i, 0))]
            + any_specs(events),
            out_specs=pl.BlockSpec((tile, width), lambda i, s: (i, 0)),
        ),
        compiler_params=pltpu.CompilerParams(vmem_limit_bytes=60 * 2**20),
        name="pick_other",
    )(info, pair, *events)


def pack_kernel(*refs, count):
    out = refs[-1]
    c = out.shape[1]
    at = 0
    for ref in refs[:count]:
        rows, cols = ref.shape
        for start in range(0, cols, c):
            out[at : at + rows, :] = ref[:, start : start + c]
            at += rows


def pack_after(shards, events):
    c = min(s.shape[1] for s in shards)
    rows = sum(s.size for s in shards) // c
    return pl.pallas_call(
        functools.partial(pack_kernel, count=len(shards)),
        out_shape=jax.ShapeDtypeStruct((rows, c), BF16),
        in_specs=[pl.BlockSpec(memory_space=pltpu.VMEM)] * len(shards) + any_specs(events),
        compiler_params=pltpu.CompilerParams(vmem_limit_bytes=60 * 2**20),
        name="pack",
    )(*shards, *events)


def add_kernel(*refs, count, extra):
    parts, outs = refs[:count], refs[count + extra :]
    each = outs[0].shape[0]
    for k, out in enumerate(outs):
        here = slice(k * each, (k + 1) * each)
        out[...] = sum(part[here].astype(F32) for part in parts).astype(BF16)


def add_blocks(parts, groups, events):
    shape = (parts[0].shape[0] // groups,) + parts[0].shape[1:]
    return pl.pallas_call(
        functools.partial(add_kernel, count=len(parts), extra=len(events)),
        out_shape=(jax.ShapeDtypeStruct(shape, BF16),) * groups,
        in_specs=[pl.BlockSpec(memory_space=pltpu.VMEM)] * len(parts) + any_specs(events),
        compiler_params=pltpu.CompilerParams(vmem_limit_bytes=60 * 2**20),
        name="add_blocks",
    )(*parts, *events)


def place_kernel(info, base_ref, other_ref, out_ref):
    out_ref[0] = other_ref[...].astype(out_ref.dtype)


def place_other(info, base, other):
    block_len, width = other.shape
    tile = min(512, block_len)
    return pl.pallas_call(
        place_kernel,
        out_shape=jax.ShapeDtypeStruct(base.shape, base.dtype),
        grid_spec=pltpu.PrefetchScalarGridSpec(
            num_scalar_prefetch=1,
            grid=(block_len // tile,),
            in_specs=[
                pl.BlockSpec(memory_space=pl.ANY),
                pl.BlockSpec((tile, width), lambda i, s: (i, 0)),
            ],
            out_specs=pl.BlockSpec((1, tile, width), lambda i, s: (1 - s[2], i, 0)),
        ),
        input_output_aliases={1: 0},
        compiler_params=pltpu.CompilerParams(vmem_limit_bytes=60 * 2**20),
        name="place_other",
    )(info, base, other)


def swap(block, axis, route):
    if all(a == b for a, b in route):
        return block
    return lax.ppermute(block, axis, route)


class Regroup:
    def __init__(self):
        self.n = lax.axis_size("blk")
        self.me = lax.axis_index("blk")
        self.per = self.n // 2
        self.passage = self.me // self.per
        self.part = lax.rem(self.me, 2)
        self.first = [(i, (i % 2) * self.per + i // 2) for i in range(self.n)]
        self.second = [(i, (1 - i % 2) * self.per + i // 2) for i in range(self.n)]
        self.stays = all(a == b for a, b in self.first)

    def pick(self, info, pair, events=()):
        if self.stays and events:
            return pick_other(info, pair, events)
        return lax.dynamic_index_in_dim(pair, 1 - self.part, 0, keepdims=False)

    def gather(self, pair, picked):
        other = swap(picked, "blk", self.second)
        if self.stays:
            return (pair, other)
        kept = lax.dynamic_index_in_dim(pair, self.part, 0, keepdims=True)
        return (swap(kept, "blk", self.first), other)

    def kept_index(self):
        return self.part if self.stays else jnp.zeros_like(self.part)

    def all_blocks(self, block):
        if self.n != 2:
            return lax.all_gather(block, "blk", axis=0)
        other = lax.ppermute(block, "blk", [(0, 1), (1, 0)])
        return jnp.where(self.me == 0, jnp.stack([block, other]), jnp.stack([other, block]))

    def send_back(self, other):
        return swap(other, "blk", [(b, a) for a, b in self.second])

    def join(self, info, kept, other):
        if self.stays:
            return place_other(info, kept, other)
        kept = swap(kept[0], "blk", [(b, a) for a, b in self.first])
        other = other.astype(kept.dtype)
        return jnp.where(self.part == 0, jnp.stack([kept, other]), jnp.stack([other, kept]))


def pack(shards):
    c = min(s.shape[1] for s in shards)
    return jnp.concatenate(
        [s[:, at : at + c] for s in shards for at in range(0, s.shape[1], c)], axis=0
    )


def unpack(block, shapes):
    c = block.shape[-1]
    found, at = [], 0
    for rows, cols in shapes:
        parts = []
        for _ in range(cols // c):
            parts.append(block[..., at : at + rows, :])
            at += rows
        found.append(jnp.concatenate(parts, axis=-1) if len(parts) > 1 else parts[0])
    return found


def exchanged(block, mask):
    both = ("batch", "blk")
    places = range(lax.axis_size("batch") * lax.axis_size("blk"))
    return lax.ppermute(block, both, [(i, i ^ mask) for i in places])


def xor_gather(block, stages):
    found, masks = block[None], [0]
    for stage in stages:
        parts = [found] + [exchanged(found, mask) for mask in stage]
        masks = masks + [held ^ mask for mask in stage for held in masks]
        found = jnp.concatenate(parts, 0)
    return found, masks


def xor_masks(stages):
    masks = [0]
    for stage in stages:
        masks = [held ^ mask for held in masks for mask in [0] + stage]
    return masks


def xor_sum(groups, stages, meanwhile):
    for at, stage in enumerate(stages):
        parts = [groups[0]] + [exchanged(g, mask) for mask, g in zip(stage, groups[1:])]
        if at == len(stages) - 1:
            return [part[0] for part in parts]
        events = meanwhile if at == len(stages) - 2 else ()
        groups = add_blocks(parts, len(stages[at + 1]) + 1, events)


class Weights:
    def __init__(self, shards, by_pairs, events=()):
        self.shapes = [s.shape for s in shards]
        self.m, self.n = lax.axis_size("batch"), lax.axis_size("blk")
        m, n = self.m, self.n
        r, c = min(s[0] for s in self.shapes), min(s[1] for s in self.shapes)
        self.fits = r % 16 == 0 and c % 128 == 0
        powers = m & (m - 1) == 0 and n == 2 and m >= 8
        self.by_pairs = by_pairs and self.fits and powers
        self.local = powers and self.fits
        every = list(range(len(shards)))
        if self.by_pairs:
            y, core, x = list(range(1, n)), [n], [2 * n]
            z = list(range(4 * n, m * n, 4 * n))
            own = pack_after(shards, ())
            found, masks = xor_gather(own, [z, x])
            self.packed, self.grids = [], []
            for far in (0, 1):
                if far:
                    found = exchanged(found, y[0])
                    masks = [mask ^ y[0] for mask in masks]
                self.packed.append([found, exchanged(found, core[0])])
                bundles = [(masks, every), ([mask ^ core[0] for mask in masks], every)]
                self.grids.append(Pieces((r, c), (m, n), bundles))
            self.stages = [core, [a ^ b for a in [0] + x for b in [0] + y][1:], z]
            self.sums_of = Pieces((r, c), (m, n), [(xor_masks(self.stages), every)])
            return
        packed = pack_after(shards, events) if self.fits else pack(shards)
        packed = lax.all_gather(packed, ("batch", "blk"), axis=0)
        if self.fits:
            turned = (0,) if self.local else ()
            self.grid_of = Pieces((r, c), (m, n), [(None, every)], turned)
            self.packed = [packed]
        else:
            self.grid_of = Pieces((r * m, c * n), (1, 1), [(None, every)])
            whole = []
            for part in unpack(packed, self.shapes):
                rows, cols = part.shape[1:]
                part = part.reshape(m, n, rows, cols).transpose(0, 2, 1, 3)
                whole.append(part.reshape(m * rows, n * cols))
            self.packed = [pack(whole)[None]]
        self.sums_of = self.grid_of

    def scatter(self, sums, meanwhile=()):
        extra = 16
        if self.by_pairs:
            return finish_sums(xor_sum(sums, self.stages, meanwhile), self.shapes)
        (sums,) = sums
        if not self.fits:
            rows = sums.shape[1] - extra
            wide = [(a * self.m, b * self.n) for a, b in self.shapes]
            parts = []
            for part in unpack(sums[0, :rows], wide):
                a, b = part.shape[0] // self.m, part.shape[1] // self.n
                part = part.reshape(self.m, a, self.n, b).transpose(0, 2, 1, 3)
                parts.append(part.reshape(self.m * self.n, a, b))
            c = min(s[1] for s in self.shapes)
            blocks = jnp.stack([pack([p[d] for p in parts]) for d in range(self.m * self.n)])
            vecs = sums[0, rows:].reshape(extra, self.n, c).transpose(1, 0, 2)
            vecs = jnp.broadcast_to(vecs[None], (self.m, self.n, extra, c))
            sums = jnp.concatenate([blocks, vecs.reshape(self.m * self.n, extra, c)], axis=1)
        height, c = sums.shape[1:]
        own = lax.psum_scatter(
            sums.reshape(-1, c), ("batch", "blk"), scatter_dimension=0, tiled=True
        )
        return finish_sums([own], self.shapes)


def finish_kernel(*refs, count):
    parts, outs = refs[:count], refs[count:]
    at = 0
    for out in outs:
        rows, cols = out.shape
        c = parts[0].shape[1]
        for start in range(0, cols, c):
            here = slice(at, at + rows)
            out[:, start : start + c] = sum(part[here, :].astype(F32) for part in parts)
            at += rows


def finish_sums(parts, shapes):
    height, c = parts[0].shape
    used = sum(a * b for a, b in shapes) // c
    shapes = list(shapes) + [(height - used, c)]
    if used % 16:
        total = sum(part.astype(F32) for part in parts)
        return [*unpack(total[:used], shapes[:-1]), total[used:]]
    return pl.pallas_call(
        functools.partial(finish_kernel, count=len(parts)),
        out_shape=tuple(jax.ShapeDtypeStruct(shape, F32) for shape in shapes),
        compiler_params=pltpu.CompilerParams(vmem_limit_bytes=60 * 2**20),
        name="finish_sums",
    )(*parts)


def on_device(
    hidden_in,
    lengths,
    cot_out,
    cot_cls,
    w_query,
    w_key,
    w_value,
    w_out,
    w_inner,
    w_outer,
    b_query,
    b_value,
    b_out,
    norm1_gain,
    norm1_shift,
    b_inner,
    b_outer,
    norm2_gain,
    norm2_shift,
):
    plan = Regroup()
    groups, block_len, width = hidden_in.shape
    span = groups * block_len
    per = plan.per
    fleets = [[i * per + j for j in range(per)] for i in range(2)]
    first_row = plan.passage * block_len
    owner = lax.rem(plan.me, per) == 0

    length = lax.dynamic_index_in_dim(lengths, plan.passage, 0, keepdims=False)
    info = jnp.stack(
        [
            length,
            first_row,
            plan.kept_index(),
            plan.kept_index(),
            jnp.where(owner, first_row, -1),
            lax.axis_index("batch"),
            plan.me,
        ]
    ).astype(jnp.int32)

    share = width // plan.n
    narrow = jnp.stack(
        [b_query, b_value, b_out, norm1_gain, norm1_shift, b_outer, norm2_gain, norm2_shift]
    )
    vec_shard = jnp.concatenate([narrow, b_inner.reshape(-1, share)], 0)
    vec_all = plan.all_blocks(vec_shard)
    narrow = vec_all[:, :8].transpose(1, 0, 2).reshape(8, width).astype(F32)
    bias_inner = vec_all[:, 8:].reshape(1, -1).astype(F32)

    def head_bias(query, value):
        return jnp.concatenate([query, jnp.zeros_like(query), value])[None].astype(F32)

    pairs = HEADS // 2
    hidden = plan.gather(hidden_in, plan.pick(info, hidden_in))
    heads = Weights([w_query, w_key, w_value], True)
    dense = Weights([w_out, w_inner, w_outer], False)
    if heads.by_pairs:
        near = jnp.where(plan.me == 0, vec_all[0], vec_all[1])
        far = jnp.where(plan.me == 0, vec_all[1], vec_all[0])
        biases = [head_bias(near[0], near[1]), head_bias(far[0], far[1])]
        packed, grids = heads.packed, heads.grids
    else:
        biases = [head_bias(narrow[0], narrow[1])]
        packed, grids = [heads.packed], [heads.grid_of]
    groups = len(grids)
    each = pairs // groups
    at = lambda kind: lambda j: (j // each) * 3 * each + kind * each + j % each
    found, result = None, None
    for group in range(groups):
        found = queries_keys_values(
            info, *hidden, packed[group], grids[group], biases[group], group, found
        )
        qkv, *mats = found
        if group == 0:
            cots = plan.gather(cot_out, plan.pick(info, cot_out, (qkv,)))
        if per == 1:
            sources = [(qkv, at(kind)) for kind in range(3)]
        else:
            kv = lax.all_gather(
                qkv[:, width:], "blk", axis=0, tiled=True, axis_index_groups=fleets
            )
            sources = [(qkv, at(0)), (kv, at(0)), (kv, at(1))]
        result = attend(info, sources, span, group * each, each, result)
    context_low, probs, sums = result

    own_cls = lax.dynamic_index_in_dim(cot_cls, plan.passage, 0, keepdims=True).astype(F32)
    layer_kept, layer_other, top, grad_context, grad_resid, dense_sums = middle(
        info, hidden, cots, context_low, own_cls, dense, narrow[2:], bias_inner
    )
    part_wo, part_wi, part_wu, dense_vecs = dense.scatter([dense_sums])
    part_bo, part_g1, part_s1, part_bu, part_g2, part_s2 = [dense_vecs[t] for t in range(6)]
    part_bi = dense_vecs[6 : 6 + b_inner.size // share].reshape(-1)
    layer_rows = plan.join(info, layer_kept, plan.send_back(layer_other))
    tops = plan.all_blocks(top)[::per, 0, :]
    cls_part = lax.dynamic_slice_in_dim(tops, plan.me * share, share, 1)

    back = functools.partial(
        attend_back, info, sources, grad_context, context_low, sums, probs, span
    )
    give = functools.partial(input_grad, info, resid=grad_resid, mats=mats)
    if per == 1:
        most = back([(1, 1), (1, 0), (0, 1)], None)
        other = give(
            most, out_shape=(block_len, width), dtype=BF16, kept=False, events=(cls_part,)
        )
        rest = back([(0, 0)], most, (other, layer_rows))
        other = plan.send_back(other)
    else:
        blocks = span * per // min(1024, span * per)
        grad_q, *grad_kv = back([(k, q) for k in range(blocks) for q in range(2)], None)
        most = [grad_q] + [
            lax.psum_scatter(g, "blk", scatter_dimension=0, tiled=True, axis_index_groups=fleets)
            for g in grad_kv
        ]
        other = plan.send_back(give(most, out_shape=(block_len, width), dtype=BF16, kept=False))
        rest = most
    head_sums = head_grads(
        info, hidden, rest, most, heads.sums_of, 2 if heads.by_pairs else 1, (other,)
    )
    kept = give(rest, out_shape=hidden[0].shape, dtype=F32, kept=True)
    grad_input = plan.join(info, kept, other)
    part_wq, part_wk, part_wv, head_vecs = heads.scatter(
        head_sums, (grad_input, part_wo, dense_vecs)
    )
    part_bq, part_bv = head_vecs[0], head_vecs[1]
    return (
        layer_rows,
        cls_part,
        grad_input,
        part_wq,
        part_wk,
        part_wv,
        part_wo,
        part_wi,
        part_wu,
        part_bq,
        part_bv,
        part_bo,
        part_g1,
        part_s1,
        part_bi,
        part_bu,
        part_g2,
        part_s2,
    )


def solution(mesh):
    rows = P("batch", "blk", None)
    mats = (P("batch", "blk"),) * 6
    vecs = (P("blk"),) * 9
    return jax.shard_map(
        on_device,
        mesh=mesh,
        in_specs=(rows, P("batch"), rows, P("batch", None)) + mats + vecs,
        out_specs=(rows, P("batch", "blk"), rows) + mats + vecs,
        check_vma=False,
    )
```

```python
import functools

import jax
import jax.numpy as jnp
from jax import lax
from jax.experimental import pallas as pl
from jax.experimental.pallas import tpu as pltpu
from jax.sharding import PartitionSpec as P

HEADS = 12
HDIM = 64
PAIR = 2 * HDIM
LOG2E = 1.4426950408889634
BF16 = jnp.bfloat16
F32 = jnp.float32


def live_rows(shape, axis, start, length, shift, span):
    rows = shape[axis]
    step = min(rows, span)
    parts = []
    for at in range(0, rows, step):
        first = start + at
        base = (first // span) * span
        sizes = list(shape)
        sizes[axis] = step
        turned = lax.broadcasted_iota(jnp.int32, tuple(sizes), axis) + (first - base + shift)
        turned = jnp.where(turned >= span, turned - span, turned)
        parts.append(turned < length - base)
    return parts[0] if len(parts) == 1 else jnp.concatenate(parts, axis)


def chunk_of(rows):
    return min(1024, rows // 2)


def segments(rows, size):
    for at in range(0, rows, size):
        for h in range(2):
            yield h, slice(at, at + size), slice(2 * at + h * size, 2 * at + (h + 1) * size)


def beside(part, h):
    blank = jnp.zeros_like(part)
    return jnp.concatenate([part, blank] if h == 0 else [blank, part], 0)


def head_rows(h):
    return slice(h * HDIM, (h + 1) * HDIM)


def attend_kernel(
    info, q_ref, k_ref, v_ref, *rest, chunk, across, span, extra
):
    out_ref, p_ref, sum_ref, keys, vals, ques, bound, turned = rest[extra:]
    pos = pl.program_id(1)
    kv = k_ref.shape[0]
    size, width = out_ref.shape[0], p_ref.shape[2]
    factor = HDIM**-0.5 * LOG2E

    @pl.when(pos == 0)
    def prepare():
        live = live_rows((kv, PAIR), 0, 0, info[0], info[1], span)
        kept = jnp.where(live, k_ref[...], jnp.zeros((), BF16))
        keys[...] = kept
        vals[0:PAIR, :] = jnp.where(live, v_ref[...], jnp.zeros((), BF16)).T
        vals[PAIR:, :] = live_rows((16, kv), 1, 0, info[0], info[1], span).astype(BF16)
        turned_q = q_ref[...].T
        squares = kept.astype(F32)
        squares = (squares * squares).astype(BF16)
        half = lambda axis: lax.broadcasted_iota(jnp.int32, (PAIR, PAIR), axis) // HDIM
        sizes = jnp.dot(squares, (half(0) == half(1)).astype(BF16), preferred_element_type=F32)
        largest = jnp.max(sizes, axis=0, keepdims=True)
        tops = [jnp.max(largest[:, head_rows(h)], axis=1, keepdims=True) for h in range(2)]
        for h, queries, cols in segments(q_ref.shape[0], size):
            mine = turned_q[head_rows(h), queries]
            ques[:, cols] = beside(mine, h)
            sharp = mine.astype(F32)
            reach = jnp.sum(sharp * sharp, axis=0, keepdims=True)
            bound[:, cols] = jnp.sqrt(reach * tops[h] * 1.03) * factor

    cols = pl.ds(pl.multiple_of(pos * width, width), width)

    def weigh(peak):
        for start in range(0, width, across):
            own = slice(start, start + across)
            query = ques[:, pl.ds(pl.multiple_of(pos * width + start, across), across)]
            for at in range(0, kv, chunk):
                rows = slice(at, at + chunk)
                scores = jnp.dot(keys[rows, :], query, preferred_element_type=F32)
                p_ref[0, rows, own] = jnp.exp2(scores * factor - peak[:, own]).astype(BF16)
        total = jnp.dot(vals[...], p_ref[0], preferred_element_type=F32)
        sums = total[PAIR : PAIR + 1, :]
        sum_ref[0] = sums
        for h in range(2):
            own = slice(h * size, (h + 1) * size)
            turned[head_rows(h), :] = total[head_rows(h), own] / sums[:, own]
        return jnp.min(sums)

    def exact_peak():
        query = ques[:, cols]

        def largest(at, peak):
            rows = pl.ds(pl.multiple_of(at * chunk, chunk), chunk)
            scores = jnp.dot(keys[rows, :], query, preferred_element_type=F32)
            live = live_rows((chunk, width), 0, at * chunk, info[0], info[1], span)
            return jnp.maximum(peak, jnp.max(jnp.where(live, scores, -1e30), axis=0, keepdims=True))

        return lax.fori_loop(0, kv // chunk, largest, jnp.full((1, width), -1e30, F32)) * factor

    lowest = weigh(bound[:, cols])

    @pl.when(jnp.logical_not(lowest > 2.0**-70))
    def again():
        weigh(exact_peak())

    out_ref[...] = turned[...].T.astype(BF16)


def attend(info, sources, span, first, count, before):
    (queries, q_at), (keys, k_at), (values, v_at) = sources
    rows, kv = queries.shape[0], keys.shape[0]
    size = chunk_of(rows)
    pairs = HEADS // 2
    before = before or ()
    return pl.pallas_call(
        functools.partial(
            attend_kernel,
            chunk=min(256, kv),
            across=min(256, 2 * size),
            span=span,
            extra=len(before),
        ),
        out_shape=(
            jax.ShapeDtypeStruct((rows, HEADS * HDIM), BF16),
            jax.ShapeDtypeStruct((pairs, kv, 2 * rows), BF16),
            jax.ShapeDtypeStruct((pairs, 1, 2 * rows), F32),
        ),
        grid_spec=pltpu.PrefetchScalarGridSpec(
            num_scalar_prefetch=1,
            grid=(count, rows // size),
            in_specs=[
                pl.BlockSpec((rows, PAIR), lambda j, c, s: (0, q_at(first + j))),
                pl.BlockSpec((kv, PAIR), lambda j, c, s: (0, k_at(first + j))),
                pl.BlockSpec((kv, PAIR), lambda j, c, s: (0, v_at(first + j))),
            ]
            + any_specs(before),
            out_specs=(
                pl.BlockSpec((size, PAIR), lambda j, c, s: (c, first + j)),
                pl.BlockSpec((1, kv, 2 * size), lambda j, c, s: (first + j, 0, c)),
                pl.BlockSpec((1, 1, 2 * size), lambda j, c, s: (first + j, 0, c)),
            ),
            scratch_shapes=[
                pltpu.VMEM((kv, PAIR), BF16),
                pltpu.VMEM((PAIR + 16, kv), BF16),
                pltpu.VMEM((PAIR, 2 * rows), BF16),
                pltpu.VMEM((1, 2 * rows), F32),
                pltpu.VMEM((PAIR, size), F32),
            ],
        ),
        input_output_aliases={4 + t: t for t in range(len(before))},
        compiler_params=pltpu.CompilerParams(vmem_limit_bytes=60 * 2**20),
        name="attend",
    )(info, queries, keys, values, *before)


def attend_back_kernel(
    info,
    units,
    q_ref,
    k_ref,
    v_ref,
    g_ref,
    ctx_ref,
    sum_ref,
    p_ref,
    *rest,
    chunk,
    size,
    span,
    more,
    extra,
):
    before, rest = (rest[:3], rest[3:]) if more else (None, rest)
    rest = rest[extra:]
    gq_ref, gk_ref, gv_ref, keys, grads, grads_up, ques_up, delta, low, total, key_sum, value_sum = rest
    step = pl.program_id(1)
    kv, rows = k_ref.shape[0], q_ref.shape[0]
    block, part = p_ref.shape[1:]
    scale = HDIM**-0.5

    @pl.when(step == 0)
    def prepare():
        live = live_rows((kv, PAIR), 0, 0, info[0], info[1], span)
        keys[...] = jnp.where(live, k_ref[...], jnp.zeros((), BF16)).T
        turned = g_ref[...].T.astype(F32)
        dots = turned * ctx_ref[...].T.astype(F32)
        for h, queries, cols in segments(rows, size):
            inverse = 1.0 / sum_ref[0, :, cols]
            own = head_rows(h)
            delta[:, cols] = jnp.sum(dots[own, queries], axis=0, keepdims=True) * inverse
            shared = beside((turned[own, queries] * inverse).astype(BF16), h)
            grads[:, cols] = shared
            grads_up[cols, :] = shared.T
            lane = lax.broadcasted_iota(jnp.int32, (queries.stop - queries.start, PAIR), 1)
            ques_up[cols, :] = jnp.where(lane // HDIM == h, q_ref[queries, :], jnp.zeros((), BF16))
        for held in (total, key_sum, value_sum):
            held[...] = jnp.zeros_like(held)

    here = pl.ds(pl.multiple_of(units[0, step] * block, block), block)
    there = pl.multiple_of(units[1, step] * part, part)
    cols = pl.ds(there, part)
    values = v_ref[here, :]
    for start in range(0, part, chunk):
        own = slice(start, start + chunk)
        from_all = pl.ds(there + start, chunk)
        change = jnp.dot(values, grads[:, from_all], preferred_element_type=F32)
        low[:, own] = (p_ref[0, :, own].astype(F32) * (change - delta[:, from_all])).astype(BF16)
    value_sum[here, :] += jnp.dot(p_ref[0], grads_up[cols, :], preferred_element_type=F32)
    key_sum[here, :] += jnp.dot(low[...], ques_up[cols, :], preferred_element_type=F32)
    total[:, cols] += jnp.dot(keys[:, here], low[...], preferred_element_type=F32)

    @pl.when(step == pl.num_programs(1) - 1)
    def finish():
        live = live_rows((kv, PAIR), 0, 0, info[0], info[1], span)
        zero = jnp.zeros((), F32)
        found = [jnp.where(live, key_sum[...] * scale, zero), jnp.where(live, value_sum[...], zero)]
        for t, (ref, value) in enumerate(zip((gk_ref, gv_ref), found)):
            if more:
                value += before[t + 1][...].astype(F32)
            ref[...] = value.astype(BF16)
        parts = [[], []]
        for h, queries, cols in segments(rows, size):
            parts[h].append(total[head_rows(h), cols])
        value = (jnp.concatenate([jnp.concatenate(p, 1) for p in parts], 0) * scale).T
        if more:
            value += before[0][...].astype(F32)
        gq_ref[...] = value.astype(BF16)


def attend_back(info, sources, grad, context, sums, probs, span, units, before, events=()):
    (queries, q_at), (keys, k_at), (values, v_at) = sources
    rows, kv = queries.shape[0], keys.shape[0]
    pairs = HEADS // 2
    wide = HEADS * HDIM
    more = before is not None
    block, part, size = min(1024, kv), rows, chunk_of(rows)
    cut = 2 if more else 1
    rows, kv = rows // cut, kv // cut
    out_rows = [rows, kv, kv]
    heights = [rows * cut, kv * cut, kv * cut]
    units = jnp.array(list(zip(*units)), jnp.int32)
    col = lambda height, at=lambda j: j: pl.BlockSpec(
        (height, PAIR), lambda j, c, s, u: (0, at(j))
    )
    return pl.pallas_call(
        functools.partial(
            attend_back_kernel,
            chunk=min(512, part),
            size=size,
            span=span,
            more=more,
            extra=len(events),
        ),
        out_shape=tuple(jax.ShapeDtypeStruct((height, wide), BF16) for height in heights),
        grid_spec=pltpu.PrefetchScalarGridSpec(
            num_scalar_prefetch=2,
            grid=(pairs, units.shape[1]),
            in_specs=[
                col(rows, q_at),
                col(kv, k_at),
                col(kv, v_at),
                col(rows),
                col(rows),
                pl.BlockSpec((1, 1, 2 * rows), lambda j, c, s, u: (j, 0, 0)),
                pl.BlockSpec((1, block, part), lambda j, c, s, u: (j, u[0, c], u[1, c])),
            ]
            + ([col(height) for height in out_rows] if more else [])
            + any_specs(events),
            out_specs=tuple(col(height) for height in out_rows),
            scratch_shapes=[
                pltpu.VMEM((PAIR, kv), BF16),
                pltpu.VMEM((PAIR, 2 * rows), BF16),
                pltpu.VMEM((2 * rows, PAIR), BF16),
                pltpu.VMEM((2 * rows, PAIR), BF16),
                pltpu.VMEM((1, 2 * rows), F32),
                pltpu.VMEM((block, part), BF16),
                pltpu.VMEM((PAIR, 2 * rows), F32),
                pltpu.VMEM((kv, PAIR), F32),
                pltpu.VMEM((kv, PAIR), F32),
            ],
        ),
        input_output_aliases={9 + t: t for t in range(3)} if more else {},
        compiler_params=pltpu.CompilerParams(vmem_limit_bytes=60 * 2**20),
        name="attend_back_last" if more else "attend_back",
    )(info, units, queries, keys, values, grad, context, sums, probs, *(before or ()), *events)


def rows_of(kept_ref, other_ref, step, split):
    return jnp.where(step < split, kept_ref[0], other_ref[...])


def project(rows, weight):
    return jnp.dot(rows, weight, preferred_element_type=F32)


def project_back(grads, weight):
    return lax.dot_general(grads, weight, (((1,), (1,)), ((), ())), preferred_element_type=F32)


def weight_grad(rows, grads):
    return lax.dot_general(rows, grads, (((0,), (0,)), ((), ())), preferred_element_type=F32)


def run_all(copies):
    for copy in copies:
        copy.start()
    return copies


def wait_all(copies):
    for copy in copies:
        copy.wait()


class Pieces:
    def __init__(self, shape, mesh_shape, bundles, turned=()):
        self.turned = turned
        self.r, self.c = shape
        self.m, self.n = mesh_shape
        self.bundles = bundles
        self.slots = self.m * self.n

    def place(self, masks, slot, info):
        if masks is None:
            return slot // self.n, lax.rem(slot, self.n)
        return info[5] ^ (masks[slot] // self.n), masks[slot] % self.n

    def copies(self, refs, mats, sems, info, out):
        found = [[] for _ in mats]
        r, c = self.r, self.c
        count = 0
        for (masks, members), ref in zip(self.bundles, refs):
            for slot in range(self.slots if masks is None else len(masks)):
                j, i = self.place(masks, slot, info)
                at = 0
                for t in members:
                    mat = mats[t]
                    tall = mat.shape[0] // (self.m * r)
                    wide = max(mat.shape[1] // (self.n * c), 1)
                    for w in range(wide):
                        if isinstance(ref, (tuple, list)):
                            each = self.slots // len(ref)
                            block = ref[slot // each].at[slot % each, pl.ds(at, tall * r), :]
                        else:
                            block = ref.at[slot, pl.ds(at, tall * r), :]
                        row = j ^ (info[6] * (self.m // 2)) if t in self.turned else j
                        down = pl.multiple_of(row * (tall * r), tall * r)
                        side = (i * wide + w) * c if mat.shape[1] > c else 0
                        place = mat.at[pl.ds(down, tall * r), pl.ds(side, c)]
                        at += tall * r
                        pair = (place, block) if out else (block, place)
                        found[t].append(pltpu.make_async_copy(*pair, sems.at[count]))
                        count += 1
        return found

    def count(self):
        return 9 * self.slots


def any_specs(arrays):
    return [pl.BlockSpec(memory_space=pl.ANY)] * len(arrays)


def queries_kernel(info, kept_ref, other_ref, bias_ref, *rest, split, grid_of, extra, carry):
    count = len(grid_of.bundles)
    packed, rest = rest[:count], rest[count + extra :]
    step = pl.program_id(0)
    if carry:
        carried, (out_ref, mat_q, mat_k, mat_v, picked, sems) = rest[0], rest[1:]
        if carried.shape == picked.shape:

            @pl.when(step == 0)
            def copy():
                picked[...] = carried[...]

        else:
            picked[...] = carried[0]
    else:
        out_ref, mat_q, mat_k, mat_v, sems = rest
    mats = [mat_q, mat_k, mat_v]

    @pl.when(step == 0)
    def load():
        loads = grid_of.copies(packed, mats, sems, info, False)
        for group in loads:
            run_all(group)
        for group in loads:
            wait_all(group)

    rows = rows_of(kept_ref, other_ref, step, split)
    width = mat_q.shape[1]
    for t, mat in enumerate(mats):
        cols = slice(t * width, (t + 1) * width)
        out_ref[:, cols] = (project(rows, mat[...]) + bias_ref[:, cols]).astype(BF16)


def split_specs(kept_at, tile, split, width):
    return [
        pl.BlockSpec((1, tile, width), lambda i, s: (s[kept_at], jnp.minimum(i, split - 1), 0)),
        pl.BlockSpec((tile, width), lambda i, s: (jnp.maximum(i - split, 0), 0)),
    ]


def whole_spec(shape):
    return pl.BlockSpec(shape, lambda i, s: (0,) * len(shape))


def queries_keys_values(info, kept, other, packed, grid_of, bias, group, before, carried=None):
    block_len, width = other.shape
    tile = min(512, block_len)
    split = block_len // tile
    wide = bias.shape[1]
    before = before or ()
    carried = [] if carried is None else [carried]
    if not carried:
        moves = ([], (), ())
    elif carried[0].shape[1:] == other.shape:
        part = block_len // (2 * split)
        moves = (
            [pl.BlockSpec((1, part, width), lambda i, s: (1 - s[2], i, 0))],
            (pl.BlockSpec((part, width), lambda i, s: (i, 0)),),
            (jax.ShapeDtypeStruct(other.shape, BF16),),
        )
    else:
        spec = whole_spec(carried[0].shape)
        moves = ([spec], (spec,), (jax.ShapeDtypeStruct(carried[0].shape, BF16),))
    mat = jax.ShapeDtypeStruct((width, width), BF16)
    inputs = [kept, other, bias, *packed]
    return pl.pallas_call(
        functools.partial(
            queries_kernel,
            split=split,
            grid_of=grid_of,
            extra=len(before),
            carry=bool(carried),
        ),
        out_shape=(jax.ShapeDtypeStruct((2 * block_len, 3 * width), BF16), mat, mat, mat)
        + moves[2],
        grid_spec=pltpu.PrefetchScalarGridSpec(
            num_scalar_prefetch=1,
            grid=(2 * split,),
            in_specs=split_specs(2, tile, split, width)
            + [whole_spec(bias.shape)]
            + any_specs(packed)
            + any_specs(before)
            + moves[0],
            out_specs=(pl.BlockSpec((tile, wide), lambda i, s: (i, group)),)
            + (pl.BlockSpec((width, wide // 3), lambda i, s: (0, group)),) * 3
            + moves[1],
            scratch_shapes=[pltpu.SemaphoreType.DMA((grid_of.count(),))],
        ),
        input_output_aliases={1 + len(inputs) + t: t for t in range(len(before))},
        compiler_params=pltpu.CompilerParams(vmem_limit_bytes=60 * 2**20),
        name="queries",
    )(info, *inputs, *before, *carried)


def normal(values):
    middle = jnp.mean(values, axis=-1, keepdims=True)
    centered = values - middle
    spread = jnp.mean(centered * centered, axis=-1, keepdims=True)
    inverse = lax.rsqrt(spread + 1e-12)
    return centered * inverse, inverse


def normal_back(grad, unit, inverse, gain):
    scaled = grad * gain
    mean = jnp.mean(scaled, axis=-1, keepdims=True)
    along = jnp.mean(scaled * unit, axis=-1, keepdims=True)
    return (scaled - mean - unit * along) * inverse


def gelu_pair(u):
    phi = 0.5 + 0.5 * lax.erf(0.7071067811865476 * u)
    bell = jnp.exp2((-0.5 * LOG2E) * (u * u))
    return u * phi, phi + (0.3989422804014327 * u) * bell


def add_rows(total, at, values):
    total[at : at + 1, 0 : values.shape[1]] += jnp.sum(values, axis=0, keepdims=True)


def middle_kernel(
    info,
    hid_kept,
    hid_other,
    cot_kept,
    cot_other,
    ctx_ref,
    cls_ref,
    vec_ref,
    inner_bias,
    packed,
    layer_kept,
    layer_other,
    top_ref,
    grad_ctx_ref,
    resid_ref,
    sums_ref,
    mat_out,
    mat_inner,
    mat_outer,
    acc_out,
    acc_inner,
    acc_outer,
    totals,
    active,
    slope,
    low,
    vec_low,
    sems,
    vec_sems,
    *,
    split,
    grid_of,
    chunk,
):
    step = pl.program_id(0)
    last = pl.num_programs(0) - 1
    mats = [mat_out, mat_inner, mat_outer]
    tile, width = ctx_ref.shape
    ff = mat_inner.shape[1]
    loads = grid_of.copies([packed], mats, sems, info, False)

    @pl.when(step == 0)
    def start():
        for group in loads:
            run_all(group)
        for acc in (acc_out, acc_inner, acc_outer, totals):
            acc[...] = jnp.zeros_like(acc)
        wait_all(loads[0])

    bias_out, gain_one, shift_one, bias_outer, gain_two, shift_two = [
        vec_ref[t : t + 1, :] for t in range(6)
    ]
    hidden = rows_of(hid_kept, hid_other, step, split).astype(F32)
    context = ctx_ref[...]
    unit_one, inverse_one = normal(hidden + project(context, mat_out[...]) + bias_out)
    normed = unit_one * gain_one + shift_one
    normed_low = normed.astype(BF16)

    @pl.when(step == 0)
    def more():
        wait_all(loads[1])
        wait_all(loads[2])

    for at in range(0, ff, chunk):
        cols = slice(at, at + chunk)
        inner = project(normed_low, mat_inner[:, cols]) + inner_bias[:, cols]
        value, change = gelu_pair(inner)
        active[:, cols] = value.astype(BF16)
        slope[:, cols] = change.astype(BF16)
    unit_two, inverse_two = normal(normed + project(active[...], mat_outer[...]) + bias_outer)
    layer = (unit_two * gain_two + shift_two).astype(BF16)

    @pl.when(step < split)
    def kept():
        layer_kept[0] = layer

    @pl.when(step >= split)
    def other():
        layer_other[...] = layer

    @pl.when(step * tile == info[1])
    def top():
        top_ref[...] = layer[0:16, :]


    row = step * tile + lax.broadcasted_iota(jnp.int32, (tile, width), 0)
    grad_result = rows_of(cot_kept, cot_other, step, split).astype(F32)
    grad_result += jnp.where(row == info[4], cls_ref[...], 0.0)
    add_rows(totals, 4, grad_result * unit_two)
    add_rows(totals, 5, grad_result)
    grad_resid_two = normal_back(grad_result, unit_two, inverse_two, gain_two)
    grad_outer = grad_resid_two.astype(BF16)
    add_rows(totals, 3, grad_outer.astype(F32))
    for at in range(0, ff, chunk):
        cols = slice(at, at + chunk)
        grad_inner = project_back(grad_outer, mat_outer[cols, :]) * slope[:, cols].astype(F32)
        low[:, cols] = grad_inner.astype(BF16)
        totals[8:9, cols] += jnp.sum(grad_inner, axis=0, keepdims=True)
        acc_outer[cols, :] += weight_grad(active[:, cols], grad_outer)
    grad_normed = grad_resid_two + project_back(low[...], mat_inner[...])
    for at in range(0, ff, chunk):
        cols = slice(at, at + chunk)
        acc_inner[:, cols] += weight_grad(normed_low, low[:, cols])
    add_rows(totals, 1, grad_normed * unit_one)
    add_rows(totals, 2, grad_normed)
    grad_resid_one = normal_back(grad_normed, unit_one, inverse_one, gain_one)
    resid_ref[...] = grad_resid_one
    grad_attn = grad_resid_one.astype(BF16)
    add_rows(totals, 0, grad_attn.astype(F32))
    acc_out[...] += weight_grad(context, grad_attn)
    grad_ctx_ref[...] = project_back(grad_attn, mat_out[...]).astype(BF16)

    @pl.when(step == last)
    def finish():
        r, c, m, n = grid_of.r, grid_of.c, grid_of.m, grid_of.n
        stores = grid_of.copies([sums_ref], mats, sems, info, True)
        for mat, acc, group in zip(mats, (acc_out, acc_inner, acc_outer), stores):
            mat[...] = acc[...].astype(BF16)
            run_all(group)
        vec_low[...] = jnp.zeros_like(vec_low)
        for i in range(n):
            for t in range(6):
                vec_low[i, t : t + 1, :] = totals[t : t + 1, i * c : (i + 1) * c]
            wide = ff // (n * c)
            for t in range(wide):
                at = (i * wide + t) * c
                vec_low[i, 6 + t : 7 + t, :] = totals[8:9, at : at + c]
        tails = []
        vec_bits = vec_low[...].astype(BF16)
        for i in range(n):
            active[16 * i : 16 * i + 16, 0:c] = vec_bits[i]
        for j in range(m):
            for i in range(n):
                tails.append(
                    pltpu.make_async_copy(
                        active.at[pl.ds(16 * i, 16), pl.ds(0, c)],
                        sums_ref.at[j * n + i, pl.ds(9 * r, 16), :],
                        vec_sems.at[j * n + i],
                    )
                )
        run_all(tails)
        for group in stores:
            wait_all(group)
        wait_all(tails)


def kept_spec(tile, split, width):
    return pl.BlockSpec((1, tile, width), lambda i, s: (s[2], jnp.minimum(i, split - 1), 0))


def other_spec(tile, split, width):
    return pl.BlockSpec((tile, width), lambda i, s: (jnp.maximum(i - split, 0), 0))


def middle(info, hidden, cots, context, cls_row, weights, vectors, inner_bias):
    block_len, width = hidden[1].shape
    grid_of = weights.grid_of
    ff = inner_bias.shape[1]
    tile = min(256, block_len)
    split = block_len // tile
    row_spec = pl.BlockSpec((tile, width), lambda i, s: (i, 0))
    return pl.pallas_call(
        functools.partial(middle_kernel, split=split, grid_of=grid_of, chunk=768),
        out_shape=(
            jax.ShapeDtypeStruct(hidden[0].shape, BF16),
            jax.ShapeDtypeStruct((block_len, width), BF16),
            jax.ShapeDtypeStruct((16, width), BF16),
            jax.ShapeDtypeStruct((2 * block_len, width), BF16),
            jax.ShapeDtypeStruct((2 * block_len, width), F32),
            jax.ShapeDtypeStruct((grid_of.slots, 9 * grid_of.r + 16, grid_of.c), BF16),
        ),
        grid_spec=pltpu.PrefetchScalarGridSpec(
            num_scalar_prefetch=1,
            grid=(2 * split,),
            in_specs=split_specs(2, tile, split, width)
            + split_specs(2, tile, split, width)
            + [
                row_spec,
                whole_spec(cls_row.shape),
                whole_spec(vectors.shape),
                whole_spec(inner_bias.shape),
                pl.BlockSpec(memory_space=pl.ANY),
            ],
            out_specs=(
                kept_spec(tile, split, width),
                other_spec(tile, split, width),
                whole_spec((16, width)),
                row_spec,
                row_spec,
                pl.BlockSpec(memory_space=pl.ANY),
            ),
            scratch_shapes=[
                pltpu.VMEM((width, width), BF16),
                pltpu.VMEM((width, ff), BF16),
                pltpu.VMEM((ff, width), BF16),
                pltpu.VMEM((width, width), F32),
                pltpu.VMEM((width, ff), F32),
                pltpu.VMEM((ff, width), F32),
                pltpu.VMEM((16, ff), F32),
                pltpu.VMEM((tile, ff), BF16),
                pltpu.VMEM((tile, ff), BF16),
                pltpu.VMEM((tile, ff), BF16),
                pltpu.VMEM((grid_of.n, 16, grid_of.c), F32),
                pltpu.SemaphoreType.DMA((grid_of.count(),)),
                pltpu.SemaphoreType.DMA((grid_of.slots,)),
            ],
        ),
        compiler_params=pltpu.CompilerParams(vmem_limit_bytes=60 * 2**20),
        name="middle",
    )(info, *hidden, *cots, context, cls_row, vectors, inner_bias, *weights.packed)


def input_grad_kernel(info, gq_ref, gk_ref, gv_ref, resid_ref, mat_q, mat_k, mat_v, *rest, kept, join):
    if join:
        arrived, grad_ref, joined = rest[0], rest[-2], rest[-1]
        joined[0] = arrived[...].astype(joined.dtype)
    else:
        grad_ref = rest[-1]
    total = resid_ref[...]
    for ref, mat in zip((gq_ref, gk_ref, gv_ref), (mat_q, mat_k, mat_v)):
        total += project_back(ref[...], mat[...])
    if kept:
        grad_ref[0] = total.astype(grad_ref.dtype)
    else:
        grad_ref[...] = total.astype(grad_ref.dtype)


def input_grad(info, grads, resid, mats, out_shape, dtype, kept, join=(), events=()):
    rows, width = resid.shape
    block_len = rows // 2
    tile = min(512, block_len)
    split = block_len // tile
    off = 0 if kept else split
    spec = pl.BlockSpec((tile, width), lambda i, s: (i + off, 0))
    place = kept_spec(tile, split, width) if kept else other_spec(tile, 0, width)
    out = (jax.ShapeDtypeStruct(out_shape, dtype),)
    in_specs = [spec] * 4 + [whole_spec(mat.shape) for mat in mats]
    out_specs = (place,)
    aliases = {}
    if join:
        in_specs += [pl.BlockSpec((tile, width), lambda i, s: (i, 0))] + any_specs(join[:1])
        out += (jax.ShapeDtypeStruct(join[0].shape, join[0].dtype),)
        out_specs += (pl.BlockSpec((1, tile, width), lambda i, s: (1 - s[2], i, 0)),)
        aliases = {len(in_specs): 1}
    return pl.pallas_call(
        functools.partial(input_grad_kernel, kept=kept, join=bool(join)),
        out_shape=out,
        grid_spec=pltpu.PrefetchScalarGridSpec(
            num_scalar_prefetch=1,
            grid=(split,),
            in_specs=in_specs + any_specs(events),
            out_specs=out_specs,
        ),
        input_output_aliases=aliases,
        compiler_params=pltpu.CompilerParams(vmem_limit_bytes=60 * 2**20),
        name="input_grad_kept" if kept else "input_grad_other",
    )(info, *grads, resid, *mats, *join[::-1], *events)


def head_grads_kernel(info, hid_kept, hid_other, *rest, split, grid_of, outs, extra):
    found, rest = rest[:3], rest[3 + extra :]
    sums, (acc, mat_q, mat_k, mat_v, totals, vec_low, sems, vec_sems) = rest[:outs], rest[outs:]
    mats = [mat_q, mat_k, mat_v]
    step = pl.program_id(0)

    @pl.when(step == 0)
    def clear():
        acc[...] = jnp.zeros_like(acc)
        totals[...] = jnp.zeros_like(totals)

    rows = rows_of(hid_kept, hid_other, step, split)
    grads = [ref[...] for ref in found]
    for t, grad in enumerate(grads):
        acc[t] += weight_grad(rows, grad)
    add_rows(totals, 0, grads[0].astype(F32))
    add_rows(totals, 1, grads[2].astype(F32))

    @pl.when(step == pl.num_programs(0) - 1)
    def finish():
        r, c, n = grid_of.r, grid_of.c, grid_of.n
        ((masks, _),) = grid_of.bundles
        stores = grid_of.copies([list(sums)], mats, sems, info, True)
        for t, mat in enumerate(mats):
            mat[...] = acc[t].astype(BF16)
            run_all(stores[t])
        for i in range(n):
            part = jnp.concatenate([totals[0:2, i * c : (i + 1) * c], jnp.zeros((14, c), F32)], 0)
            vec_low[i] = part.astype(BF16)
        tails = []
        each = grid_of.slots // outs
        for slot in range(grid_of.slots):
            j, i = grid_of.place(masks, slot, info)
            place = sums[slot // each].at[slot % each, pl.ds(3 * r, 16), :]
            tails.append(pltpu.make_async_copy(vec_low.at[i], place, vec_sems.at[slot]))
        run_all(tails)
        for group in stores:
            wait_all(group)
        wait_all(tails)


def head_grads(info, hidden, grads, grid_of, outs, events=()):
    block_len, width = hidden[1].shape
    tile = min(512, block_len)
    split = block_len // tile
    rows = pl.BlockSpec((tile, width), lambda i, s: (i, 0))
    block = (grid_of.slots // outs, 3 * grid_of.r + 16, grid_of.c)
    return pl.pallas_call(
        functools.partial(
            head_grads_kernel, split=split, grid_of=grid_of, outs=outs, extra=len(events)
        ),
        out_shape=(jax.ShapeDtypeStruct(block, BF16),) * outs,
        grid_spec=pltpu.PrefetchScalarGridSpec(
            num_scalar_prefetch=1,
            grid=(2 * split,),
            in_specs=split_specs(2, tile, split, width) + [rows] * 3 + any_specs(events),
            out_specs=(pl.BlockSpec(memory_space=pl.ANY),) * outs,
            scratch_shapes=[pltpu.VMEM((3, width, width), F32)]
            + [pltpu.VMEM((width, width), BF16)] * 3
            + [
                pltpu.VMEM((8, width), F32),
                pltpu.VMEM((grid_of.n, 16, grid_of.c), BF16),
                pltpu.SemaphoreType.DMA((grid_of.count(),)),
                pltpu.SemaphoreType.DMA((grid_of.slots,)),
            ],
        ),
        compiler_params=pltpu.CompilerParams(vmem_limit_bytes=60 * 2**20),
        name="head_grads",
    )(info, *hidden, *grads, *events)


def pack_kernel(*refs, count):
    out = refs[-1]
    c = out.shape[1]
    at = 0
    for ref in refs[:count]:
        rows, cols = ref.shape
        for start in range(0, cols, c):
            out[at : at + rows, :] = ref[:, start : start + c]
            at += rows


def pack_after(shards, events):
    c = min(s.shape[1] for s in shards)
    rows = sum(s.size for s in shards) // c
    return pl.pallas_call(
        functools.partial(pack_kernel, count=len(shards)),
        out_shape=jax.ShapeDtypeStruct((rows, c), BF16),
        in_specs=[pl.BlockSpec(memory_space=pltpu.VMEM)] * len(shards) + any_specs(events),
        compiler_params=pltpu.CompilerParams(vmem_limit_bytes=60 * 2**20),
        name="pack",
    )(*shards, *events)


def add_kernel(*refs, count, extra):
    parts, outs = refs[:count], refs[count + extra :]
    each = outs[0].shape[0]
    for k, out in enumerate(outs):
        here = slice(k * each, (k + 1) * each)
        out[...] = sum(part[here].astype(F32) for part in parts).astype(BF16)


def add_blocks(parts, groups, events):
    shape = (parts[0].shape[0] // groups,) + parts[0].shape[1:]
    return pl.pallas_call(
        functools.partial(add_kernel, count=len(parts), extra=len(events)),
        out_shape=(jax.ShapeDtypeStruct(shape, BF16),) * groups,
        in_specs=[pl.BlockSpec(memory_space=pltpu.VMEM)] * len(parts) + any_specs(events),
        compiler_params=pltpu.CompilerParams(vmem_limit_bytes=60 * 2**20),
        name="add_blocks",
    )(*parts, *events)


def place_kernel(info, base_ref, other_ref, out_ref):
    out_ref[0] = other_ref[...].astype(out_ref.dtype)


def place_other(info, base, other):
    block_len, width = other.shape
    tile = min(512, block_len)
    return pl.pallas_call(
        place_kernel,
        out_shape=jax.ShapeDtypeStruct(base.shape, base.dtype),
        grid_spec=pltpu.PrefetchScalarGridSpec(
            num_scalar_prefetch=1,
            grid=(block_len // tile,),
            in_specs=[
                pl.BlockSpec(memory_space=pl.ANY),
                pl.BlockSpec((tile, width), lambda i, s: (i, 0)),
            ],
            out_specs=pl.BlockSpec((1, tile, width), lambda i, s: (1 - s[2], i, 0)),
        ),
        input_output_aliases={1: 0},
        compiler_params=pltpu.CompilerParams(vmem_limit_bytes=60 * 2**20),
        name="place_other",
    )(info, base, other)


def swap(block, axis, route):
    if all(a == b for a, b in route):
        return block
    return lax.ppermute(block, axis, route)


class Regroup:
    def __init__(self):
        self.n = lax.axis_size("blk")
        self.me = lax.axis_index("blk")
        self.per = self.n // 2
        self.passage = self.me // self.per
        self.part = lax.rem(self.me, 2)
        self.first = [(i, (i % 2) * self.per + i // 2) for i in range(self.n)]
        self.second = [(i, (1 - i % 2) * self.per + i // 2) for i in range(self.n)]
        self.stays = all(a == b for a, b in self.first)

    def pick(self, pair):
        return lax.dynamic_index_in_dim(pair, 1 - self.part, 0, keepdims=False)

    def gather(self, pair, picked):
        other = swap(picked, "blk", self.second)
        if self.stays:
            return (pair, other)
        kept = lax.dynamic_index_in_dim(pair, self.part, 0, keepdims=True)
        return (swap(kept, "blk", self.first), other)

    def kept_index(self):
        return self.part if self.stays else jnp.zeros_like(self.part)

    def all_blocks(self, block):
        if self.n != 2:
            return lax.all_gather(block, "blk", axis=0)
        other = lax.ppermute(block, "blk", [(0, 1), (1, 0)])
        return jnp.where(self.me == 0, jnp.stack([block, other]), jnp.stack([other, block]))

    def send_back(self, other):
        return swap(other, "blk", [(b, a) for a, b in self.second])

    def join(self, info, kept, other):
        if self.stays:
            return place_other(info, kept, other)
        kept = swap(kept[0], "blk", [(b, a) for a, b in self.first])
        other = other.astype(kept.dtype)
        return jnp.where(self.part == 0, jnp.stack([kept, other]), jnp.stack([other, kept]))


def pack(shards):
    c = min(s.shape[1] for s in shards)
    return jnp.concatenate(
        [s[:, at : at + c] for s in shards for at in range(0, s.shape[1], c)], axis=0
    )


def unpack(block, shapes):
    c = block.shape[-1]
    found, at = [], 0
    for rows, cols in shapes:
        parts = []
        for _ in range(cols // c):
            parts.append(block[..., at : at + rows, :])
            at += rows
        found.append(jnp.concatenate(parts, axis=-1) if len(parts) > 1 else parts[0])
    return found


def exchanged(block, mask):
    both = ("batch", "blk")
    places = range(lax.axis_size("batch") * lax.axis_size("blk"))
    return lax.ppermute(block, both, [(i, i ^ mask) for i in places])


def xor_gather(block, stages):
    found, masks = block[None], [0]
    for stage in stages:
        parts = [found] + [exchanged(found, mask) for mask in stage]
        masks = masks + [held ^ mask for mask in stage for held in masks]
        found = jnp.concatenate(parts, 0)
    return found, masks


def xor_masks(stages):
    masks = [0]
    for stage in stages:
        masks = [held ^ mask for held in masks for mask in [0] + stage]
    return masks


def xor_sum(groups, stages, meanwhile):
    for at, stage in enumerate(stages):
        parts = [groups[0]] + [exchanged(g, mask) for mask, g in zip(stage, groups[1:])]
        if at == len(stages) - 1:
            return [part[0] for part in parts]
        events = meanwhile if at == len(stages) - 2 else ()
        groups = add_blocks(parts, len(stages[at + 1]) + 1, events)


class Weights:
    def __init__(self, shards, by_pairs, events=()):
        self.shapes = [s.shape for s in shards]
        self.m, self.n = lax.axis_size("batch"), lax.axis_size("blk")
        m, n = self.m, self.n
        r, c = min(s[0] for s in self.shapes), min(s[1] for s in self.shapes)
        self.fits = r % 16 == 0 and c % 128 == 0
        powers = m & (m - 1) == 0 and n == 2 and m >= 8
        self.by_pairs = by_pairs and self.fits and powers
        self.local = powers and self.fits
        every = list(range(len(shards)))
        if self.by_pairs:
            y, core, x = list(range(1, n)), [n], [2 * n]
            z = list(range(4 * n, m * n, 4 * n))
            own = pack_after(shards, ())
            found, masks = xor_gather(own, [z, x])
            self.found, self.masks, self.far = found, masks, [y[0], y[0] ^ core[0]]
            self.every, self.shape = every, (r, c)
            self.near = self.half([found, exchanged(found, core[0])], [0, core[0]])
            self.stages = [core, [a ^ b for a in [0] + x for b in [0] + y][1:], z]
            self.sums_of = Pieces((r, c), (m, n), [(xor_masks(self.stages), every)])
            return
        packed = pack_after(shards, events) if self.fits else pack(shards)
        packed = lax.all_gather(packed, ("batch", "blk"), axis=0)
        if self.fits:
            turned = (0,) if self.local else ()
            self.grid_of = Pieces((r, c), (m, n), [(None, every)], turned)
            self.packed = [packed]
        else:
            self.grid_of = Pieces((r * m, c * n), (1, 1), [(None, every)])
            whole = []
            for part in unpack(packed, self.shapes):
                rows, cols = part.shape[1:]
                part = part.reshape(m, n, rows, cols).transpose(0, 2, 1, 3)
                whole.append(part.reshape(m * rows, n * cols))
            self.packed = [pack(whole)[None]]
        self.sums_of = self.grid_of

    def half(self, blocks, steps):
        bundles = [([mask ^ step for mask in self.masks], self.every) for step in steps]
        return blocks, Pieces(self.shape, (self.m, self.n), bundles)

    def other_half(self, found):
        return self.half([exchanged(found, step) for step in self.far], self.far)

    def scatter(self, sums, meanwhile=()):
        extra = 16
        if self.by_pairs:
            return finish_sums(xor_sum(sums, self.stages, meanwhile), self.shapes)
        (sums,) = sums
        if not self.fits:
            rows = sums.shape[1] - extra
            wide = [(a * self.m, b * self.n) for a, b in self.shapes]
            parts = []
            for part in unpack(sums[0, :rows], wide):
                a, b = part.shape[0] // self.m, part.shape[1] // self.n
                part = part.reshape(self.m, a, self.n, b).transpose(0, 2, 1, 3)
                parts.append(part.reshape(self.m * self.n, a, b))
            c = min(s[1] for s in self.shapes)
            blocks = jnp.stack([pack([p[d] for p in parts]) for d in range(self.m * self.n)])
            vecs = sums[0, rows:].reshape(extra, self.n, c).transpose(1, 0, 2)
            vecs = jnp.broadcast_to(vecs[None], (self.m, self.n, extra, c))
            sums = jnp.concatenate([blocks, vecs.reshape(self.m * self.n, extra, c)], axis=1)
        height, c = sums.shape[1:]
        own = lax.psum_scatter(
            sums.reshape(-1, c), ("batch", "blk"), scatter_dimension=0, tiled=True
        )
        return finish_sums([own], self.shapes)


def finish_kernel(*refs, count):
    parts, outs = refs[:count], refs[count:]
    at = 0
    for out in outs:
        rows, cols = out.shape
        c = parts[0].shape[1]
        for start in range(0, cols, c):
            here = slice(at, at + rows)
            out[:, start : start + c] = sum(part[here, :].astype(F32) for part in parts)
            at += rows


def finish_sums(parts, shapes):
    height, c = parts[0].shape
    used = sum(a * b for a, b in shapes) // c
    shapes = list(shapes) + [(height - used, c)]
    if used % 16:
        total = sum(part.astype(F32) for part in parts)
        return [*unpack(total[:used], shapes[:-1]), total[used:]]
    return pl.pallas_call(
        functools.partial(finish_kernel, count=len(parts)),
        out_shape=tuple(jax.ShapeDtypeStruct(shape, F32) for shape in shapes),
        compiler_params=pltpu.CompilerParams(vmem_limit_bytes=60 * 2**20),
        name="finish_sums",
    )(*parts)


def on_device(
    hidden_in,
    lengths,
    cot_out,
    cot_cls,
    w_query,
    w_key,
    w_value,
    w_out,
    w_inner,
    w_outer,
    b_query,
    b_value,
    b_out,
    norm1_gain,
    norm1_shift,
    b_inner,
    b_outer,
    norm2_gain,
    norm2_shift,
):
    plan = Regroup()
    groups, block_len, width = hidden_in.shape
    span = groups * block_len
    per = plan.per
    fleets = [[i * per + j for j in range(per)] for i in range(2)]
    first_row = plan.passage * block_len
    owner = lax.rem(plan.me, per) == 0

    length = lax.dynamic_index_in_dim(lengths, plan.passage, 0, keepdims=False)
    info = jnp.stack(
        [
            length,
            first_row,
            plan.kept_index(),
            plan.kept_index(),
            jnp.where(owner, first_row, -1),
            lax.axis_index("batch"),
            plan.me,
        ]
    ).astype(jnp.int32)

    share = width // plan.n
    narrow = jnp.stack(
        [b_query, b_value, b_out, norm1_gain, norm1_shift, b_outer, norm2_gain, norm2_shift]
    )
    vec_shard = jnp.concatenate([narrow, b_inner.reshape(-1, share)], 0)
    vec_all = plan.all_blocks(vec_shard)
    narrow = vec_all[:, :8].transpose(1, 0, 2).reshape(8, width).astype(F32)
    bias_inner = vec_all[:, 8:].reshape(1, -1).astype(F32)

    def head_bias(query, value):
        return jnp.concatenate([query, jnp.zeros_like(query), value])[None].astype(F32)

    pairs = HEADS // 2
    hidden = plan.gather(hidden_in, plan.pick(hidden_in))
    heads = Weights([w_query, w_key, w_value], True)
    dense = Weights([w_out, w_inner, w_outer], False)
    if heads.by_pairs:
        far = jnp.where(plan.me == 0, vec_all[1], vec_all[0])
        biases = [head_bias(b_query, b_value), head_bias(far[0], far[1])]
        packed, grid_of = heads.near
    else:
        biases = [head_bias(narrow[0], narrow[1])]
        packed, grid_of = heads.packed, heads.grid_of
    groups = len(biases)
    each = pairs // groups
    at = lambda kind: lambda j: (j // each) * 3 * each + kind * each + j % each
    found, result = None, None
    for group in range(groups):
        last = group == groups - 1
        carried = None
        if not last:
            carried = heads.found
        elif plan.stays:
            carried = cot_out
        found = queries_keys_values(
            info, *hidden, packed, grid_of, biases[group], group, found, carried
        )
        if last:
            cots = plan.gather(cot_out, found[4] if plan.stays else plan.pick(cot_out))
        else:
            packed, grid_of = heads.other_half(found[4])
        found = found[:4]
        qkv, *mats = found
        if per == 1:
            sources = [(qkv, at(kind)) for kind in range(3)]
        else:
            kv = lax.all_gather(
                qkv[:, width:], "blk", axis=0, tiled=True, axis_index_groups=fleets
            )
            sources = [(qkv, at(0)), (kv, at(0)), (kv, at(1))]
        result = attend(info, sources, span, group * each, each, result)
    context_low, probs, sums = result

    own_cls = lax.dynamic_index_in_dim(cot_cls, plan.passage, 0, keepdims=True).astype(F32)
    layer_kept, layer_other, top, grad_context, grad_resid, dense_sums = middle(
        info, hidden, cots, context_low, own_cls, dense, narrow[2:], bias_inner
    )
    part_wo, part_wi, part_wu, dense_vecs = dense.scatter([dense_sums])
    part_bo, part_g1, part_s1, part_bu, part_g2, part_s2 = [dense_vecs[t] for t in range(6)]
    part_bi = dense_vecs[6 : 6 + b_inner.size // share].reshape(-1)
    layer_other = plan.send_back(layer_other)
    tops = plan.all_blocks(top)[::per, 0, :]
    cls_part = lax.dynamic_slice_in_dim(tops, plan.me * share, share, 1)

    back = functools.partial(
        attend_back, info, sources, grad_context, context_low, sums, probs, span
    )
    give = functools.partial(input_grad, info, resid=grad_resid, mats=mats)
    if per == 1:
        most = back([(1, 1), (1, 0), (0, 1)], None)
        other, *layer_rows = give(
            most,
            out_shape=(block_len, width),
            dtype=BF16,
            kept=False,
            join=(layer_kept, layer_other) if plan.stays else (),
            events=(cls_part,),
        )
        layer_rows = layer_rows[0] if layer_rows else plan.join(info, layer_kept, layer_other)
        rest = back([(0, 0)], most, (other, layer_rows))
        other = plan.send_back(other)
    else:
        blocks = span * per // min(1024, span * per)
        grad_q, *grad_kv = back([(k, q) for k in range(blocks) for q in range(2)], None)
        most = [grad_q] + [
            lax.psum_scatter(g, "blk", scatter_dimension=0, tiled=True, axis_index_groups=fleets)
            for g in grad_kv
        ]
        (other,) = give(most, out_shape=(block_len, width), dtype=BF16, kept=False)
        other = plan.send_back(other)
        rest = most
        layer_rows = plan.join(info, layer_kept, layer_other)
    head_sums = head_grads(
        info, hidden, rest, heads.sums_of, 2 if heads.by_pairs else 1, (other,)
    )
    (kept,) = give(rest, out_shape=hidden[0].shape, dtype=F32, kept=True)
    grad_input = plan.join(info, kept, other)
    part_wq, part_wk, part_wv, head_vecs = heads.scatter(
        head_sums, (grad_input, part_wo, dense_vecs)
    )
    part_bq, part_bv = head_vecs[0], head_vecs[1]
    return (
        layer_rows,
        cls_part,
        grad_input,
        part_wq,
        part_wk,
        part_wv,
        part_wo,
        part_wi,
        part_wu,
        part_bq,
        part_bv,
        part_bo,
        part_g1,
        part_s1,
        part_bi,
        part_bu,
        part_g2,
        part_s2,
    )


def solution(mesh):
    rows = P("batch", "blk", None)
    mats = (P("batch", "blk"),) * 6
    vecs = (P("blk"),) * 9
    return jax.shard_map(
        on_device,
        mesh=mesh,
        in_specs=(rows, P("batch"), rows, P("batch", None)) + mats + vecs,
        out_specs=(rows, P("batch", "blk"), rows) + mats + vecs,
        check_vma=False,
    )
```

```python
import functools

import jax
import jax.numpy as jnp
from jax import lax
from jax.experimental import pallas as pl
from jax.experimental.pallas import tpu as pltpu
from jax.sharding import PartitionSpec as P

HEADS = 12
HDIM = 64
PAIR = 2 * HDIM
LOG2E = 1.4426950408889634
BF16 = jnp.bfloat16
F32 = jnp.float32


def live_rows(shape, axis, start, length, shift, span):
    rows = shape[axis]
    step = min(rows, span)
    parts = []
    for at in range(0, rows, step):
        first = start + at
        base = (first // span) * span
        sizes = list(shape)
        sizes[axis] = step
        turned = lax.broadcasted_iota(jnp.int32, tuple(sizes), axis) + (first - base + shift)
        turned = jnp.where(turned >= span, turned - span, turned)
        parts.append(turned < length - base)
    return parts[0] if len(parts) == 1 else jnp.concatenate(parts, axis)


def chunk_of(rows):
    return min(1024, rows // 2)


def segments(rows, size):
    for at in range(0, rows, size):
        for h in range(2):
            yield h, slice(at, at + size), slice(2 * at + h * size, 2 * at + (h + 1) * size)


def beside(part, h):
    blank = jnp.zeros_like(part)
    return jnp.concatenate([part, blank] if h == 0 else [blank, part], 0)


def head_rows(h):
    return slice(h * HDIM, (h + 1) * HDIM)


def attend_kernel(
    info,
    q_ref,
    k_ref,
    v_ref,
    out_ref,
    p_ref,
    sum_ref,
    keys,
    vals,
    ques,
    bound,
    turned,
    *,
    chunk,
    across,
    span,
):
    pos = pl.program_id(1)
    kv = k_ref.shape[0]
    size, width = out_ref.shape[0], p_ref.shape[2]
    factor = HDIM**-0.5 * LOG2E

    @pl.when(pos == 0)
    def prepare():
        live = live_rows((kv, PAIR), 0, 0, info[0], info[1], span)
        kept = jnp.where(live, k_ref[...], jnp.zeros((), BF16))
        keys[...] = kept
        vals[0:PAIR, :] = jnp.where(live, v_ref[...], jnp.zeros((), BF16)).T
        vals[PAIR:, :] = live_rows((16, kv), 1, 0, info[0], info[1], span).astype(BF16)
        turned_q = q_ref[...].T
        squares = kept.astype(F32)
        squares = (squares * squares).astype(BF16)
        half = lambda axis: lax.broadcasted_iota(jnp.int32, (PAIR, PAIR), axis) // HDIM
        sizes = jnp.dot(squares, (half(0) == half(1)).astype(BF16), preferred_element_type=F32)
        largest = jnp.max(sizes, axis=0, keepdims=True)
        tops = [jnp.max(largest[:, head_rows(h)], axis=1, keepdims=True) for h in range(2)]
        for h, queries, cols in segments(q_ref.shape[0], size):
            mine = turned_q[head_rows(h), queries]
            ques[:, cols] = beside(mine, h)
            sharp = mine.astype(F32)
            reach = jnp.sum(sharp * sharp, axis=0, keepdims=True)
            bound[:, cols] = jnp.sqrt(reach * tops[h] * 1.03) * factor

    cols = pl.ds(pl.multiple_of(pos * width, width), width)

    def weigh(peak):
        for start in range(0, width, across):
            own = slice(start, start + across)
            query = ques[:, pl.ds(pl.multiple_of(pos * width + start, across), across)]
            for at in range(0, kv, chunk):
                rows = slice(at, at + chunk)
                scores = jnp.dot(keys[rows, :], query, preferred_element_type=F32)
                p_ref[0, rows, own] = jnp.exp2(scores * factor - peak[:, own]).astype(BF16)
        total = jnp.dot(vals[...], p_ref[0], preferred_element_type=F32)
        sums = total[PAIR : PAIR + 1, :]
        sum_ref[0] = sums
        for h in range(2):
            own = slice(h * size, (h + 1) * size)
            turned[head_rows(h), :] = total[head_rows(h), own] / sums[:, own]
        return jnp.min(sums)

    def exact_peak():
        query = ques[:, cols]

        def largest(at, peak):
            rows = pl.ds(pl.multiple_of(at * chunk, chunk), chunk)
            scores = jnp.dot(keys[rows, :], query, preferred_element_type=F32)
            live = live_rows((chunk, width), 0, at * chunk, info[0], info[1], span)
            return jnp.maximum(peak, jnp.max(jnp.where(live, scores, -1e30), axis=0, keepdims=True))

        return lax.fori_loop(0, kv // chunk, largest, jnp.full((1, width), -1e30, F32)) * factor

    lowest = weigh(bound[:, cols])

    @pl.when(jnp.logical_not(lowest > 2.0**-70))
    def again():
        weigh(exact_peak())

    out_ref[...] = turned[...].T.astype(BF16)


def attend(info, sources, span):
    (queries, q_at), (keys, k_at), (values, v_at) = sources
    rows, kv = queries.shape[0], keys.shape[0]
    size = chunk_of(rows)
    pairs = HEADS // 2
    return pl.pallas_call(
        functools.partial(
            attend_kernel, chunk=min(256, kv), across=min(256, 2 * size), span=span
        ),
        out_shape=(
            jax.ShapeDtypeStruct((rows, HEADS * HDIM), BF16),
            jax.ShapeDtypeStruct((pairs, kv, 2 * rows), BF16),
            jax.ShapeDtypeStruct((pairs, 1, 2 * rows), F32),
        ),
        grid_spec=pltpu.PrefetchScalarGridSpec(
            num_scalar_prefetch=1,
            grid=(pairs, rows // size),
            in_specs=[
                pl.BlockSpec((rows, PAIR), lambda j, c, s: (0, q_at(j))),
                pl.BlockSpec((kv, PAIR), lambda j, c, s: (0, k_at(j))),
                pl.BlockSpec((kv, PAIR), lambda j, c, s: (0, v_at(j))),
            ],
            out_specs=(
                pl.BlockSpec((size, PAIR), lambda j, c, s: (c, j)),
                pl.BlockSpec((1, kv, 2 * size), lambda j, c, s: (j, 0, c)),
                pl.BlockSpec((1, 1, 2 * size), lambda j, c, s: (j, 0, c)),
            ),
            scratch_shapes=[
                pltpu.VMEM((kv, PAIR), BF16),
                pltpu.VMEM((PAIR + 16, kv), BF16),
                pltpu.VMEM((PAIR, 2 * rows), BF16),
                pltpu.VMEM((1, 2 * rows), F32),
                pltpu.VMEM((PAIR, size), F32),
            ],
        ),
        compiler_params=pltpu.CompilerParams(vmem_limit_bytes=60 * 2**20),
        name="attend",
    )(info, queries, keys, values)


def attend_back_kernel(
    info,
    units,
    q_ref,
    k_ref,
    v_ref,
    g_ref,
    ctx_ref,
    sum_ref,
    p_ref,
    *rest,
    chunk,
    size,
    span,
    more,
    extra,
):
    before, rest = (rest[:3], rest[3:]) if more else (None, rest)
    rest = rest[extra:]
    gq_ref, gk_ref, gv_ref, keys, grads, grads_up, ques_up, delta, low, total, key_sum, value_sum = rest
    step = pl.program_id(1)
    kv, rows = k_ref.shape[0], q_ref.shape[0]
    block, part = p_ref.shape[1:]
    scale = HDIM**-0.5

    @pl.when(step == 0)
    def prepare():
        live = live_rows((kv, PAIR), 0, 0, info[0], info[1], span)
        keys[...] = jnp.where(live, k_ref[...], jnp.zeros((), BF16)).T
        turned = g_ref[...].T.astype(F32)
        dots = turned * ctx_ref[...].T.astype(F32)
        for h, queries, cols in segments(rows, size):
            inverse = 1.0 / sum_ref[0, :, cols]
            own = head_rows(h)
            delta[:, cols] = jnp.sum(dots[own, queries], axis=0, keepdims=True) * inverse
            shared = beside((turned[own, queries] * inverse).astype(BF16), h)
            grads[:, cols] = shared
            grads_up[cols, :] = shared.T
            lane = lax.broadcasted_iota(jnp.int32, (queries.stop - queries.start, PAIR), 1)
            ques_up[cols, :] = jnp.where(lane // HDIM == h, q_ref[queries, :], jnp.zeros((), BF16))
        for held in (total, key_sum, value_sum):
            held[...] = jnp.zeros_like(held)

    here = pl.ds(pl.multiple_of(units[0, step] * block, block), block)
    there = pl.multiple_of(units[1, step] * part, part)
    cols = pl.ds(there, part)
    values = v_ref[here, :]
    for start in range(0, part, chunk):
        own = slice(start, start + chunk)
        from_all = pl.ds(there + start, chunk)
        change = jnp.dot(values, grads[:, from_all], preferred_element_type=F32)
        low[:, own] = (p_ref[0, :, own].astype(F32) * (change - delta[:, from_all])).astype(BF16)
    value_sum[here, :] += jnp.dot(p_ref[0], grads_up[cols, :], preferred_element_type=F32)
    key_sum[here, :] += jnp.dot(low[...], ques_up[cols, :], preferred_element_type=F32)
    total[:, cols] += jnp.dot(keys[:, here], low[...], preferred_element_type=F32)

    @pl.when(step == pl.num_programs(1) - 1)
    def finish():
        live = live_rows((kv, PAIR), 0, 0, info[0], info[1], span)
        zero = jnp.zeros((), F32)
        found = [jnp.where(live, key_sum[...] * scale, zero), jnp.where(live, value_sum[...], zero)]
        for t, (ref, value) in enumerate(zip((gk_ref, gv_ref), found)):
            if more:
                value += before[t + 1][...].astype(F32)
            ref[...] = value.astype(BF16)
        parts = [[], []]
        for h, queries, cols in segments(rows, size):
            parts[h].append(total[head_rows(h), cols])
        value = (jnp.concatenate([jnp.concatenate(p, 1) for p in parts], 0) * scale).T
        if more:
            value += before[0][...].astype(F32)
        gq_ref[...] = value.astype(BF16)


def attend_back(info, sources, grad, context, sums, probs, span, units, before, events=()):
    (queries, q_at), (keys, k_at), (values, v_at) = sources
    rows, kv = queries.shape[0], keys.shape[0]
    pairs = HEADS // 2
    wide = HEADS * HDIM
    more = before is not None
    block, part, size = min(1024, kv), rows, chunk_of(rows)
    cut = 2 if more else 1
    rows, kv = rows // cut, kv // cut
    out_rows = [rows, kv, kv]
    heights = [rows * cut, kv * cut, kv * cut]
    units = jnp.array(list(zip(*units)), jnp.int32)
    col = lambda height, at=lambda j: j: pl.BlockSpec(
        (height, PAIR), lambda j, c, s, u: (0, at(j))
    )
    return pl.pallas_call(
        functools.partial(
            attend_back_kernel,
            chunk=min(512, part),
            size=size,
            span=span,
            more=more,
            extra=len(events),
        ),
        out_shape=tuple(jax.ShapeDtypeStruct((height, wide), BF16) for height in heights),
        grid_spec=pltpu.PrefetchScalarGridSpec(
            num_scalar_prefetch=2,
            grid=(pairs, units.shape[1]),
            in_specs=[
                col(rows, q_at),
                col(kv, k_at),
                col(kv, v_at),
                col(rows),
                col(rows),
                pl.BlockSpec((1, 1, 2 * rows), lambda j, c, s, u: (j, 0, 0)),
                pl.BlockSpec((1, block, part), lambda j, c, s, u: (j, u[0, c], u[1, c])),
            ]
            + ([col(height) for height in out_rows] if more else [])
            + any_specs(events),
            out_specs=tuple(col(height) for height in out_rows),
            scratch_shapes=[
                pltpu.VMEM((PAIR, kv), BF16),
                pltpu.VMEM((PAIR, 2 * rows), BF16),
                pltpu.VMEM((2 * rows, PAIR), BF16),
                pltpu.VMEM((2 * rows, PAIR), BF16),
                pltpu.VMEM((1, 2 * rows), F32),
                pltpu.VMEM((block, part), BF16),
                pltpu.VMEM((PAIR, 2 * rows), F32),
                pltpu.VMEM((kv, PAIR), F32),
                pltpu.VMEM((kv, PAIR), F32),
            ],
        ),
        input_output_aliases={9 + t: t for t in range(3)} if more else {},
        compiler_params=pltpu.CompilerParams(vmem_limit_bytes=60 * 2**20),
        name="attend_back_last" if more else "attend_back",
    )(info, units, queries, keys, values, grad, context, sums, probs, *(before or ()), *events)


def rows_of(kept_ref, other_ref, step, split):
    return jnp.where(step < split, kept_ref[0], other_ref[...])


def project(rows, weight):
    return jnp.dot(rows, weight, preferred_element_type=F32)


def project_back(grads, weight):
    return lax.dot_general(grads, weight, (((1,), (1,)), ((), ())), preferred_element_type=F32)


def weight_grad(rows, grads):
    return lax.dot_general(rows, grads, (((0,), (0,)), ((), ())), preferred_element_type=F32)


def run_all(copies):
    for copy in copies:
        copy.start()
    return copies


def wait_all(copies):
    for copy in copies:
        copy.wait()


class Pieces:
    def __init__(self, shape, mesh_shape, bundles):
        self.r, self.c = shape
        self.m, self.n = mesh_shape
        self.bundles = bundles
        self.slots = self.m * self.n

    def place(self, masks, slot, info):
        if masks is None:
            return slot // self.n, lax.rem(slot, self.n)
        return info[5] ^ (masks[slot] // self.n), info[6] ^ (masks[slot] % self.n)

    def copies(self, refs, mats, sems, info, out):
        found = [[] for _ in mats]
        r, c = self.r, self.c
        count = 0
        for (masks, members), ref in zip(self.bundles, refs):
            for slot in range(self.slots if masks is None else len(masks)):
                j, i = self.place(masks, slot, info)
                at = 0
                for t in members:
                    mat = mats[t]
                    tall = mat.shape[0] // (self.m * r)
                    wide = mat.shape[1] // (self.n * c)
                    for w in range(wide):
                        if isinstance(ref, (tuple, list)):
                            each = self.slots // len(ref)
                            block = ref[slot // each].at[slot % each, pl.ds(at, tall * r), :]
                        else:
                            block = ref.at[slot, pl.ds(at, tall * r), :]
                        down = pl.multiple_of(j * (tall * r), tall * r)
                        side = pl.multiple_of((i * wide + w) * c, c)
                        place = mat.at[pl.ds(down, tall * r), pl.ds(side, c)]
                        at += tall * r
                        pair = (place, block) if out else (block, place)
                        found[t].append(pltpu.make_async_copy(*pair, sems.at[count]))
                        count += 1
        return found

    def count(self):
        return 9 * self.slots


def any_specs(arrays):
    return [pl.BlockSpec(memory_space=pl.ANY)] * len(arrays)


def queries_kernel(info, kept_ref, other_ref, bias_ref, *rest, split, grid_of, carry):
    count = len(grid_of.bundles)
    packed, rest = rest[:count], rest[count:]
    step = pl.program_id(0)
    if carry:
        pair_ref, out_ref, mat_q, mat_k, mat_v, picked, sems = rest
        picked[...] = pair_ref[0]
    else:
        out_ref, mat_q, mat_k, mat_v, sems = rest
    mats = [mat_q, mat_k, mat_v]

    @pl.when(step == 0)
    def load():
        loads = grid_of.copies(packed, mats, sems, info, False)
        for group in loads:
            run_all(group)
        for group in loads:
            wait_all(group)

    rows = rows_of(kept_ref, other_ref, step, split)
    width = mat_q.shape[1]
    for t, mat in enumerate(mats):
        cols = slice(t * width, (t + 1) * width)
        out_ref[:, cols] = (project(rows, mat[...]) + bias_ref[:, cols]).astype(BF16)


def split_specs(kept_at, tile, split, width):
    return [
        pl.BlockSpec((1, tile, width), lambda i, s: (s[kept_at], jnp.minimum(i, split - 1), 0)),
        pl.BlockSpec((tile, width), lambda i, s: (jnp.maximum(i - split, 0), 0)),
    ]


def whole_spec(shape):
    return pl.BlockSpec(shape, lambda i, s: (0,) * len(shape))


def queries_keys_values(info, kept, other, weights, bias, pair):
    block_len, width = other.shape
    tile = min(512, block_len)
    split = block_len // tile
    part = block_len // (2 * split)
    carried = [] if pair is None else [pair]
    mat = jax.ShapeDtypeStruct((width, width), BF16)
    return pl.pallas_call(
        functools.partial(
            queries_kernel, split=split, grid_of=weights.grid_of, carry=bool(carried)
        ),
        out_shape=(jax.ShapeDtypeStruct((2 * block_len, 3 * width), BF16), mat, mat, mat)
        + (jax.ShapeDtypeStruct((block_len, width), BF16),) * len(carried),
        grid_spec=pltpu.PrefetchScalarGridSpec(
            num_scalar_prefetch=1,
            grid=(2 * split,),
            in_specs=split_specs(2, tile, split, width)
            + [whole_spec(bias.shape)]
            + any_specs(weights.packed)
            + [pl.BlockSpec((1, part, width), lambda i, s: (1 - s[2], i, 0))] * len(carried),
            out_specs=(pl.BlockSpec((tile, 3 * width), lambda i, s: (i, 0)),)
            + (whole_spec(mat.shape),) * 3
            + (pl.BlockSpec((part, width), lambda i, s: (i, 0)),) * len(carried),
            scratch_shapes=[pltpu.SemaphoreType.DMA((weights.grid_of.count(),))],
        ),
        compiler_params=pltpu.CompilerParams(vmem_limit_bytes=60 * 2**20),
        name="queries",
    )(info, kept, other, bias, *weights.packed, *carried)


def normal(values):
    middle = jnp.mean(values, axis=-1, keepdims=True)
    centered = values - middle
    spread = jnp.mean(centered * centered, axis=-1, keepdims=True)
    inverse = lax.rsqrt(spread + 1e-12)
    return centered * inverse, inverse


def normal_back(grad, unit, inverse, gain):
    scaled = grad * gain
    mean = jnp.mean(scaled, axis=-1, keepdims=True)
    along = jnp.mean(scaled * unit, axis=-1, keepdims=True)
    return (scaled - mean - unit * along) * inverse


def gelu_pair(u):
    phi = 0.5 + 0.5 * lax.erf(0.7071067811865476 * u)
    bell = jnp.exp2((-0.5 * LOG2E) * (u * u))
    return u * phi, phi + (0.3989422804014327 * u) * bell


def add_rows(total, at, values):
    total[at : at + 1, 0 : values.shape[1]] += jnp.sum(values, axis=0, keepdims=True)


def middle_kernel(
    info,
    hid_kept,
    hid_other,
    cot_kept,
    cot_other,
    ctx_ref,
    cls_ref,
    vec_ref,
    inner_bias,
    packed,
    layer_kept,
    layer_other,
    top_ref,
    grad_ctx_ref,
    resid_ref,
    sums_ref,
    mat_out,
    mat_inner,
    mat_outer,
    acc_out,
    acc_inner,
    acc_outer,
    totals,
    active,
    slope,
    low,
    vec_low,
    sems,
    vec_sems,
    *,
    split,
    grid_of,
    chunk,
):
    step = pl.program_id(0)
    last = pl.num_programs(0) - 1
    mats = [mat_out, mat_inner, mat_outer]
    tile, width = ctx_ref.shape
    ff = mat_inner.shape[1]
    loads = grid_of.copies([packed], mats, sems, info, False)

    @pl.when(step == 0)
    def start():
        for group in loads:
            run_all(group)
        for acc in (acc_out, acc_inner, acc_outer, totals):
            acc[...] = jnp.zeros_like(acc)
        wait_all(loads[0])

    bias_out, gain_one, shift_one, bias_outer, gain_two, shift_two = [
        vec_ref[t : t + 1, :] for t in range(6)
    ]
    hidden = rows_of(hid_kept, hid_other, step, split).astype(F32)
    context = ctx_ref[...]
    unit_one, inverse_one = normal(hidden + project(context, mat_out[...]) + bias_out)
    normed = unit_one * gain_one + shift_one
    normed_low = normed.astype(BF16)

    @pl.when(step == 0)
    def more():
        wait_all(loads[1])
        wait_all(loads[2])

    for at in range(0, ff, chunk):
        cols = slice(at, at + chunk)
        inner = project(normed_low, mat_inner[:, cols]) + inner_bias[:, cols]
        value, change = gelu_pair(inner)
        active[:, cols] = value.astype(BF16)
        slope[:, cols] = change.astype(BF16)
    unit_two, inverse_two = normal(normed + project(active[...], mat_outer[...]) + bias_outer)
    layer = (unit_two * gain_two + shift_two).astype(BF16)

    @pl.when(step < split)
    def kept():
        layer_kept[0] = layer

    @pl.when(step >= split)
    def other():
        layer_other[...] = layer

    @pl.when(step * tile == info[1])
    def top():
        top_ref[...] = layer[0:16, :]


    row = step * tile + lax.broadcasted_iota(jnp.int32, (tile, width), 0)
    grad_result = rows_of(cot_kept, cot_other, step, split).astype(F32)
    grad_result += jnp.where(row == info[4], cls_ref[...], 0.0)
    add_rows(totals, 4, grad_result * unit_two)
    add_rows(totals, 5, grad_result)
    grad_resid_two = normal_back(grad_result, unit_two, inverse_two, gain_two)
    grad_outer = grad_resid_two.astype(BF16)
    add_rows(totals, 3, grad_outer.astype(F32))
    for at in range(0, ff, chunk):
        cols = slice(at, at + chunk)
        grad_inner = project_back(grad_outer, mat_outer[cols, :]) * slope[:, cols].astype(F32)
        low[:, cols] = grad_inner.astype(BF16)
        totals[8:9, cols] += jnp.sum(grad_inner, axis=0, keepdims=True)
        acc_outer[cols, :] += weight_grad(active[:, cols], grad_outer)
    grad_normed = grad_resid_two + project_back(low[...], mat_inner[...])
    for at in range(0, ff, chunk):
        cols = slice(at, at + chunk)
        acc_inner[:, cols] += weight_grad(normed_low, low[:, cols])
    add_rows(totals, 1, grad_normed * unit_one)
    add_rows(totals, 2, grad_normed)
    grad_resid_one = normal_back(grad_normed, unit_one, inverse_one, gain_one)
    resid_ref[...] = grad_resid_one
    grad_attn = grad_resid_one.astype(BF16)
    add_rows(totals, 0, grad_attn.astype(F32))
    acc_out[...] += weight_grad(context, grad_attn)
    grad_ctx_ref[...] = project_back(grad_attn, mat_out[...]).astype(BF16)

    @pl.when(step == last)
    def finish():
        r, c, m, n = grid_of.r, grid_of.c, grid_of.m, grid_of.n
        stores = grid_of.copies([sums_ref], mats, sems, info, True)
        for mat, acc, group in zip(mats, (acc_out, acc_inner, acc_outer), stores):
            mat[...] = acc[...].astype(BF16)
            run_all(group)
        vec_low[...] = jnp.zeros_like(vec_low)
        for i in range(n):
            for t in range(6):
                vec_low[i, t : t + 1, :] = totals[t : t + 1, i * c : (i + 1) * c]
            wide = ff // (n * c)
            for t in range(wide):
                at = (i * wide + t) * c
                vec_low[i, 6 + t : 7 + t, :] = totals[8:9, at : at + c]
        tails = []
        vec_bits = vec_low[...].astype(BF16)
        for i in range(n):
            active[16 * i : 16 * i + 16, 0:c] = vec_bits[i]
        for j in range(m):
            for i in range(n):
                tails.append(
                    pltpu.make_async_copy(
                        active.at[pl.ds(16 * i, 16), pl.ds(0, c)],
                        sums_ref.at[j * n + i, pl.ds(9 * r, 16), :],
                        vec_sems.at[j * n + i],
                    )
                )
        run_all(tails)
        for group in stores:
            wait_all(group)
        wait_all(tails)


def kept_spec(tile, split, width):
    return pl.BlockSpec((1, tile, width), lambda i, s: (s[2], jnp.minimum(i, split - 1), 0))


def other_spec(tile, split, width):
    return pl.BlockSpec((tile, width), lambda i, s: (jnp.maximum(i - split, 0), 0))


def middle(info, hidden, cots, context, cls_row, weights, vectors, inner_bias):
    block_len, width = hidden[1].shape
    grid_of = weights.grid_of
    ff = inner_bias.shape[1]
    tile = min(256, block_len)
    split = block_len // tile
    row_spec = pl.BlockSpec((tile, width), lambda i, s: (i, 0))
    return pl.pallas_call(
        functools.partial(middle_kernel, split=split, grid_of=grid_of, chunk=768),
        out_shape=(
            jax.ShapeDtypeStruct(hidden[0].shape, BF16),
            jax.ShapeDtypeStruct((block_len, width), BF16),
            jax.ShapeDtypeStruct((16, width), BF16),
            jax.ShapeDtypeStruct((2 * block_len, width), BF16),
            jax.ShapeDtypeStruct((2 * block_len, width), F32),
            jax.ShapeDtypeStruct((grid_of.slots, 9 * grid_of.r + 16, grid_of.c), BF16),
        ),
        grid_spec=pltpu.PrefetchScalarGridSpec(
            num_scalar_prefetch=1,
            grid=(2 * split,),
            in_specs=split_specs(2, tile, split, width)
            + split_specs(2, tile, split, width)
            + [
                row_spec,
                whole_spec(cls_row.shape),
                whole_spec(vectors.shape),
                whole_spec(inner_bias.shape),
                pl.BlockSpec(memory_space=pl.ANY),
            ],
            out_specs=(
                kept_spec(tile, split, width),
                other_spec(tile, split, width),
                whole_spec((16, width)),
                row_spec,
                row_spec,
                pl.BlockSpec(memory_space=pl.ANY),
            ),
            scratch_shapes=[
                pltpu.VMEM((width, width), BF16),
                pltpu.VMEM((width, ff), BF16),
                pltpu.VMEM((ff, width), BF16),
                pltpu.VMEM((width, width), F32),
                pltpu.VMEM((width, ff), F32),
                pltpu.VMEM((ff, width), F32),
                pltpu.VMEM((16, ff), F32),
                pltpu.VMEM((tile, ff), BF16),
                pltpu.VMEM((tile, ff), BF16),
                pltpu.VMEM((tile, ff), BF16),
                pltpu.VMEM((grid_of.n, 16, grid_of.c), F32),
                pltpu.SemaphoreType.DMA((grid_of.count(),)),
                pltpu.SemaphoreType.DMA((grid_of.slots,)),
            ],
        ),
        compiler_params=pltpu.CompilerParams(vmem_limit_bytes=60 * 2**20),
        name="middle",
    )(info, *hidden, *cots, context, cls_row, vectors, inner_bias, *weights.packed)


def input_grad_kernel(info, gq_ref, gk_ref, gv_ref, resid_ref, mat_q, mat_k, mat_v, *rest, kept, join):
    if join:
        arrived, grad_ref, joined = rest[0], rest[-2], rest[-1]
        joined[0] = arrived[...].astype(joined.dtype)
    else:
        grad_ref = rest[-1]
    total = resid_ref[...]
    for ref, mat in zip((gq_ref, gk_ref, gv_ref), (mat_q, mat_k, mat_v)):
        total += project_back(ref[...], mat[...])
    if kept:
        grad_ref[0] = total.astype(grad_ref.dtype)
    else:
        grad_ref[...] = total.astype(grad_ref.dtype)


def input_grad(info, grads, resid, mats, out_shape, dtype, kept, join=(), events=()):
    rows, width = resid.shape
    block_len = rows // 2
    tile = min(512, block_len)
    split = block_len // tile
    off = 0 if kept else split
    spec = pl.BlockSpec((tile, width), lambda i, s: (i + off, 0))
    place = kept_spec(tile, split, width) if kept else other_spec(tile, 0, width)
    out = (jax.ShapeDtypeStruct(out_shape, dtype),)
    in_specs = [spec] * 4 + [whole_spec(mat.shape) for mat in mats]
    out_specs = (place,)
    aliases = {}
    if join:
        in_specs += [pl.BlockSpec((tile, width), lambda i, s: (i, 0))] + any_specs(join[:1])
        out += (jax.ShapeDtypeStruct(join[0].shape, join[0].dtype),)
        out_specs += (pl.BlockSpec((1, tile, width), lambda i, s: (1 - s[2], i, 0)),)
        aliases = {len(in_specs): 1}
    return pl.pallas_call(
        functools.partial(input_grad_kernel, kept=kept, join=bool(join)),
        out_shape=out,
        grid_spec=pltpu.PrefetchScalarGridSpec(
            num_scalar_prefetch=1,
            grid=(split,),
            in_specs=in_specs + any_specs(events),
            out_specs=out_specs,
        ),
        input_output_aliases=aliases,
        compiler_params=pltpu.CompilerParams(vmem_limit_bytes=60 * 2**20),
        name="input_grad_kept" if kept else "input_grad_other",
    )(info, *grads, resid, *mats, *join[::-1], *events)


def head_grads_kernel(info, hid_kept, hid_other, *rest, split, grid_of, outs, extra):
    found, rest = rest[:3], rest[3 + extra :]
    sums, (acc, mat_q, mat_k, mat_v, totals, vec_low, sems, vec_sems) = rest[:outs], rest[outs:]
    mats = [mat_q, mat_k, mat_v]
    step = pl.program_id(0)

    @pl.when(step == 0)
    def clear():
        acc[...] = jnp.zeros_like(acc)
        totals[...] = jnp.zeros_like(totals)

    rows = rows_of(hid_kept, hid_other, step, split)
    grads = [ref[...] for ref in found]
    for t, grad in enumerate(grads):
        acc[t] += weight_grad(rows, grad)
    add_rows(totals, 0, grads[0].astype(F32))
    add_rows(totals, 1, grads[2].astype(F32))

    @pl.when(step == pl.num_programs(0) - 1)
    def finish():
        r, c, n = grid_of.r, grid_of.c, grid_of.n
        ((masks, _),) = grid_of.bundles
        stores = grid_of.copies([list(sums)], mats, sems, info, True)
        for t, mat in enumerate(mats):
            mat[...] = acc[t].astype(BF16)
            run_all(stores[t])
        for i in range(n):
            part = jnp.concatenate([totals[0:2, i * c : (i + 1) * c], jnp.zeros((14, c), F32)], 0)
            vec_low[i] = part.astype(BF16)
        tails = []
        each = grid_of.slots // outs
        for slot in range(grid_of.slots):
            j, i = grid_of.place(masks, slot, info)
            place = sums[slot // each].at[slot % each, pl.ds(3 * r, 16), :]
            tails.append(pltpu.make_async_copy(vec_low.at[i], place, vec_sems.at[slot]))
        run_all(tails)
        for group in stores:
            wait_all(group)
        wait_all(tails)


def head_grads(info, hidden, grads, grid_of, outs, events=()):
    block_len, width = hidden[1].shape
    tile = min(512, block_len)
    split = block_len // tile
    rows = pl.BlockSpec((tile, width), lambda i, s: (i, 0))
    block = (grid_of.slots // outs, 3 * grid_of.r + 16, grid_of.c)
    return pl.pallas_call(
        functools.partial(
            head_grads_kernel, split=split, grid_of=grid_of, outs=outs, extra=len(events)
        ),
        out_shape=(jax.ShapeDtypeStruct(block, BF16),) * outs,
        grid_spec=pltpu.PrefetchScalarGridSpec(
            num_scalar_prefetch=1,
            grid=(2 * split,),
            in_specs=split_specs(2, tile, split, width) + [rows] * 3 + any_specs(events),
            out_specs=(pl.BlockSpec(memory_space=pl.ANY),) * outs,
            scratch_shapes=[pltpu.VMEM((3, width, width), F32)]
            + [pltpu.VMEM((width, width), BF16)] * 3
            + [
                pltpu.VMEM((8, width), F32),
                pltpu.VMEM((grid_of.n, 16, grid_of.c), BF16),
                pltpu.SemaphoreType.DMA((grid_of.count(),)),
                pltpu.SemaphoreType.DMA((grid_of.slots,)),
            ],
        ),
        compiler_params=pltpu.CompilerParams(vmem_limit_bytes=60 * 2**20),
        name="head_grads",
    )(info, *hidden, *grads, *events)


def pick_kernel(info, pair_ref, *rest):
    rest[-1][...] = pair_ref[0]


def pick_other(info, pair, events):
    _, block_len, width = pair.shape
    tile = min(512, block_len)
    return pl.pallas_call(
        pick_kernel,
        out_shape=jax.ShapeDtypeStruct((block_len, width), pair.dtype),
        grid_spec=pltpu.PrefetchScalarGridSpec(
            num_scalar_prefetch=1,
            grid=(block_len // tile,),
            in_specs=[pl.BlockSpec((1, tile, width), lambda i, s: (1 - s[2], i, 0))]
            + any_specs(events),
            out_specs=pl.BlockSpec((tile, width), lambda i, s: (i, 0)),
        ),
        compiler_params=pltpu.CompilerParams(vmem_limit_bytes=60 * 2**20),
        name="pick_other",
    )(info, pair, *events)


def pack_kernel(*refs, count):
    out = refs[-1]
    c = out.shape[1]
    at = 0
    for ref in refs[:count]:
        rows, cols = ref.shape
        for start in range(0, cols, c):
            out[at : at + rows, :] = ref[:, start : start + c]
            at += rows


def pack_after(shards, events):
    c = min(s.shape[1] for s in shards)
    rows = sum(s.size for s in shards) // c
    return pl.pallas_call(
        functools.partial(pack_kernel, count=len(shards)),
        out_shape=jax.ShapeDtypeStruct((rows, c), BF16),
        in_specs=[pl.BlockSpec(memory_space=pltpu.VMEM)] * len(shards) + any_specs(events),
        compiler_params=pltpu.CompilerParams(vmem_limit_bytes=60 * 2**20),
        name="pack",
    )(*shards, *events)


def stack_kernel(*refs, count, outs):
    at = 0
    for out in refs[-outs:]:
        rows = out.shape[1]
        for k, ref in enumerate(refs[:count]):
            out[k] = ref[at : at + rows, :]
        at += rows


def stack_rows(blocks, cuts, events):
    c = blocks[0].shape[1]
    return pl.pallas_call(
        functools.partial(stack_kernel, count=len(blocks), outs=len(cuts)),
        out_shape=tuple(jax.ShapeDtypeStruct((len(blocks), rows, c), BF16) for rows in cuts),
        in_specs=[pl.BlockSpec(memory_space=pltpu.VMEM)] * len(blocks) + any_specs(events),
        compiler_params=pltpu.CompilerParams(vmem_limit_bytes=60 * 2**20),
        name="stack_rows",
    )(*blocks, *events)


def join_kernel(*refs, count):
    out = refs[-1]
    each = refs[0].shape[0]
    for k, ref in enumerate(refs[:count]):
        out[k * each : (k + 1) * each] = ref[...]


def join_blocks(parts, events):
    shape = (parts[0].shape[0] * len(parts),) + parts[0].shape[1:]
    return pl.pallas_call(
        functools.partial(join_kernel, count=len(parts)),
        out_shape=jax.ShapeDtypeStruct(shape, BF16),
        in_specs=[pl.BlockSpec(memory_space=pltpu.VMEM)] * len(parts) + any_specs(events),
        compiler_params=pltpu.CompilerParams(vmem_limit_bytes=60 * 2**20),
        name="join_blocks",
    )(*parts, *events)


def add_kernel(*refs, count, extra):
    parts, outs = refs[:count], refs[count + extra :]
    each = outs[0].shape[0]
    for k, out in enumerate(outs):
        here = slice(k * each, (k + 1) * each)
        out[...] = sum(part[here].astype(F32) for part in parts).astype(BF16)


def add_blocks(parts, groups, events):
    shape = (parts[0].shape[0] // groups,) + parts[0].shape[1:]
    return pl.pallas_call(
        functools.partial(add_kernel, count=len(parts), extra=len(events)),
        out_shape=(jax.ShapeDtypeStruct(shape, BF16),) * groups,
        in_specs=[pl.BlockSpec(memory_space=pltpu.VMEM)] * len(parts) + any_specs(events),
        compiler_params=pltpu.CompilerParams(vmem_limit_bytes=60 * 2**20),
        name="add_blocks",
    )(*parts, *events)


def place_kernel(info, base_ref, other_ref, out_ref):
    out_ref[0] = other_ref[...].astype(out_ref.dtype)


def place_other(info, base, other):
    block_len, width = other.shape
    tile = min(512, block_len)
    return pl.pallas_call(
        place_kernel,
        out_shape=jax.ShapeDtypeStruct(base.shape, base.dtype),
        grid_spec=pltpu.PrefetchScalarGridSpec(
            num_scalar_prefetch=1,
            grid=(block_len // tile,),
            in_specs=[
                pl.BlockSpec(memory_space=pl.ANY),
                pl.BlockSpec((tile, width), lambda i, s: (i, 0)),
            ],
            out_specs=pl.BlockSpec((1, tile, width), lambda i, s: (1 - s[2], i, 0)),
        ),
        input_output_aliases={1: 0},
        compiler_params=pltpu.CompilerParams(vmem_limit_bytes=60 * 2**20),
        name="place_other",
    )(info, base, other)


def swap(block, axis, route):
    if all(a == b for a, b in route):
        return block
    return lax.ppermute(block, axis, route)


class Regroup:
    def __init__(self):
        self.n = lax.axis_size("blk")
        self.me = lax.axis_index("blk")
        self.per = self.n // 2
        self.passage = self.me // self.per
        self.part = lax.rem(self.me, 2)
        self.first = [(i, (i % 2) * self.per + i // 2) for i in range(self.n)]
        self.second = [(i, (1 - i % 2) * self.per + i // 2) for i in range(self.n)]
        self.stays = all(a == b for a, b in self.first)

    def pick(self, pair):
        return lax.dynamic_index_in_dim(pair, 1 - self.part, 0, keepdims=False)

    def gather(self, pair, picked):
        other = swap(picked, "blk", self.second)
        if self.stays:
            return (pair, other)
        kept = lax.dynamic_index_in_dim(pair, self.part, 0, keepdims=True)
        return (swap(kept, "blk", self.first), other)

    def kept_index(self):
        return self.part if self.stays else jnp.zeros_like(self.part)

    def all_blocks(self, block):
        if self.n != 2:
            return lax.all_gather(block, "blk", axis=0)
        other = lax.ppermute(block, "blk", [(0, 1), (1, 0)])
        return jnp.where(self.me == 0, jnp.stack([block, other]), jnp.stack([other, block]))

    def send_back(self, other):
        return swap(other, "blk", [(b, a) for a, b in self.second])

    def join(self, info, kept, other):
        if self.stays:
            return place_other(info, kept, other)
        kept = swap(kept[0], "blk", [(b, a) for a, b in self.first])
        other = other.astype(kept.dtype)
        return jnp.where(self.part == 0, jnp.stack([kept, other]), jnp.stack([other, kept]))


def pack(shards):
    c = min(s.shape[1] for s in shards)
    return jnp.concatenate(
        [s[:, at : at + c] for s in shards for at in range(0, s.shape[1], c)], axis=0
    )


def unpack(block, shapes):
    c = block.shape[-1]
    found, at = [], 0
    for rows, cols in shapes:
        parts = []
        for _ in range(cols // c):
            parts.append(block[..., at : at + rows, :])
            at += rows
        found.append(jnp.concatenate(parts, axis=-1) if len(parts) > 1 else parts[0])
    return found


def exchanged(block, mask):
    both = ("batch", "blk")
    places = range(lax.axis_size("batch") * lax.axis_size("blk"))
    return lax.ppermute(block, both, [(i, i ^ mask) for i in places])


def xor_gather(found, masks, stage, events):
    parts = [found] + [exchanged(found, mask) for mask in stage]
    masks = [held ^ mask for mask in [0] + stage for held in masks]
    return join_blocks(parts, events), masks


def xor_masks(stages):
    masks = [0]
    for stage in stages:
        masks = [held ^ mask for held in masks for mask in [0] + stage]
    return masks


def xor_sum(groups, stages, meanwhile):
    for at, stage in enumerate(stages):
        parts = [groups[0]] + [exchanged(g, mask) for mask, g in zip(stage, groups[1:])]
        if at == len(stages) - 1:
            return [part[0] for part in parts]
        events = meanwhile if at == len(stages) - 2 else ()
        groups = add_blocks(parts, len(stages[at + 1]) + 1, events)


class Weights:
    def __init__(self, shards, vectors=None, begin=None):
        self.shapes = [s.shape for s in shards]
        self.m, self.n = lax.axis_size("batch"), lax.axis_size("blk")
        m, n = self.m, self.n
        r, c = min(s[0] for s in self.shapes), min(s[1] for s in self.shapes)
        self.fits = r % 16 == 0 and c % 128 == 0
        powers = m & (m - 1) == 0 and n == 2 and m >= 8
        self.by_pairs = begin is not None and self.fits and powers
        every = list(range(len(shards)))
        if self.by_pairs:
            y, core, x = list(range(1, n)), [n], [2 * n]
            z = list(range(4 * n, m * n, 4 * n))
            near = pack_after([*shards, vectors], ())
            near = [near] + [exchanged(near, mask) for mask in y]
            cut = sum(s.size for s in shards[:-1]) // c
            cuts = [cut, shards[-1].size // c, vectors.shape[0]]
            picked, arrival = begin(near[1:])
            most, least, self.vectors = stack_rows(near, cuts, (picked,))
            flat = lambda part: part.reshape(-1, *part.shape[-2:])
            first = [0] + y
            b, b_masks = xor_gather(flat(least), first, x, ())
            a, a_masks = xor_gather(flat(most), first, z, (b,))
            b, b_masks = xor_gather(b, b_masks, z, ())
            a, a_masks = xor_gather(a, a_masks, x, (arrival, b))
            self.packed, bundles = [], []
            for part, masks, members in ((a, a_masks, every[:-1]), (b, b_masks, every[-1:])):
                for mask in [0] + core:
                    self.packed.append(exchanged(part, mask) if mask else part)
                    bundles.append(([held ^ mask for held in masks], members))
            self.grid_of = Pieces((r, c), (m, n), bundles)
            self.stages = [core, [a ^ b for a in [0] + x for b in [0] + y][1:], z]
            self.sums_of = Pieces((r, c), (m, n), [(xor_masks(self.stages), every)])
            return
        packed = pack_after(shards, ()) if self.fits else pack(shards)
        packed = lax.all_gather(packed, ("batch", "blk"), axis=0)
        if self.fits:
            self.grid_of = Pieces((r, c), (m, n), [(None, every)])
            self.packed = [packed]
        else:
            self.grid_of = Pieces((r * m, c * n), (1, 1), [(None, every)])
            whole = []
            for part in unpack(packed, self.shapes):
                rows, cols = part.shape[1:]
                part = part.reshape(m, n, rows, cols).transpose(0, 2, 1, 3)
                whole.append(part.reshape(m * rows, n * cols))
            self.packed = [pack(whole)[None]]
        self.sums_of = self.grid_of

    def scatter(self, sums, meanwhile=()):
        extra = 16
        if self.by_pairs:
            return finish_sums(xor_sum(sums, self.stages, meanwhile), self.shapes)
        (sums,) = sums
        if not self.fits:
            rows = sums.shape[1] - extra
            wide = [(a * self.m, b * self.n) for a, b in self.shapes]
            parts = []
            for part in unpack(sums[0, :rows], wide):
                a, b = part.shape[0] // self.m, part.shape[1] // self.n
                part = part.reshape(self.m, a, self.n, b).transpose(0, 2, 1, 3)
                parts.append(part.reshape(self.m * self.n, a, b))
            c = min(s[1] for s in self.shapes)
            blocks = jnp.stack([pack([p[d] for p in parts]) for d in range(self.m * self.n)])
            vecs = sums[0, rows:].reshape(extra, self.n, c).transpose(1, 0, 2)
            vecs = jnp.broadcast_to(vecs[None], (self.m, self.n, extra, c))
            sums = jnp.concatenate([blocks, vecs.reshape(self.m * self.n, extra, c)], axis=1)
        height, c = sums.shape[1:]
        own = lax.psum_scatter(
            sums.reshape(-1, c), ("batch", "blk"), scatter_dimension=0, tiled=True
        )
        return finish_sums([own], self.shapes)


def finish_kernel(*refs, count):
    parts, outs = refs[:count], refs[count:]
    at = 0
    for out in outs:
        rows, cols = out.shape
        c = parts[0].shape[1]
        for start in range(0, cols, c):
            here = slice(at, at + rows)
            out[:, start : start + c] = sum(part[here, :].astype(F32) for part in parts)
            at += rows


def finish_sums(parts, shapes):
    height, c = parts[0].shape
    used = sum(a * b for a, b in shapes) // c
    shapes = list(shapes) + [(height - used, c)]
    if used % 16:
        total = sum(part.astype(F32) for part in parts)
        return [*unpack(total[:used], shapes[:-1]), total[used:]]
    return pl.pallas_call(
        functools.partial(finish_kernel, count=len(parts)),
        out_shape=tuple(jax.ShapeDtypeStruct(shape, F32) for shape in shapes),
        compiler_params=pltpu.CompilerParams(vmem_limit_bytes=60 * 2**20),
        name="finish_sums",
    )(*parts)


def on_device(
    hidden_in,
    lengths,
    cot_out,
    cot_cls,
    w_query,
    w_key,
    w_value,
    w_out,
    w_inner,
    w_outer,
    b_query,
    b_value,
    b_out,
    norm1_gain,
    norm1_shift,
    b_inner,
    b_outer,
    norm2_gain,
    norm2_shift,
):
    plan = Regroup()
    groups, block_len, width = hidden_in.shape
    span = groups * block_len
    per = plan.per
    fleets = [[i * per + j for j in range(per)] for i in range(2)]
    first_row = plan.passage * block_len
    owner = lax.rem(plan.me, per) == 0

    length = lax.dynamic_index_in_dim(lengths, plan.passage, 0, keepdims=False)
    info = jnp.stack(
        [
            length,
            first_row,
            plan.kept_index(),
            plan.kept_index(),
            jnp.where(owner, first_row, -1),
            lax.axis_index("batch"),
            plan.me,
        ]
    ).astype(jnp.int32)

    share = width // plan.n
    narrow = jnp.stack(
        [b_query, b_value, b_out, norm1_gain, norm1_shift, b_outer, norm2_gain, norm2_shift]
    )
    parts = [narrow, b_inner.reshape(-1, share)]
    used = narrow.shape[0] + parts[1].shape[0]
    parts.append(jnp.zeros((-used % 16, share), BF16))
    vec_shard = jnp.concatenate(parts, 0)

    hidden = None

    def begin(near):
        nonlocal hidden
        picked = pick_other(info, hidden_in, near)
        hidden = plan.gather(hidden_in, picked)
        return picked, hidden[1]

    heads = Weights([w_query, w_key, w_value], vec_shard, begin if plan.stays else None)
    if hidden is None:
        hidden = plan.gather(hidden_in, plan.pick(hidden_in))
    if heads.by_pairs:
        vec_all = jnp.where(plan.me == 0, heads.vectors, heads.vectors[::-1])
    else:
        vec_all = plan.all_blocks(vec_shard)
    dense = Weights([w_out, w_inner, w_outer])
    narrow = vec_all[:, :8].transpose(1, 0, 2).reshape(8, width).astype(F32)
    bias_inner = vec_all[:, 8:used].reshape(1, -1).astype(F32)
    bias_heads = jnp.concatenate([narrow[0:1], jnp.zeros_like(narrow[0:1]), narrow[1:2]], 1)

    qkv, *mats = queries_keys_values(
        info, *hidden, heads, bias_heads, cot_out if plan.stays else None
    )
    cots = plan.gather(cot_out, mats.pop() if plan.stays else plan.pick(cot_out))
    at = lambda kind: lambda j: kind * HEADS // 2 + j
    if per == 1:
        sources = [(qkv, at(kind)) for kind in range(3)]
    else:
        kv = lax.all_gather(qkv[:, width:], "blk", axis=0, tiled=True, axis_index_groups=fleets)
        sources = [(qkv, at(0)), (kv, at(0)), (kv, at(1))]
    context_low, probs, sums = attend(info, sources, span)

    own_cls = lax.dynamic_index_in_dim(cot_cls, plan.passage, 0, keepdims=True).astype(F32)
    layer_kept, layer_other, top, grad_context, grad_resid, dense_sums = middle(
        info, hidden, cots, context_low, own_cls, dense, narrow[2:], bias_inner
    )
    part_wo, part_wi, part_wu, dense_vecs = dense.scatter([dense_sums])
    part_bo, part_g1, part_s1, part_bu, part_g2, part_s2 = [dense_vecs[t] for t in range(6)]
    part_bi = dense_vecs[6 : 6 + b_inner.size // share].reshape(-1)
    layer_other = plan.send_back(layer_other)
    tops = plan.all_blocks(top)[::per, 0, :]
    cls_part = lax.dynamic_slice_in_dim(tops, plan.me * share, share, 1)

    back = functools.partial(
        attend_back, info, sources, grad_context, context_low, sums, probs, span
    )
    give = functools.partial(input_grad, info, resid=grad_resid, mats=mats)
    if per == 1:
        most = back([(1, 1), (1, 0), (0, 1)], None)
        other, *layer_rows = give(
            most,
            out_shape=(block_len, width),
            dtype=BF16,
            kept=False,
            join=(layer_kept, layer_other) if plan.stays else (),
            events=(cls_part,),
        )
        layer_rows = layer_rows[0] if layer_rows else plan.join(info, layer_kept, layer_other)
        rest = back([(0, 0)], most, (other, layer_rows))
        other = plan.send_back(other)
    else:
        blocks = span * per // min(1024, span * per)
        grad_q, *grad_kv = back([(k, q) for k in range(blocks) for q in range(2)], None)
        most = [grad_q] + [
            lax.psum_scatter(g, "blk", scatter_dimension=0, tiled=True, axis_index_groups=fleets)
            for g in grad_kv
        ]
        (other,) = give(most, out_shape=(block_len, width), dtype=BF16, kept=False)
        other = plan.send_back(other)
        rest = most
        layer_rows = plan.join(info, layer_kept, layer_other)
    head_sums = head_grads(
        info, hidden, rest, heads.sums_of, 2 if heads.by_pairs else 1, (other,)
    )
    (kept,) = give(rest, out_shape=hidden[0].shape, dtype=F32, kept=True)
    grad_input = plan.join(info, kept, other)
    part_wq, part_wk, part_wv, head_vecs = heads.scatter(
        head_sums, (grad_input, part_wo, dense_vecs)
    )
    part_bq, part_bv = head_vecs[0], head_vecs[1]
    return (
        layer_rows,
        cls_part,
        grad_input,
        part_wq,
        part_wk,
        part_wv,
        part_wo,
        part_wi,
        part_wu,
        part_bq,
        part_bv,
        part_bo,
        part_g1,
        part_s1,
        part_bi,
        part_bu,
        part_g2,
        part_s2,
    )


def solution(mesh):
    rows = P("batch", "blk", None)
    mats = (P("batch", "blk"),) * 6
    vecs = (P("blk"),) * 9
    return jax.shard_map(
        on_device,
        mesh=mesh,
        in_specs=(rows, P("batch"), rows, P("batch", None)) + mats + vecs,
        out_specs=(rows, P("batch", "blk"), rows) + mats + vecs,
        check_vma=False,
    )
```

```python
import functools

import jax
import jax.numpy as jnp
from jax import lax
from jax.experimental import pallas as pl
from jax.experimental.pallas import tpu as pltpu
from jax.sharding import PartitionSpec as P

HEADS = 12
HDIM = 64
PAIR = 2 * HDIM
LOG2E = 1.4426950408889634
BF16 = jnp.bfloat16
F32 = jnp.float32


def live_rows(shape, axis, start, length, shift, span):
    rows = shape[axis]
    step = min(rows, span)
    parts = []
    for at in range(0, rows, step):
        first = start + at
        base = (first // span) * span
        sizes = list(shape)
        sizes[axis] = step
        turned = lax.broadcasted_iota(jnp.int32, tuple(sizes), axis) + (first - base + shift)
        turned = jnp.where(turned >= span, turned - span, turned)
        parts.append(turned < length - base)
    return parts[0] if len(parts) == 1 else jnp.concatenate(parts, axis)


def chunk_of(rows):
    return min(1024, rows // 2)


def segments(rows, size):
    for at in range(0, rows, size):
        for h in range(2):
            yield h, slice(at, at + size), slice(2 * at + h * size, 2 * at + (h + 1) * size)


def beside(part, h):
    blank = jnp.zeros_like(part)
    return jnp.concatenate([part, blank] if h == 0 else [blank, part], 0)


def head_rows(h):
    return slice(h * HDIM, (h + 1) * HDIM)


def attend_kernel(
    info,
    q_ref,
    k_ref,
    v_ref,
    out_ref,
    p_ref,
    sum_ref,
    keys,
    vals,
    ques,
    bound,
    turned,
    *,
    chunk,
    across,
    span,
):
    pos = pl.program_id(1)
    kv = k_ref.shape[0]
    size, width = out_ref.shape[0], p_ref.shape[2]
    factor = HDIM**-0.5 * LOG2E

    @pl.when(pos == 0)
    def prepare():
        live = live_rows((kv, PAIR), 0, 0, info[0], info[1], span)
        kept = jnp.where(live, k_ref[...], jnp.zeros((), BF16))
        keys[...] = kept
        vals[0:PAIR, :] = jnp.where(live, v_ref[...], jnp.zeros((), BF16)).T
        vals[PAIR:, :] = live_rows((16, kv), 1, 0, info[0], info[1], span).astype(BF16)
        turned_q = q_ref[...].T
        squares = kept.astype(F32)
        squares = (squares * squares).astype(BF16)
        half = lambda axis: lax.broadcasted_iota(jnp.int32, (PAIR, PAIR), axis) // HDIM
        sizes = jnp.dot(squares, (half(0) == half(1)).astype(BF16), preferred_element_type=F32)
        largest = jnp.max(sizes, axis=0, keepdims=True)
        tops = [jnp.max(largest[:, head_rows(h)], axis=1, keepdims=True) for h in range(2)]
        for h, queries, cols in segments(q_ref.shape[0], size):
            mine = turned_q[head_rows(h), queries]
            ques[:, cols] = beside(mine, h)
            sharp = mine.astype(F32)
            reach = jnp.sum(sharp * sharp, axis=0, keepdims=True)
            bound[:, cols] = jnp.sqrt(reach * tops[h] * 1.03) * factor

    cols = pl.ds(pl.multiple_of(pos * width, width), width)

    def weigh(peak):
        for start in range(0, width, across):
            own = slice(start, start + across)
            query = ques[:, pl.ds(pl.multiple_of(pos * width + start, across), across)]
            for at in range(0, kv, chunk):
                rows = slice(at, at + chunk)
                scores = jnp.dot(keys[rows, :], query, preferred_element_type=F32)
                p_ref[0, rows, own] = jnp.exp2(scores * factor - peak[:, own]).astype(BF16)
        total = jnp.dot(vals[...], p_ref[0], preferred_element_type=F32)
        sums = total[PAIR : PAIR + 1, :]
        sum_ref[0] = sums
        for h in range(2):
            own = slice(h * size, (h + 1) * size)
            turned[head_rows(h), :] = total[head_rows(h), own] / sums[:, own]
        return jnp.min(sums)

    def exact_peak():
        query = ques[:, cols]

        def largest(at, peak):
            rows = pl.ds(pl.multiple_of(at * chunk, chunk), chunk)
            scores = jnp.dot(keys[rows, :], query, preferred_element_type=F32)
            live = live_rows((chunk, width), 0, at * chunk, info[0], info[1], span)
            return jnp.maximum(peak, jnp.max(jnp.where(live, scores, -1e30), axis=0, keepdims=True))

        return lax.fori_loop(0, kv // chunk, largest, jnp.full((1, width), -1e30, F32)) * factor

    lowest = weigh(bound[:, cols])

    @pl.when(jnp.logical_not(lowest > 2.0**-70))
    def again():
        weigh(exact_peak())

    out_ref[...] = turned[...].T.astype(BF16)


def attend(info, sources, span):
    (queries, q_at), (keys, k_at), (values, v_at) = sources
    rows, kv = queries.shape[0], keys.shape[0]
    size = chunk_of(rows)
    pairs = HEADS // 2
    return pl.pallas_call(
        functools.partial(
            attend_kernel, chunk=min(256, kv), across=min(256, 2 * size), span=span
        ),
        out_shape=(
            jax.ShapeDtypeStruct((rows, HEADS * HDIM), BF16),
            jax.ShapeDtypeStruct((pairs, kv, 2 * rows), BF16),
            jax.ShapeDtypeStruct((pairs, 1, 2 * rows), F32),
        ),
        grid_spec=pltpu.PrefetchScalarGridSpec(
            num_scalar_prefetch=1,
            grid=(pairs, rows // size),
            in_specs=[
                pl.BlockSpec((rows, PAIR), lambda j, c, s: (0, q_at(j))),
                pl.BlockSpec((kv, PAIR), lambda j, c, s: (0, k_at(j))),
                pl.BlockSpec((kv, PAIR), lambda j, c, s: (0, v_at(j))),
            ],
            out_specs=(
                pl.BlockSpec((size, PAIR), lambda j, c, s: (c, j)),
                pl.BlockSpec((1, kv, 2 * size), lambda j, c, s: (j, 0, c)),
                pl.BlockSpec((1, 1, 2 * size), lambda j, c, s: (j, 0, c)),
            ),
            scratch_shapes=[
                pltpu.VMEM((kv, PAIR), BF16),
                pltpu.VMEM((PAIR + 16, kv), BF16),
                pltpu.VMEM((PAIR, 2 * rows), BF16),
                pltpu.VMEM((1, 2 * rows), F32),
                pltpu.VMEM((PAIR, size), F32),
            ],
        ),
        compiler_params=pltpu.CompilerParams(vmem_limit_bytes=60 * 2**20),
        name="attend",
    )(info, queries, keys, values)


def attend_back_kernel(
    info,
    units,
    q_ref,
    k_ref,
    v_ref,
    g_ref,
    ctx_ref,
    sum_ref,
    p_ref,
    *rest,
    chunk,
    size,
    span,
    more,
    extra,
):
    before, rest = (rest[:3], rest[3:]) if more else (None, rest)
    rest = rest[extra:]
    gq_ref, gk_ref, gv_ref, keys, grads, grads_up, ques_up, delta, low, total, key_sum, value_sum = rest
    step = pl.program_id(1)
    kv, rows = k_ref.shape[0], q_ref.shape[0]
    block, part = p_ref.shape[1:]
    scale = HDIM**-0.5

    @pl.when(step == 0)
    def prepare():
        live = live_rows((kv, PAIR), 0, 0, info[0], info[1], span)
        keys[...] = jnp.where(live, k_ref[...], jnp.zeros((), BF16)).T
        turned = g_ref[...].T.astype(F32)
        dots = turned * ctx_ref[...].T.astype(F32)
        for h, queries, cols in segments(rows, size):
            inverse = 1.0 / sum_ref[0, :, cols]
            own = head_rows(h)
            delta[:, cols] = jnp.sum(dots[own, queries], axis=0, keepdims=True) * inverse
            shared = beside((turned[own, queries] * inverse).astype(BF16), h)
            grads[:, cols] = shared
            grads_up[cols, :] = shared.T
            lane = lax.broadcasted_iota(jnp.int32, (queries.stop - queries.start, PAIR), 1)
            ques_up[cols, :] = jnp.where(lane // HDIM == h, q_ref[queries, :], jnp.zeros((), BF16))
        for held in (total, key_sum, value_sum):
            held[...] = jnp.zeros_like(held)

    here = pl.ds(pl.multiple_of(units[0, step] * block, block), block)
    there = pl.multiple_of(units[1, step] * part, part)
    cols = pl.ds(there, part)
    values = v_ref[here, :]
    for start in range(0, part, chunk):
        own = slice(start, start + chunk)
        from_all = pl.ds(there + start, chunk)
        change = jnp.dot(values, grads[:, from_all], preferred_element_type=F32)
        low[:, own] = (p_ref[0, :, own].astype(F32) * (change - delta[:, from_all])).astype(BF16)
    value_sum[here, :] += jnp.dot(p_ref[0], grads_up[cols, :], preferred_element_type=F32)
    key_sum[here, :] += jnp.dot(low[...], ques_up[cols, :], preferred_element_type=F32)
    total[:, cols] += jnp.dot(keys[:, here], low[...], preferred_element_type=F32)

    @pl.when(step == pl.num_programs(1) - 1)
    def finish():
        live = live_rows((kv, PAIR), 0, 0, info[0], info[1], span)
        zero = jnp.zeros((), F32)
        found = [jnp.where(live, key_sum[...] * scale, zero), jnp.where(live, value_sum[...], zero)]
        for t, (ref, value) in enumerate(zip((gk_ref, gv_ref), found)):
            if more:
                value += before[t + 1][...].astype(F32)
            ref[...] = value.astype(BF16)
        parts = [[], []]
        for h, queries, cols in segments(rows, size):
            parts[h].append(total[head_rows(h), cols])
        value = (jnp.concatenate([jnp.concatenate(p, 1) for p in parts], 0) * scale).T
        if more:
            value += before[0][...].astype(F32)
        gq_ref[...] = value.astype(BF16)


def attend_back(info, sources, grad, context, sums, probs, span, units, before, events=()):
    (queries, q_at), (keys, k_at), (values, v_at) = sources
    rows, kv = queries.shape[0], keys.shape[0]
    pairs = HEADS // 2
    wide = HEADS * HDIM
    more = before is not None
    block, part, size = min(1024, kv), rows, chunk_of(rows)
    cut = 2 if more else 1
    rows, kv = rows // cut, kv // cut
    out_rows = [rows, kv, kv]
    heights = [rows * cut, kv * cut, kv * cut]
    units = jnp.array(list(zip(*units)), jnp.int32)
    col = lambda height, at=lambda j: j: pl.BlockSpec(
        (height, PAIR), lambda j, c, s, u: (0, at(j))
    )
    return pl.pallas_call(
        functools.partial(
            attend_back_kernel,
            chunk=min(512, part),
            size=size,
            span=span,
            more=more,
            extra=len(events),
        ),
        out_shape=tuple(jax.ShapeDtypeStruct((height, wide), BF16) for height in heights),
        grid_spec=pltpu.PrefetchScalarGridSpec(
            num_scalar_prefetch=2,
            grid=(pairs, units.shape[1]),
            in_specs=[
                col(rows, q_at),
                col(kv, k_at),
                col(kv, v_at),
                col(rows),
                col(rows),
                pl.BlockSpec((1, 1, 2 * rows), lambda j, c, s, u: (j, 0, 0)),
                pl.BlockSpec((1, block, part), lambda j, c, s, u: (j, u[0, c], u[1, c])),
            ]
            + ([col(height) for height in out_rows] if more else [])
            + any_specs(events),
            out_specs=tuple(col(height) for height in out_rows),
            scratch_shapes=[
                pltpu.VMEM((PAIR, kv), BF16),
                pltpu.VMEM((PAIR, 2 * rows), BF16),
                pltpu.VMEM((2 * rows, PAIR), BF16),
                pltpu.VMEM((2 * rows, PAIR), BF16),
                pltpu.VMEM((1, 2 * rows), F32),
                pltpu.VMEM((block, part), BF16),
                pltpu.VMEM((PAIR, 2 * rows), F32),
                pltpu.VMEM((kv, PAIR), F32),
                pltpu.VMEM((kv, PAIR), F32),
            ],
        ),
        input_output_aliases={9 + t: t for t in range(3)} if more else {},
        compiler_params=pltpu.CompilerParams(vmem_limit_bytes=60 * 2**20),
        name="attend_back_last" if more else "attend_back",
    )(info, units, queries, keys, values, grad, context, sums, probs, *(before or ()), *events)


def rows_of(kept_ref, other_ref, step, split):
    return jnp.where(step < split, kept_ref[0], other_ref[...])


def project(rows, weight):
    return jnp.dot(rows, weight, preferred_element_type=F32)


def project_back(grads, weight):
    return lax.dot_general(grads, weight, (((1,), (1,)), ((), ())), preferred_element_type=F32)


def weight_grad(rows, grads):
    return lax.dot_general(rows, grads, (((0,), (0,)), ((), ())), preferred_element_type=F32)


def run_all(copies):
    for copy in copies:
        copy.start()
    return copies


def wait_all(copies):
    for copy in copies:
        copy.wait()


class Pieces:
    def __init__(self, shape, mesh_shape, bundles):
        self.r, self.c = shape
        self.m, self.n = mesh_shape
        self.bundles = bundles
        self.slots = self.m * self.n

    def place(self, masks, slot, info):
        if masks is None:
            return slot // self.n, lax.rem(slot, self.n)
        return info[5] ^ (masks[slot] // self.n), info[6] ^ (masks[slot] % self.n)

    def copies(self, refs, mats, sems, info, out):
        found = [[] for _ in mats]
        r, c = self.r, self.c
        count = 0
        for (masks, members), ref in zip(self.bundles, refs):
            for slot in range(self.slots if masks is None else len(masks)):
                j, i = self.place(masks, slot, info)
                at = 0
                for t in members:
                    mat = mats[t]
                    tall = mat.shape[0] // (self.m * r)
                    wide = mat.shape[1] // (self.n * c)
                    for w in range(wide):
                        if isinstance(ref, (tuple, list)):
                            each = self.slots // len(ref)
                            block = ref[slot // each].at[slot % each, pl.ds(at, tall * r), :]
                        else:
                            block = ref.at[slot, pl.ds(at, tall * r), :]
                        down = pl.multiple_of(j * (tall * r), tall * r)
                        side = pl.multiple_of((i * wide + w) * c, c)
                        place = mat.at[pl.ds(down, tall * r), pl.ds(side, c)]
                        at += tall * r
                        pair = (place, block) if out else (block, place)
                        found[t].append(pltpu.make_async_copy(*pair, sems.at[count]))
                        count += 1
        return found

    def count(self):
        return 9 * self.slots


def any_specs(arrays):
    return [pl.BlockSpec(memory_space=pl.ANY)] * len(arrays)


def queries_kernel(info, kept_ref, other_ref, bias_ref, *rest, split, grid_of, carry):
    count = len(grid_of.bundles)
    packed, rest = rest[:count], rest[count:]
    step = pl.program_id(0)
    if carry:
        pair_ref, out_ref, mat_q, mat_k, mat_v, picked, sems = rest
        picked[...] = pair_ref[0]
    else:
        out_ref, mat_q, mat_k, mat_v, sems = rest
    mats = [mat_q, mat_k, mat_v]

    @pl.when(step == 0)
    def load():
        loads = grid_of.copies(packed, mats, sems, info, False)
        for group in loads:
            run_all(group)
        for group in loads:
            wait_all(group)

    rows = rows_of(kept_ref, other_ref, step, split)
    width = mat_q.shape[1]
    for t, mat in enumerate(mats):
        cols = slice(t * width, (t + 1) * width)
        out_ref[:, cols] = (project(rows, mat[...]) + bias_ref[:, cols]).astype(BF16)


def split_specs(kept_at, tile, split, width):
    return [
        pl.BlockSpec((1, tile, width), lambda i, s: (s[kept_at], jnp.minimum(i, split - 1), 0)),
        pl.BlockSpec((tile, width), lambda i, s: (jnp.maximum(i - split, 0), 0)),
    ]


def whole_spec(shape):
    return pl.BlockSpec(shape, lambda i, s: (0,) * len(shape))


def queries_keys_values(info, kept, other, weights, bias, pair):
    block_len, width = other.shape
    tile = min(512, block_len)
    split = block_len // tile
    part = block_len // (2 * split)
    carried = [] if pair is None else [pair]
    mat = jax.ShapeDtypeStruct((width, width), BF16)
    return pl.pallas_call(
        functools.partial(
            queries_kernel, split=split, grid_of=weights.grid_of, carry=bool(carried)
        ),
        out_shape=(jax.ShapeDtypeStruct((2 * block_len, 3 * width), BF16), mat, mat, mat)
        + (jax.ShapeDtypeStruct((block_len, width), BF16),) * len(carried),
        grid_spec=pltpu.PrefetchScalarGridSpec(
            num_scalar_prefetch=1,
            grid=(2 * split,),
            in_specs=split_specs(2, tile, split, width)
            + [whole_spec(bias.shape)]
            + any_specs(weights.packed)
            + [pl.BlockSpec((1, part, width), lambda i, s: (1 - s[2], i, 0))] * len(carried),
            out_specs=(pl.BlockSpec((tile, 3 * width), lambda i, s: (i, 0)),)
            + (whole_spec(mat.shape),) * 3
            + (pl.BlockSpec((part, width), lambda i, s: (i, 0)),) * len(carried),
            scratch_shapes=[pltpu.SemaphoreType.DMA((weights.grid_of.count(),))],
        ),
        compiler_params=pltpu.CompilerParams(vmem_limit_bytes=60 * 2**20),
        name="queries",
    )(info, kept, other, bias, *weights.packed, *carried)


def normal(values):
    middle = jnp.mean(values, axis=-1, keepdims=True)
    centered = values - middle
    spread = jnp.mean(centered * centered, axis=-1, keepdims=True)
    inverse = lax.rsqrt(spread + 1e-12)
    return centered * inverse, inverse


def normal_back(grad, unit, inverse, gain):
    scaled = grad * gain
    mean = jnp.mean(scaled, axis=-1, keepdims=True)
    along = jnp.mean(scaled * unit, axis=-1, keepdims=True)
    return (scaled - mean - unit * along) * inverse


def gelu_pair(u):
    phi = 0.5 + 0.5 * lax.erf(0.7071067811865476 * u)
    bell = jnp.exp2((-0.5 * LOG2E) * (u * u))
    return u * phi, phi + (0.3989422804014327 * u) * bell


def add_rows(total, at, values):
    total[at : at + 1, 0 : values.shape[1]] += jnp.sum(values, axis=0, keepdims=True)


def middle_kernel(
    info,
    hid_kept,
    hid_other,
    cot_kept,
    cot_other,
    ctx_ref,
    cls_ref,
    vec_ref,
    inner_bias,
    packed,
    layer_kept,
    layer_other,
    top_ref,
    grad_ctx_ref,
    resid_ref,
    sums_ref,
    mat_out,
    mat_inner,
    mat_outer,
    acc_out,
    acc_inner,
    acc_outer,
    totals,
    active,
    slope,
    low,
    vec_low,
    sems,
    vec_sems,
    *,
    split,
    grid_of,
    chunk,
):
    step = pl.program_id(0)
    last = pl.num_programs(0) - 1
    mats = [mat_out, mat_inner, mat_outer]
    tile, width = ctx_ref.shape
    ff = mat_inner.shape[1]
    loads = grid_of.copies([packed], mats, sems, info, False)

    @pl.when(step == 0)
    def start():
        for group in loads:
            run_all(group)
        for acc in (acc_out, acc_inner, acc_outer, totals):
            acc[...] = jnp.zeros_like(acc)
        wait_all(loads[0])

    bias_out, gain_one, shift_one, bias_outer, gain_two, shift_two = [
        vec_ref[t : t + 1, :] for t in range(6)
    ]
    hidden = rows_of(hid_kept, hid_other, step, split).astype(F32)
    context = ctx_ref[...]
    unit_one, inverse_one = normal(hidden + project(context, mat_out[...]) + bias_out)
    normed = unit_one * gain_one + shift_one
    normed_low = normed.astype(BF16)

    @pl.when(step == 0)
    def more():
        wait_all(loads[1])
        wait_all(loads[2])

    for at in range(0, ff, chunk):
        cols = slice(at, at + chunk)
        inner = project(normed_low, mat_inner[:, cols]) + inner_bias[:, cols]
        value, change = gelu_pair(inner)
        active[:, cols] = value.astype(BF16)
        slope[:, cols] = change.astype(BF16)
    unit_two, inverse_two = normal(normed + project(active[...], mat_outer[...]) + bias_outer)
    layer = (unit_two * gain_two + shift_two).astype(BF16)

    @pl.when(step < split)
    def kept():
        layer_kept[0] = layer

    @pl.when(step >= split)
    def other():
        layer_other[...] = layer

    @pl.when(step * tile == info[1])
    def top():
        top_ref[...] = layer[0:16, :]


    row = step * tile + lax.broadcasted_iota(jnp.int32, (tile, width), 0)
    grad_result = rows_of(cot_kept, cot_other, step, split).astype(F32)
    grad_result += jnp.where(row == info[4], cls_ref[...], 0.0)
    add_rows(totals, 4, grad_result * unit_two)
    add_rows(totals, 5, grad_result)
    grad_resid_two = normal_back(grad_result, unit_two, inverse_two, gain_two)
    grad_outer = grad_resid_two.astype(BF16)
    add_rows(totals, 3, grad_outer.astype(F32))
    for at in range(0, ff, chunk):
        cols = slice(at, at + chunk)
        grad_inner = project_back(grad_outer, mat_outer[cols, :]) * slope[:, cols].astype(F32)
        low[:, cols] = grad_inner.astype(BF16)
        totals[8:9, cols] += jnp.sum(grad_inner, axis=0, keepdims=True)
        acc_outer[cols, :] += weight_grad(active[:, cols], grad_outer)
    grad_normed = grad_resid_two + project_back(low[...], mat_inner[...])
    for at in range(0, ff, chunk):
        cols = slice(at, at + chunk)
        acc_inner[:, cols] += weight_grad(normed_low, low[:, cols])
    add_rows(totals, 1, grad_normed * unit_one)
    add_rows(totals, 2, grad_normed)
    grad_resid_one = normal_back(grad_normed, unit_one, inverse_one, gain_one)
    resid_ref[...] = grad_resid_one
    grad_attn = grad_resid_one.astype(BF16)
    add_rows(totals, 0, grad_attn.astype(F32))
    acc_out[...] += weight_grad(context, grad_attn)
    grad_ctx_ref[...] = project_back(grad_attn, mat_out[...]).astype(BF16)

    @pl.when(step == last)
    def finish():
        r, c, m, n = grid_of.r, grid_of.c, grid_of.m, grid_of.n
        stores = grid_of.copies([sums_ref], mats, sems, info, True)
        for mat, acc, group in zip(mats, (acc_out, acc_inner, acc_outer), stores):
            mat[...] = acc[...].astype(BF16)
            run_all(group)
        vec_low[...] = jnp.zeros_like(vec_low)
        for i in range(n):
            for t in range(6):
                vec_low[i, t : t + 1, :] = totals[t : t + 1, i * c : (i + 1) * c]
            wide = ff // (n * c)
            for t in range(wide):
                at = (i * wide + t) * c
                vec_low[i, 6 + t : 7 + t, :] = totals[8:9, at : at + c]
        tails = []
        vec_bits = vec_low[...].astype(BF16)
        for i in range(n):
            active[16 * i : 16 * i + 16, 0:c] = vec_bits[i]
        for j in range(m):
            for i in range(n):
                tails.append(
                    pltpu.make_async_copy(
                        active.at[pl.ds(16 * i, 16), pl.ds(0, c)],
                        sums_ref.at[j * n + i, pl.ds(9 * r, 16), :],
                        vec_sems.at[j * n + i],
                    )
                )
        run_all(tails)
        for group in stores:
            wait_all(group)
        wait_all(tails)


def kept_spec(tile, split, width):
    return pl.BlockSpec((1, tile, width), lambda i, s: (s[2], jnp.minimum(i, split - 1), 0))


def other_spec(tile, split, width):
    return pl.BlockSpec((tile, width), lambda i, s: (jnp.maximum(i - split, 0), 0))


def middle(info, hidden, cots, context, cls_row, weights, vectors, inner_bias):
    block_len, width = hidden[1].shape
    grid_of = weights.grid_of
    ff = inner_bias.shape[1]
    tile = min(256, block_len)
    split = block_len // tile
    row_spec = pl.BlockSpec((tile, width), lambda i, s: (i, 0))
    return pl.pallas_call(
        functools.partial(middle_kernel, split=split, grid_of=grid_of, chunk=768),
        out_shape=(
            jax.ShapeDtypeStruct(hidden[0].shape, BF16),
            jax.ShapeDtypeStruct((block_len, width), BF16),
            jax.ShapeDtypeStruct((16, width), BF16),
            jax.ShapeDtypeStruct((2 * block_len, width), BF16),
            jax.ShapeDtypeStruct((2 * block_len, width), F32),
            jax.ShapeDtypeStruct((grid_of.slots, 9 * grid_of.r + 16, grid_of.c), BF16),
        ),
        grid_spec=pltpu.PrefetchScalarGridSpec(
            num_scalar_prefetch=1,
            grid=(2 * split,),
            in_specs=split_specs(2, tile, split, width)
            + split_specs(2, tile, split, width)
            + [
                row_spec,
                whole_spec(cls_row.shape),
                whole_spec(vectors.shape),
                whole_spec(inner_bias.shape),
                pl.BlockSpec(memory_space=pl.ANY),
            ],
            out_specs=(
                kept_spec(tile, split, width),
                other_spec(tile, split, width),
                whole_spec((16, width)),
                row_spec,
                row_spec,
                pl.BlockSpec(memory_space=pl.ANY),
            ),
            scratch_shapes=[
                pltpu.VMEM((width, width), BF16),
                pltpu.VMEM((width, ff), BF16),
                pltpu.VMEM((ff, width), BF16),
                pltpu.VMEM((width, width), F32),
                pltpu.VMEM((width, ff), F32),
                pltpu.VMEM((ff, width), F32),
                pltpu.VMEM((16, ff), F32),
                pltpu.VMEM((tile, ff), BF16),
                pltpu.VMEM((tile, ff), BF16),
                pltpu.VMEM((tile, ff), BF16),
                pltpu.VMEM((grid_of.n, 16, grid_of.c), F32),
                pltpu.SemaphoreType.DMA((grid_of.count(),)),
                pltpu.SemaphoreType.DMA((grid_of.slots,)),
            ],
        ),
        compiler_params=pltpu.CompilerParams(vmem_limit_bytes=60 * 2**20),
        name="middle",
    )(info, *hidden, *cots, context, cls_row, vectors, inner_bias, *weights.packed)


def input_grad_kernel(info, gq_ref, gk_ref, gv_ref, resid_ref, mat_q, mat_k, mat_v, *rest, kept, join):
    if join:
        arrived, grad_ref, joined = rest[0], rest[-2], rest[-1]
        joined[0] = arrived[...].astype(joined.dtype)
    else:
        grad_ref = rest[-1]
    total = resid_ref[...]
    for ref, mat in zip((gq_ref, gk_ref, gv_ref), (mat_q, mat_k, mat_v)):
        total += project_back(ref[...], mat[...])
    if kept:
        grad_ref[0] = total.astype(grad_ref.dtype)
    else:
        grad_ref[...] = total.astype(grad_ref.dtype)


def input_grad(info, grads, resid, mats, out_shape, dtype, kept, join=(), events=()):
    rows, width = resid.shape
    block_len = rows // 2
    tile = min(512, block_len)
    split = block_len // tile
    off = 0 if kept else split
    spec = pl.BlockSpec((tile, width), lambda i, s: (i + off, 0))
    place = kept_spec(tile, split, width) if kept else other_spec(tile, 0, width)
    out = (jax.ShapeDtypeStruct(out_shape, dtype),)
    in_specs = [spec] * 4 + [whole_spec(mat.shape) for mat in mats]
    out_specs = (place,)
    aliases = {}
    if join:
        in_specs += [pl.BlockSpec((tile, width), lambda i, s: (i, 0))] + any_specs(join[:1])
        out += (jax.ShapeDtypeStruct(join[0].shape, join[0].dtype),)
        out_specs += (pl.BlockSpec((1, tile, width), lambda i, s: (1 - s[2], i, 0)),)
        aliases = {len(in_specs): 1}
    return pl.pallas_call(
        functools.partial(input_grad_kernel, kept=kept, join=bool(join)),
        out_shape=out,
        grid_spec=pltpu.PrefetchScalarGridSpec(
            num_scalar_prefetch=1,
            grid=(split,),
            in_specs=in_specs + any_specs(events),
            out_specs=out_specs,
        ),
        input_output_aliases=aliases,
        compiler_params=pltpu.CompilerParams(vmem_limit_bytes=60 * 2**20),
        name="input_grad_kept" if kept else "input_grad_other",
    )(info, *grads, resid, *mats, *join[::-1], *events)


def head_grads_kernel(info, hid_kept, hid_other, *rest, split, grid_of, outs, extra):
    found, rest = rest[:3], rest[3 + extra :]
    sums, (acc, mat_q, mat_k, mat_v, totals, vec_low, sems, vec_sems) = rest[:outs], rest[outs:]
    mats = [mat_q, mat_k, mat_v]
    step = pl.program_id(0)

    @pl.when(step == 0)
    def clear():
        acc[...] = jnp.zeros_like(acc)
        totals[...] = jnp.zeros_like(totals)

    rows = rows_of(hid_kept, hid_other, step, split)
    grads = [ref[...] for ref in found]
    for t, grad in enumerate(grads):
        acc[t] += weight_grad(rows, grad)
    add_rows(totals, 0, grads[0].astype(F32))
    add_rows(totals, 1, grads[2].astype(F32))

    @pl.when(step == pl.num_programs(0) - 1)
    def finish():
        r, c, n = grid_of.r, grid_of.c, grid_of.n
        ((masks, _),) = grid_of.bundles
        stores = grid_of.copies([list(sums)], mats, sems, info, True)
        for t, mat in enumerate(mats):
            mat[...] = acc[t].astype(BF16)
            run_all(stores[t])
        for i in range(n):
            part = jnp.concatenate([totals[0:2, i * c : (i + 1) * c], jnp.zeros((14, c), F32)], 0)
            vec_low[i] = part.astype(BF16)
        tails = []
        each = grid_of.slots // outs
        for slot in range(grid_of.slots):
            j, i = grid_of.place(masks, slot, info)
            place = sums[slot // each].at[slot % each, pl.ds(3 * r, 16), :]
            tails.append(pltpu.make_async_copy(vec_low.at[i], place, vec_sems.at[slot]))
        run_all(tails)
        for group in stores:
            wait_all(group)
        wait_all(tails)


def head_grads(info, hidden, grads, grid_of, outs, events=()):
    block_len, width = hidden[1].shape
    tile = min(512, block_len)
    split = block_len // tile
    rows = pl.BlockSpec((tile, width), lambda i, s: (i, 0))
    block = (grid_of.slots // outs, 3 * grid_of.r + 16, grid_of.c)
    return pl.pallas_call(
        functools.partial(
            head_grads_kernel, split=split, grid_of=grid_of, outs=outs, extra=len(events)
        ),
        out_shape=(jax.ShapeDtypeStruct(block, BF16),) * outs,
        grid_spec=pltpu.PrefetchScalarGridSpec(
            num_scalar_prefetch=1,
            grid=(2 * split,),
            in_specs=split_specs(2, tile, split, width) + [rows] * 3 + any_specs(events),
            out_specs=(pl.BlockSpec(memory_space=pl.ANY),) * outs,
            scratch_shapes=[pltpu.VMEM((3, width, width), F32)]
            + [pltpu.VMEM((width, width), BF16)] * 3
            + [
                pltpu.VMEM((8, width), F32),
                pltpu.VMEM((grid_of.n, 16, grid_of.c), BF16),
                pltpu.SemaphoreType.DMA((grid_of.count(),)),
                pltpu.SemaphoreType.DMA((grid_of.slots,)),
            ],
        ),
        compiler_params=pltpu.CompilerParams(vmem_limit_bytes=60 * 2**20),
        name="head_grads",
    )(info, *hidden, *grads, *events)


def pick_kernel(info, pair_ref, *rest):
    rest[-1][...] = pair_ref[0]


def pick_other(info, pair, events):
    _, block_len, width = pair.shape
    tile = min(512, block_len)
    return pl.pallas_call(
        pick_kernel,
        out_shape=jax.ShapeDtypeStruct((block_len, width), pair.dtype),
        grid_spec=pltpu.PrefetchScalarGridSpec(
            num_scalar_prefetch=1,
            grid=(block_len // tile,),
            in_specs=[pl.BlockSpec((1, tile, width), lambda i, s: (1 - s[2], i, 0))]
            + any_specs(events),
            out_specs=pl.BlockSpec((tile, width), lambda i, s: (i, 0)),
        ),
        compiler_params=pltpu.CompilerParams(vmem_limit_bytes=60 * 2**20),
        name="pick_other",
    )(info, pair, *events)


def pack_kernel(*refs, count):
    out = refs[-1]
    c = out.shape[1]
    at = 0
    for ref in refs[:count]:
        rows, cols = ref.shape
        for start in range(0, cols, c):
            out[at : at + rows, :] = ref[:, start : start + c]
            at += rows


def pack_after(shards, events):
    c = min(s.shape[1] for s in shards)
    rows = sum(s.size for s in shards) // c
    return pl.pallas_call(
        functools.partial(pack_kernel, count=len(shards)),
        out_shape=jax.ShapeDtypeStruct((rows, c), BF16),
        in_specs=[pl.BlockSpec(memory_space=pltpu.VMEM)] * len(shards) + any_specs(events),
        compiler_params=pltpu.CompilerParams(vmem_limit_bytes=60 * 2**20),
        name="pack",
    )(*shards, *events)


def stack_kernel(*refs, count, outs):
    at = 0
    for out in refs[-outs:]:
        rows = out.shape[1]
        for k, ref in enumerate(refs[:count]):
            out[k] = ref[at : at + rows, :]
        at += rows


def stack_rows(blocks, cuts, events):
    c = blocks[0].shape[1]
    return pl.pallas_call(
        functools.partial(stack_kernel, count=len(blocks), outs=len(cuts)),
        out_shape=tuple(jax.ShapeDtypeStruct((len(blocks), rows, c), BF16) for rows in cuts),
        in_specs=[pl.BlockSpec(memory_space=pltpu.VMEM)] * len(blocks) + any_specs(events),
        compiler_params=pltpu.CompilerParams(vmem_limit_bytes=60 * 2**20),
        name="stack_rows",
    )(*blocks, *events)


def join_kernel(*refs, count):
    out = refs[-1]
    each = refs[0].shape[0]
    for k, ref in enumerate(refs[:count]):
        out[k * each : (k + 1) * each] = ref[...]


def join_blocks(parts, events):
    shape = (parts[0].shape[0] * len(parts),) + parts[0].shape[1:]
    return pl.pallas_call(
        functools.partial(join_kernel, count=len(parts)),
        out_shape=jax.ShapeDtypeStruct(shape, BF16),
        in_specs=[pl.BlockSpec(memory_space=pltpu.VMEM)] * len(parts) + any_specs(events),
        compiler_params=pltpu.CompilerParams(vmem_limit_bytes=60 * 2**20),
        name="join_blocks",
    )(*parts, *events)


def add_kernel(*refs, count, extra):
    parts, outs = refs[:count], refs[count + extra :]
    each = outs[0].shape[0]
    for k, out in enumerate(outs):
        here = slice(k * each, (k + 1) * each)
        out[...] = sum(part[here].astype(F32) for part in parts).astype(BF16)


def add_blocks(parts, groups, events):
    shape = (parts[0].shape[0] // groups,) + parts[0].shape[1:]
    return pl.pallas_call(
        functools.partial(add_kernel, count=len(parts), extra=len(events)),
        out_shape=(jax.ShapeDtypeStruct(shape, BF16),) * groups,
        in_specs=[pl.BlockSpec(memory_space=pltpu.VMEM)] * len(parts) + any_specs(events),
        compiler_params=pltpu.CompilerParams(vmem_limit_bytes=60 * 2**20),
        name="add_blocks",
    )(*parts, *events)


def place_kernel(info, base_ref, other_ref, out_ref):
    out_ref[0] = other_ref[...].astype(out_ref.dtype)


def place_other(info, base, other):
    block_len, width = other.shape
    tile = min(512, block_len)
    return pl.pallas_call(
        place_kernel,
        out_shape=jax.ShapeDtypeStruct(base.shape, base.dtype),
        grid_spec=pltpu.PrefetchScalarGridSpec(
            num_scalar_prefetch=1,
            grid=(block_len // tile,),
            in_specs=[
                pl.BlockSpec(memory_space=pl.ANY),
                pl.BlockSpec((tile, width), lambda i, s: (i, 0)),
            ],
            out_specs=pl.BlockSpec((1, tile, width), lambda i, s: (1 - s[2], i, 0)),
        ),
        input_output_aliases={1: 0},
        compiler_params=pltpu.CompilerParams(vmem_limit_bytes=60 * 2**20),
        name="place_other",
    )(info, base, other)


def swap(block, axis, route):
    if all(a == b for a, b in route):
        return block
    return lax.ppermute(block, axis, route)


class Regroup:
    def __init__(self):
        self.n = lax.axis_size("blk")
        self.me = lax.axis_index("blk")
        self.per = self.n // 2
        self.passage = self.me // self.per
        self.part = lax.rem(self.me, 2)
        self.first = [(i, (i % 2) * self.per + i // 2) for i in range(self.n)]
        self.second = [(i, (1 - i % 2) * self.per + i // 2) for i in range(self.n)]
        self.stays = all(a == b for a, b in self.first)

    def pick(self, pair):
        return lax.dynamic_index_in_dim(pair, 1 - self.part, 0, keepdims=False)

    def gather(self, pair, picked):
        other = swap(picked, "blk", self.second)
        if self.stays:
            return (pair, other)
        kept = lax.dynamic_index_in_dim(pair, self.part, 0, keepdims=True)
        return (swap(kept, "blk", self.first), other)

    def kept_index(self):
        return self.part if self.stays else jnp.zeros_like(self.part)

    def all_blocks(self, block):
        if self.n != 2:
            return lax.all_gather(block, "blk", axis=0)
        other = lax.ppermute(block, "blk", [(0, 1), (1, 0)])
        return jnp.where(self.me == 0, jnp.stack([block, other]), jnp.stack([other, block]))

    def send_back(self, other):
        return swap(other, "blk", [(b, a) for a, b in self.second])

    def join(self, info, kept, other):
        if self.stays:
            return place_other(info, kept, other)
        kept = swap(kept[0], "blk", [(b, a) for a, b in self.first])
        other = other.astype(kept.dtype)
        return jnp.where(self.part == 0, jnp.stack([kept, other]), jnp.stack([other, kept]))


def pack(shards):
    c = min(s.shape[1] for s in shards)
    return jnp.concatenate(
        [s[:, at : at + c] for s in shards for at in range(0, s.shape[1], c)], axis=0
    )


def unpack(block, shapes):
    c = block.shape[-1]
    found, at = [], 0
    for rows, cols in shapes:
        parts = []
        for _ in range(cols // c):
            parts.append(block[..., at : at + rows, :])
            at += rows
        found.append(jnp.concatenate(parts, axis=-1) if len(parts) > 1 else parts[0])
    return found


def exchanged(block, mask):
    both = ("batch", "blk")
    places = range(lax.axis_size("batch") * lax.axis_size("blk"))
    return lax.ppermute(block, both, [(i, i ^ mask) for i in places])


def xor_gather(found, masks, stage, events):
    parts = [found] + [exchanged(found, mask) for mask in stage]
    masks = [held ^ mask for mask in [0] + stage for held in masks]
    return join_blocks(parts, events), masks


def xor_masks(stages):
    masks = [0]
    for stage in stages:
        masks = [held ^ mask for held in masks for mask in [0] + stage]
    return masks


def xor_sum(groups, stages, meanwhile):
    for at, stage in enumerate(stages):
        parts = [groups[0]] + [exchanged(g, mask) for mask, g in zip(stage, groups[1:])]
        if at == len(stages) - 1:
            return [part[0] for part in parts]
        events = meanwhile if at == len(stages) - 2 else ()
        groups = add_blocks(parts, len(stages[at + 1]) + 1, events)


class Weights:
    def __init__(self, shards, vectors=None, begin=None):
        self.shapes = [s.shape for s in shards]
        self.m, self.n = lax.axis_size("batch"), lax.axis_size("blk")
        m, n = self.m, self.n
        r, c = min(s[0] for s in self.shapes), min(s[1] for s in self.shapes)
        self.fits = r % 16 == 0 and c % 128 == 0
        powers = m & (m - 1) == 0 and n == 2 and m >= 8
        self.by_pairs = begin is not None and self.fits and powers
        every = list(range(len(shards)))
        if self.by_pairs:
            y, core, x = list(range(1, n)), [n], [2 * n]
            z = list(range(4 * n, m * n, 4 * n))
            near = pack_after([*shards, vectors], ())
            near = [near] + [exchanged(near, mask) for mask in y]
            cut = sum(s.size for s in shards[:-1]) // c
            cuts = [cut, shards[-1].size // c, vectors.shape[0]]
            picked, arrival = begin(near[1:])
            most, least, self.vectors = stack_rows(near, cuts, (picked,))
            flat = lambda part: part.reshape(-1, *part.shape[-2:])
            first = [0] + y
            b, b_masks = xor_gather(flat(least), first, x, ())
            a, a_masks = xor_gather(flat(most), first, z, (b,))
            b, b_masks = xor_gather(b, b_masks, z, ())
            a, a_masks = xor_gather(a, a_masks, x, (arrival, b))
            self.packed, bundles = [], []
            for part, masks, members in ((a, a_masks, every[:-1]), (b, b_masks, every[-1:])):
                for mask in [0] + core:
                    self.packed.append(exchanged(part, mask) if mask else part)
                    bundles.append(([held ^ mask for held in masks], members))
            self.grid_of = Pieces((r, c), (m, n), bundles)
            self.stages = [core, [a ^ b for a in [0] + x for b in [0] + y][1:], z]
            self.sums_of = Pieces((r, c), (m, n), [(xor_masks(self.stages), every)])
            return
        packed = pack_after(shards, ()) if self.fits else pack(shards)
        packed = lax.all_gather(packed, ("batch", "blk"), axis=0)
        if self.fits:
            self.grid_of = Pieces((r, c), (m, n), [(None, every)])
            self.packed = [packed]
        else:
            self.grid_of = Pieces((r * m, c * n), (1, 1), [(None, every)])
            whole = []
            for part in unpack(packed, self.shapes):
                rows, cols = part.shape[1:]
                part = part.reshape(m, n, rows, cols).transpose(0, 2, 1, 3)
                whole.append(part.reshape(m * rows, n * cols))
            self.packed = [pack(whole)[None]]
        self.sums_of = self.grid_of

    def scatter(self, sums, meanwhile=()):
        extra = 16
        if self.by_pairs:
            return finish_sums(xor_sum(sums, self.stages, meanwhile), self.shapes)
        (sums,) = sums
        if not self.fits:
            rows = sums.shape[1] - extra
            wide = [(a * self.m, b * self.n) for a, b in self.shapes]
            parts = []
            for part in unpack(sums[0, :rows], wide):
                a, b = part.shape[0] // self.m, part.shape[1] // self.n
                part = part.reshape(self.m, a, self.n, b).transpose(0, 2, 1, 3)
                parts.append(part.reshape(self.m * self.n, a, b))
            c = min(s[1] for s in self.shapes)
            blocks = jnp.stack([pack([p[d] for p in parts]) for d in range(self.m * self.n)])
            vecs = sums[0, rows:].reshape(extra, self.n, c).transpose(1, 0, 2)
            vecs = jnp.broadcast_to(vecs[None], (self.m, self.n, extra, c))
            sums = jnp.concatenate([blocks, vecs.reshape(self.m * self.n, extra, c)], axis=1)
        height, c = sums.shape[1:]
        own = lax.psum_scatter(
            sums.reshape(-1, c), ("batch", "blk"), scatter_dimension=0, tiled=True
        )
        return finish_sums([own], self.shapes)


def finish_kernel(*refs, count):
    parts, outs = refs[:count], refs[count:]
    at = 0
    for out in outs:
        rows, cols = out.shape
        c = parts[0].shape[1]
        for start in range(0, cols, c):
            here = slice(at, at + rows)
            out[:, start : start + c] = sum(part[here, :].astype(F32) for part in parts)
            at += rows


def finish_sums(parts, shapes):
    height, c = parts[0].shape
    used = sum(a * b for a, b in shapes) // c
    shapes = list(shapes) + [(height - used, c)]
    if used % 16:
        total = sum(part.astype(F32) for part in parts)
        return [*unpack(total[:used], shapes[:-1]), total[used:]]
    return pl.pallas_call(
        functools.partial(finish_kernel, count=len(parts)),
        out_shape=tuple(jax.ShapeDtypeStruct(shape, F32) for shape in shapes),
        compiler_params=pltpu.CompilerParams(vmem_limit_bytes=60 * 2**20),
        name="finish_sums",
    )(*parts)


def on_device(
    hidden_in,
    lengths,
    cot_out,
    cot_cls,
    w_query,
    w_key,
    w_value,
    w_out,
    w_inner,
    w_outer,
    b_query,
    b_value,
    b_out,
    norm1_gain,
    norm1_shift,
    b_inner,
    b_outer,
    norm2_gain,
    norm2_shift,
):
    plan = Regroup()
    groups, block_len, width = hidden_in.shape
    span = groups * block_len
    per = plan.per
    fleets = [[i * per + j for j in range(per)] for i in range(2)]
    first_row = plan.passage * block_len
    owner = lax.rem(plan.me, per) == 0

    length = lax.dynamic_index_in_dim(lengths, plan.passage, 0, keepdims=False)
    info = jnp.stack(
        [
            length,
            first_row,
            plan.kept_index(),
            plan.kept_index(),
            jnp.where(owner, first_row, -1),
            lax.axis_index("batch"),
            plan.me,
        ]
    ).astype(jnp.int32)

    share = width // plan.n
    flat = [b_query, b_value, b_out, norm1_gain, norm1_shift, b_outer, norm2_gain, norm2_shift]
    used = 8 + b_inner.size // share
    flat += [b_inner, jnp.zeros((-used % 16 * share,), BF16)]
    vec_shard = jnp.concatenate(flat).reshape(-1, share)

    hidden = None

    def begin(near):
        nonlocal hidden
        picked = pick_other(info, hidden_in, near)
        hidden = plan.gather(hidden_in, picked)
        return picked, hidden[1]

    heads = Weights([w_query, w_key, w_value], vec_shard, begin if plan.stays else None)
    if hidden is None:
        hidden = plan.gather(hidden_in, plan.pick(hidden_in))
    if heads.by_pairs:
        vec_all = jnp.where(plan.me == 0, heads.vectors, heads.vectors[::-1])
    else:
        vec_all = plan.all_blocks(vec_shard)
    dense = Weights([w_out, w_inner, w_outer])
    narrow = vec_all[:, :8].transpose(1, 0, 2).reshape(8, width).astype(F32)
    bias_inner = vec_all[:, 8:used].reshape(1, -1).astype(F32)
    bias_heads = jnp.concatenate([narrow[0:1], jnp.zeros_like(narrow[0:1]), narrow[1:2]], 1)

    qkv, *mats = queries_keys_values(
        info, *hidden, heads, bias_heads, cot_out if plan.stays else None
    )
    cots = plan.gather(cot_out, mats.pop() if plan.stays else plan.pick(cot_out))
    at = lambda kind: lambda j: kind * HEADS // 2 + j
    if per == 1:
        sources = [(qkv, at(kind)) for kind in range(3)]
    else:
        kv = lax.all_gather(qkv[:, width:], "blk", axis=0, tiled=True, axis_index_groups=fleets)
        sources = [(qkv, at(0)), (kv, at(0)), (kv, at(1))]
    context_low, probs, sums = attend(info, sources, span)

    own_cls = lax.dynamic_index_in_dim(cot_cls, plan.passage, 0, keepdims=True).astype(F32)
    layer_kept, layer_other, top, grad_context, grad_resid, dense_sums = middle(
        info, hidden, cots, context_low, own_cls, dense, narrow[2:], bias_inner
    )
    part_wo, part_wi, part_wu, dense_vecs = dense.scatter([dense_sums])
    part_bo, part_g1, part_s1, part_bu, part_g2, part_s2 = [dense_vecs[t] for t in range(6)]
    part_bi = dense_vecs[6 : 6 + b_inner.size // share].reshape(-1)
    layer_other = plan.send_back(layer_other)
    tops = plan.all_blocks(top)[::per, 0, :]
    cls_part = lax.dynamic_slice_in_dim(tops, plan.me * share, share, 1)

    back = functools.partial(
        attend_back, info, sources, grad_context, context_low, sums, probs, span
    )
    give = functools.partial(input_grad, info, resid=grad_resid, mats=mats)
    if per == 1:
        most = back([(1, 1), (1, 0), (0, 1)], None)
        other, *layer_rows = give(
            most,
            out_shape=(block_len, width),
            dtype=BF16,
            kept=False,
            join=(layer_kept, layer_other) if plan.stays else (),
            events=(cls_part,),
        )
        layer_rows = layer_rows[0] if layer_rows else plan.join(info, layer_kept, layer_other)
        rest = back([(0, 0)], most, (other, layer_rows))
        other = plan.send_back(other)
    else:
        blocks = span * per // min(1024, span * per)
        grad_q, *grad_kv = back([(k, q) for k in range(blocks) for q in range(2)], None)
        most = [grad_q] + [
            lax.psum_scatter(g, "blk", scatter_dimension=0, tiled=True, axis_index_groups=fleets)
            for g in grad_kv
        ]
        (other,) = give(most, out_shape=(block_len, width), dtype=BF16, kept=False)
        other = plan.send_back(other)
        rest = most
        layer_rows = plan.join(info, layer_kept, layer_other)
    head_sums = head_grads(
        info, hidden, rest, heads.sums_of, 2 if heads.by_pairs else 1, (other,)
    )
    (kept,) = give(rest, out_shape=hidden[0].shape, dtype=F32, kept=True)
    grad_input = plan.join(info, kept, other)
    part_wq, part_wk, part_wv, head_vecs = heads.scatter(
        head_sums, (grad_input, part_wo, dense_vecs)
    )
    part_bq, part_bv = head_vecs[0], head_vecs[1]
    return (
        layer_rows,
        cls_part,
        grad_input,
        part_wq,
        part_wk,
        part_wv,
        part_wo,
        part_wi,
        part_wu,
        part_bq,
        part_bv,
        part_bo,
        part_g1,
        part_s1,
        part_bi,
        part_bu,
        part_g2,
        part_s2,
    )


def solution(mesh):
    rows = P("batch", "blk", None)
    mats = (P("batch", "blk"),) * 6
    vecs = (P("blk"),) * 9
    return jax.shard_map(
        on_device,
        mesh=mesh,
        in_specs=(rows, P("batch"), rows, P("batch", None)) + mats + vecs,
        out_specs=(rows, P("batch", "blk"), rows) + mats + vecs,
        check_vma=False,
    )
```

```python
import functools

import jax
import jax.numpy as jnp
from jax import lax
from jax.experimental import pallas as pl
from jax.experimental.pallas import tpu as pltpu
from jax.sharding import PartitionSpec as P

HEADS = 12
HDIM = 64
PAIR = 2 * HDIM
LOG2E = 1.4426950408889634
BF16 = jnp.bfloat16
F32 = jnp.float32


def live_rows(shape, axis, start, length, shift, span):
    rows = shape[axis]
    step = min(rows, span)
    parts = []
    for at in range(0, rows, step):
        first = start + at
        base = (first // span) * span
        sizes = list(shape)
        sizes[axis] = step
        turned = lax.broadcasted_iota(jnp.int32, tuple(sizes), axis) + (first - base + shift)
        turned = jnp.where(turned >= span, turned - span, turned)
        parts.append(turned < length - base)
    return parts[0] if len(parts) == 1 else jnp.concatenate(parts, axis)


def chunk_of(rows):
    return min(1024, rows // 2)


def segments(rows, size):
    for at in range(0, rows, size):
        for h in range(2):
            yield h, slice(at, at + size), slice(2 * at + h * size, 2 * at + (h + 1) * size)


def beside(part, h):
    blank = jnp.zeros_like(part)
    return jnp.concatenate([part, blank] if h == 0 else [blank, part], 0)


def head_rows(h):
    return slice(h * HDIM, (h + 1) * HDIM)


def attend_kernel(
    info,
    q_ref,
    k_ref,
    v_ref,
    out_ref,
    p_ref,
    sum_ref,
    keys,
    vals,
    ques,
    bound,
    turned,
    *,
    chunk,
    across,
    span,
):
    pos = pl.program_id(1)
    kv = k_ref.shape[0]
    size, width = out_ref.shape[0], p_ref.shape[2]
    factor = HDIM**-0.5 * LOG2E

    @pl.when(pos == 0)
    def prepare():
        live = live_rows((kv, PAIR), 0, 0, info[0], info[1], span)
        kept = jnp.where(live, k_ref[...], jnp.zeros((), BF16))
        keys[...] = kept
        vals[0:PAIR, :] = jnp.where(live, v_ref[...], jnp.zeros((), BF16)).T
        vals[PAIR:, :] = live_rows((16, kv), 1, 0, info[0], info[1], span).astype(BF16)
        turned_q = q_ref[...].T
        squares = kept.astype(F32)
        squares = (squares * squares).astype(BF16)
        half = lambda axis: lax.broadcasted_iota(jnp.int32, (PAIR, PAIR), axis) // HDIM
        sizes = jnp.dot(squares, (half(0) == half(1)).astype(BF16), preferred_element_type=F32)
        largest = jnp.max(sizes, axis=0, keepdims=True)
        tops = [jnp.max(largest[:, head_rows(h)], axis=1, keepdims=True) for h in range(2)]
        for h, queries, cols in segments(q_ref.shape[0], size):
            mine = turned_q[head_rows(h), queries]
            ques[:, cols] = beside(mine, h)
            sharp = mine.astype(F32)
            reach = jnp.sum(sharp * sharp, axis=0, keepdims=True)
            bound[:, cols] = jnp.sqrt(reach * tops[h] * 1.03) * factor

    cols = pl.ds(pl.multiple_of(pos * width, width), width)

    def weigh(peak):
        for start in range(0, width, across):
            own = slice(start, start + across)
            query = ques[:, pl.ds(pl.multiple_of(pos * width + start, across), across)]
            for at in range(0, kv, chunk):
                rows = slice(at, at + chunk)
                scores = jnp.dot(keys[rows, :], query, preferred_element_type=F32)
                p_ref[0, rows, own] = jnp.exp2(scores * factor - peak[:, own]).astype(BF16)
        total = jnp.dot(vals[...], p_ref[0], preferred_element_type=F32)
        sums = total[PAIR : PAIR + 1, :]
        sum_ref[0] = sums
        for h in range(2):
            own = slice(h * size, (h + 1) * size)
            turned[head_rows(h), :] = total[head_rows(h), own] / sums[:, own]
        return jnp.min(sums)

    def exact_peak():
        query = ques[:, cols]

        def largest(at, peak):
            rows = pl.ds(pl.multiple_of(at * chunk, chunk), chunk)
            scores = jnp.dot(keys[rows, :], query, preferred_element_type=F32)
            live = live_rows((chunk, width), 0, at * chunk, info[0], info[1], span)
            return jnp.maximum(peak, jnp.max(jnp.where(live, scores, -1e30), axis=0, keepdims=True))

        return lax.fori_loop(0, kv // chunk, largest, jnp.full((1, width), -1e30, F32)) * factor

    lowest = weigh(bound[:, cols])

    @pl.when(jnp.logical_not(lowest > 2.0**-70))
    def again():
        weigh(exact_peak())

    out_ref[...] = turned[...].T.astype(BF16)


def attend(info, sources, span):
    (queries, q_at), (keys, k_at), (values, v_at) = sources
    rows, kv = queries.shape[0], keys.shape[0]
    size = chunk_of(rows)
    pairs = HEADS // 2
    return pl.pallas_call(
        functools.partial(
            attend_kernel, chunk=min(256, kv), across=min(256, 2 * size), span=span
        ),
        out_shape=(
            jax.ShapeDtypeStruct((rows, HEADS * HDIM), BF16),
            jax.ShapeDtypeStruct((pairs, kv, 2 * rows), BF16),
            jax.ShapeDtypeStruct((pairs, 1, 2 * rows), F32),
        ),
        grid_spec=pltpu.PrefetchScalarGridSpec(
            num_scalar_prefetch=1,
            grid=(pairs, rows // size),
            in_specs=[
                pl.BlockSpec((rows, PAIR), lambda j, c, s: (0, q_at(j))),
                pl.BlockSpec((kv, PAIR), lambda j, c, s: (0, k_at(j))),
                pl.BlockSpec((kv, PAIR), lambda j, c, s: (0, v_at(j))),
            ],
            out_specs=(
                pl.BlockSpec((size, PAIR), lambda j, c, s: (c, j)),
                pl.BlockSpec((1, kv, 2 * size), lambda j, c, s: (j, 0, c)),
                pl.BlockSpec((1, 1, 2 * size), lambda j, c, s: (j, 0, c)),
            ),
            scratch_shapes=[
                pltpu.VMEM((kv, PAIR), BF16),
                pltpu.VMEM((PAIR + 16, kv), BF16),
                pltpu.VMEM((PAIR, 2 * rows), BF16),
                pltpu.VMEM((1, 2 * rows), F32),
                pltpu.VMEM((PAIR, size), F32),
            ],
        ),
        compiler_params=pltpu.CompilerParams(vmem_limit_bytes=60 * 2**20),
        name="attend",
    )(info, queries, keys, values)


def attend_back_kernel(
    info,
    units,
    q_ref,
    k_ref,
    v_ref,
    g_ref,
    ctx_ref,
    sum_ref,
    p_ref,
    *rest,
    chunk,
    size,
    span,
    more,
    extra,
):
    before, rest = (rest[:3], rest[3:]) if more else (None, rest)
    rest = rest[extra:]
    gq_ref, gk_ref, gv_ref, keys, grads, grads_up, ques_up, delta, low, total, key_sum, value_sum = rest
    step = pl.program_id(1)
    kv, rows = k_ref.shape[0], q_ref.shape[0]
    block, part = p_ref.shape[1:]
    scale = HDIM**-0.5

    @pl.when(step == 0)
    def prepare():
        live = live_rows((kv, PAIR), 0, 0, info[0], info[1], span)
        keys[...] = jnp.where(live, k_ref[...], jnp.zeros((), BF16)).T
        turned = g_ref[...].T.astype(F32)
        dots = turned * ctx_ref[...].T.astype(F32)
        for h, queries, cols in segments(rows, size):
            inverse = 1.0 / sum_ref[0, :, cols]
            own = head_rows(h)
            delta[:, cols] = jnp.sum(dots[own, queries], axis=0, keepdims=True) * inverse
            shared = beside((turned[own, queries] * inverse).astype(BF16), h)
            grads[:, cols] = shared
            grads_up[cols, :] = shared.T
            lane = lax.broadcasted_iota(jnp.int32, (queries.stop - queries.start, PAIR), 1)
            ques_up[cols, :] = jnp.where(lane // HDIM == h, q_ref[queries, :], jnp.zeros((), BF16))
        for held in (total, key_sum, value_sum):
            held[...] = jnp.zeros_like(held)

    here = pl.ds(pl.multiple_of(units[0, step] * block, block), block)
    there = pl.multiple_of(units[1, step] * part, part)
    cols = pl.ds(there, part)
    values = v_ref[here, :]
    for start in range(0, part, chunk):
        own = slice(start, start + chunk)
        from_all = pl.ds(there + start, chunk)
        change = jnp.dot(values, grads[:, from_all], preferred_element_type=F32)
        low[:, own] = (p_ref[0, :, own].astype(F32) * (change - delta[:, from_all])).astype(BF16)
    value_sum[here, :] += jnp.dot(p_ref[0], grads_up[cols, :], preferred_element_type=F32)
    key_sum[here, :] += jnp.dot(low[...], ques_up[cols, :], preferred_element_type=F32)
    total[:, cols] += jnp.dot(keys[:, here], low[...], preferred_element_type=F32)

    @pl.when(step == pl.num_programs(1) - 1)
    def finish():
        live = live_rows((kv, PAIR), 0, 0, info[0], info[1], span)
        zero = jnp.zeros((), F32)
        found = [jnp.where(live, key_sum[...] * scale, zero), jnp.where(live, value_sum[...], zero)]
        for t, (ref, value) in enumerate(zip((gk_ref, gv_ref), found)):
            if more:
                value += before[t + 1][...].astype(F32)
            ref[...] = value.astype(BF16)
        parts = [[], []]
        for h, queries, cols in segments(rows, size):
            parts[h].append(total[head_rows(h), cols])
        value = (jnp.concatenate([jnp.concatenate(p, 1) for p in parts], 0) * scale).T
        if more:
            value += before[0][...].astype(F32)
        gq_ref[...] = value.astype(BF16)


def attend_back(info, sources, grad, context, sums, probs, span, units, before, events=()):
    (queries, q_at), (keys, k_at), (values, v_at) = sources
    rows, kv = queries.shape[0], keys.shape[0]
    pairs = HEADS // 2
    wide = HEADS * HDIM
    more = before is not None
    block, part, size = min(1024, kv), rows, chunk_of(rows)
    cut = 2 if more else 1
    rows, kv = rows // cut, kv // cut
    out_rows = [rows, kv, kv]
    heights = [rows * cut, kv * cut, kv * cut]
    units = jnp.array(list(zip(*units)), jnp.int32)
    col = lambda height, at=lambda j: j: pl.BlockSpec(
        (height, PAIR), lambda j, c, s, u: (0, at(j))
    )
    return pl.pallas_call(
        functools.partial(
            attend_back_kernel,
            chunk=min(512, part),
            size=size,
            span=span,
            more=more,
            extra=len(events),
        ),
        out_shape=tuple(jax.ShapeDtypeStruct((height, wide), BF16) for height in heights),
        grid_spec=pltpu.PrefetchScalarGridSpec(
            num_scalar_prefetch=2,
            grid=(pairs, units.shape[1]),
            in_specs=[
                col(rows, q_at),
                col(kv, k_at),
                col(kv, v_at),
                col(rows),
                col(rows),
                pl.BlockSpec((1, 1, 2 * rows), lambda j, c, s, u: (j, 0, 0)),
                pl.BlockSpec((1, block, part), lambda j, c, s, u: (j, u[0, c], u[1, c])),
            ]
            + ([col(height) for height in out_rows] if more else [])
            + any_specs(events),
            out_specs=tuple(col(height) for height in out_rows),
            scratch_shapes=[
                pltpu.VMEM((PAIR, kv), BF16),
                pltpu.VMEM((PAIR, 2 * rows), BF16),
                pltpu.VMEM((2 * rows, PAIR), BF16),
                pltpu.VMEM((2 * rows, PAIR), BF16),
                pltpu.VMEM((1, 2 * rows), F32),
                pltpu.VMEM((block, part), BF16),
                pltpu.VMEM((PAIR, 2 * rows), F32),
                pltpu.VMEM((kv, PAIR), F32),
                pltpu.VMEM((kv, PAIR), F32),
            ],
        ),
        input_output_aliases={9 + t: t for t in range(3)} if more else {},
        compiler_params=pltpu.CompilerParams(vmem_limit_bytes=60 * 2**20),
        name="attend_back_last" if more else "attend_back",
    )(info, units, queries, keys, values, grad, context, sums, probs, *(before or ()), *events)


def rows_of(kept_ref, other_ref, step, split):
    return jnp.where(step < split, kept_ref[0], other_ref[...])


def project(rows, weight):
    return jnp.dot(rows, weight, preferred_element_type=F32)


def project_back(grads, weight):
    return lax.dot_general(grads, weight, (((1,), (1,)), ((), ())), preferred_element_type=F32)


def weight_grad(rows, grads):
    return lax.dot_general(rows, grads, (((0,), (0,)), ((), ())), preferred_element_type=F32)


def run_all(copies):
    for copy in copies:
        copy.start()
    return copies


def wait_all(copies):
    for copy in copies:
        copy.wait()


class Pieces:
    def __init__(self, shape, mesh_shape, bundles):
        self.r, self.c = shape
        self.m, self.n = mesh_shape
        self.bundles = bundles
        self.slots = self.m * self.n

    def place(self, masks, slot, info):
        if masks is None:
            return slot // self.n, lax.rem(slot, self.n)
        return info[5] ^ (masks[slot] // self.n), info[6] ^ (masks[slot] % self.n)

    def copies(self, refs, mats, sems, info, out):
        found = [[] for _ in mats]
        r, c = self.r, self.c
        count = 0
        for (masks, members), ref in zip(self.bundles, refs):
            for slot in range(self.slots if masks is None else len(masks)):
                j, i = self.place(masks, slot, info)
                at = 0
                for t in members:
                    mat = mats[t]
                    tall = mat.shape[0] // (self.m * r)
                    wide = mat.shape[1] // (self.n * c)
                    for w in range(wide):
                        if isinstance(ref, (tuple, list)):
                            each = self.slots // len(ref)
                            block = ref[slot // each].at[slot % each, pl.ds(at, tall * r), :]
                        else:
                            block = ref.at[slot, pl.ds(at, tall * r), :]
                        down = pl.multiple_of(j * (tall * r), tall * r)
                        side = pl.multiple_of((i * wide + w) * c, c)
                        place = mat.at[pl.ds(down, tall * r), pl.ds(side, c)]
                        at += tall * r
                        pair = (place, block) if out else (block, place)
                        found[t].append(pltpu.make_async_copy(*pair, sems.at[count]))
                        count += 1
        return found

    def count(self):
        return 9 * self.slots


def any_specs(arrays):
    return [pl.BlockSpec(memory_space=pl.ANY)] * len(arrays)


def queries_kernel(info, kept_ref, other_ref, bias_ref, *rest, split, grid_of, carry):
    count = len(grid_of.bundles)
    packed, rest = rest[:count], rest[count:]
    step = pl.program_id(0)
    if carry:
        pair_ref, out_ref, mat_q, mat_k, mat_v, picked, sems = rest
        picked[...] = pair_ref[0]
    else:
        out_ref, mat_q, mat_k, mat_v, sems = rest
    mats = [mat_q, mat_k, mat_v]

    @pl.when(step == 0)
    def load():
        loads = grid_of.copies(packed, mats, sems, info, False)
        for group in loads:
            run_all(group)
        for group in loads:
            wait_all(group)

    rows = rows_of(kept_ref, other_ref, step, split)
    width = mat_q.shape[1]
    for t, mat in enumerate(mats):
        cols = slice(t * width, (t + 1) * width)
        out_ref[:, cols] = (project(rows, mat[...]) + bias_ref[:, cols]).astype(BF16)


def split_specs(kept_at, tile, split, width):
    return [
        pl.BlockSpec((1, tile, width), lambda i, s: (s[kept_at], jnp.minimum(i, split - 1), 0)),
        pl.BlockSpec((tile, width), lambda i, s: (jnp.maximum(i - split, 0), 0)),
    ]


def whole_spec(shape):
    return pl.BlockSpec(shape, lambda i, s: (0,) * len(shape))


def queries_keys_values(info, kept, other, weights, bias, pair):
    block_len, width = other.shape
    tile = min(512, block_len)
    split = block_len // tile
    part = block_len // (2 * split)
    carried = [] if pair is None else [pair]
    mat = jax.ShapeDtypeStruct((width, width), BF16)
    return pl.pallas_call(
        functools.partial(
            queries_kernel, split=split, grid_of=weights.grid_of, carry=bool(carried)
        ),
        out_shape=(jax.ShapeDtypeStruct((2 * block_len, 3 * width), BF16), mat, mat, mat)
        + (jax.ShapeDtypeStruct((block_len, width), BF16),) * len(carried),
        grid_spec=pltpu.PrefetchScalarGridSpec(
            num_scalar_prefetch=1,
            grid=(2 * split,),
            in_specs=split_specs(2, tile, split, width)
            + [whole_spec(bias.shape)]
            + any_specs(weights.packed)
            + [pl.BlockSpec((1, part, width), lambda i, s: (1 - s[2], i, 0))] * len(carried),
            out_specs=(pl.BlockSpec((tile, 3 * width), lambda i, s: (i, 0)),)
            + (whole_spec(mat.shape),) * 3
            + (pl.BlockSpec((part, width), lambda i, s: (i, 0)),) * len(carried),
            scratch_shapes=[pltpu.SemaphoreType.DMA((weights.grid_of.count(),))],
        ),
        compiler_params=pltpu.CompilerParams(vmem_limit_bytes=60 * 2**20),
        name="queries",
    )(info, kept, other, bias, *weights.packed, *carried)


def normal(values):
    middle = jnp.mean(values, axis=-1, keepdims=True)
    centered = values - middle
    spread = jnp.mean(centered * centered, axis=-1, keepdims=True)
    inverse = lax.rsqrt(spread + 1e-12)
    return centered * inverse, inverse


def normal_back(grad, unit, inverse, gain):
    scaled = grad * gain
    mean = jnp.mean(scaled, axis=-1, keepdims=True)
    along = jnp.mean(scaled * unit, axis=-1, keepdims=True)
    return (scaled - mean - unit * along) * inverse


def gelu_pair(u):
    phi = 0.5 + 0.5 * lax.erf(0.7071067811865476 * u)
    bell = jnp.exp2((-0.5 * LOG2E) * (u * u))
    return u * phi, phi + (0.3989422804014327 * u) * bell


def add_rows(total, at, values):
    total[at : at + 1, 0 : values.shape[1]] += jnp.sum(values, axis=0, keepdims=True)


def middle_kernel(
    info,
    hid_kept,
    hid_other,
    cot_kept,
    cot_other,
    ctx_ref,
    cls_ref,
    vec_ref,
    inner_bias,
    packed,
    layer_kept,
    layer_other,
    top_ref,
    grad_ctx_ref,
    resid_ref,
    sums_ref,
    mat_out,
    mat_inner,
    mat_outer,
    acc_out,
    acc_inner,
    acc_outer,
    totals,
    active,
    slope,
    low,
    vec_low,
    sems,
    vec_sems,
    *,
    split,
    grid_of,
    chunk,
):
    step = pl.program_id(0)
    last = pl.num_programs(0) - 1
    mats = [mat_out, mat_inner, mat_outer]
    tile, width = ctx_ref.shape
    ff = mat_inner.shape[1]
    loads = grid_of.copies([packed], mats, sems, info, False)

    @pl.when(step == 0)
    def start():
        for group in loads:
            run_all(group)
        for acc in (acc_out, acc_inner, acc_outer, totals):
            acc[...] = jnp.zeros_like(acc)
        wait_all(loads[0])

    bias_out, gain_one, shift_one, bias_outer, gain_two, shift_two = [
        vec_ref[t : t + 1, :] for t in range(6)
    ]
    hidden = rows_of(hid_kept, hid_other, step, split).astype(F32)
    context = ctx_ref[...]
    unit_one, inverse_one = normal(hidden + project(context, mat_out[...]) + bias_out)
    normed = unit_one * gain_one + shift_one
    normed_low = normed.astype(BF16)

    @pl.when(step == 0)
    def more():
        wait_all(loads[1])
        wait_all(loads[2])

    for at in range(0, ff, chunk):
        cols = slice(at, at + chunk)
        inner = project(normed_low, mat_inner[:, cols]) + inner_bias[:, cols]
        value, change = gelu_pair(inner)
        active[:, cols] = value.astype(BF16)
        slope[:, cols] = change.astype(BF16)
    unit_two, inverse_two = normal(normed + project(active[...], mat_outer[...]) + bias_outer)
    layer = (unit_two * gain_two + shift_two).astype(BF16)

    @pl.when(step < split)
    def kept():
        layer_kept[0] = layer

    @pl.when(step >= split)
    def other():
        layer_other[...] = layer

    @pl.when(step * tile == info[1])
    def top():
        top_ref[...] = layer[0:16, :]


    row = step * tile + lax.broadcasted_iota(jnp.int32, (tile, width), 0)
    grad_result = rows_of(cot_kept, cot_other, step, split).astype(F32)
    grad_result += jnp.where(row == info[4], cls_ref[...], 0.0)
    add_rows(totals, 4, grad_result * unit_two)
    add_rows(totals, 5, grad_result)
    grad_resid_two = normal_back(grad_result, unit_two, inverse_two, gain_two)
    grad_outer = grad_resid_two.astype(BF16)
    add_rows(totals, 3, grad_outer.astype(F32))
    for at in range(0, ff, chunk):
        cols = slice(at, at + chunk)
        grad_inner = project_back(grad_outer, mat_outer[cols, :]) * slope[:, cols].astype(F32)
        low[:, cols] = grad_inner.astype(BF16)
        totals[8:9, cols] += jnp.sum(grad_inner, axis=0, keepdims=True)
        acc_outer[cols, :] += weight_grad(active[:, cols], grad_outer)
    grad_normed = grad_resid_two + project_back(low[...], mat_inner[...])
    for at in range(0, ff, chunk):
        cols = slice(at, at + chunk)
        acc_inner[:, cols] += weight_grad(normed_low, low[:, cols])
    add_rows(totals, 1, grad_normed * unit_one)
    add_rows(totals, 2, grad_normed)
    grad_resid_one = normal_back(grad_normed, unit_one, inverse_one, gain_one)
    resid_ref[...] = grad_resid_one
    grad_attn = grad_resid_one.astype(BF16)
    add_rows(totals, 0, grad_attn.astype(F32))
    acc_out[...] += weight_grad(context, grad_attn)
    grad_ctx_ref[...] = project_back(grad_attn, mat_out[...]).astype(BF16)

    @pl.when(step == last)
    def finish():
        r, c, m, n = grid_of.r, grid_of.c, grid_of.m, grid_of.n
        stores = grid_of.copies([sums_ref], mats, sems, info, True)
        for mat, acc, group in zip(mats, (acc_out, acc_inner, acc_outer), stores):
            mat[...] = acc[...].astype(BF16)
            run_all(group)
        vec_low[...] = jnp.zeros_like(vec_low)
        for i in range(n):
            for t in range(6):
                vec_low[i, t : t + 1, :] = totals[t : t + 1, i * c : (i + 1) * c]
            wide = ff // (n * c)
            for t in range(wide):
                at = (i * wide + t) * c
                vec_low[i, 6 + t : 7 + t, :] = totals[8:9, at : at + c]
        tails = []
        vec_bits = vec_low[...].astype(BF16)
        for i in range(n):
            active[16 * i : 16 * i + 16, 0:c] = vec_bits[i]
        for j in range(m):
            for i in range(n):
                tails.append(
                    pltpu.make_async_copy(
                        active.at[pl.ds(16 * i, 16), pl.ds(0, c)],
                        sums_ref.at[j * n + i, pl.ds(9 * r, 16), :],
                        vec_sems.at[j * n + i],
                    )
                )
        run_all(tails)
        for group in stores:
            wait_all(group)
        wait_all(tails)


def kept_spec(tile, split, width):
    return pl.BlockSpec((1, tile, width), lambda i, s: (s[2], jnp.minimum(i, split - 1), 0))


def other_spec(tile, split, width):
    return pl.BlockSpec((tile, width), lambda i, s: (jnp.maximum(i - split, 0), 0))


def middle(info, hidden, cots, context, cls_row, weights, vectors, inner_bias):
    block_len, width = hidden[1].shape
    grid_of = weights.grid_of
    ff = inner_bias.shape[1]
    tile = min(256, block_len)
    split = block_len // tile
    row_spec = pl.BlockSpec((tile, width), lambda i, s: (i, 0))
    return pl.pallas_call(
        functools.partial(middle_kernel, split=split, grid_of=grid_of, chunk=768),
        out_shape=(
            jax.ShapeDtypeStruct(hidden[0].shape, BF16),
            jax.ShapeDtypeStruct((block_len, width), BF16),
            jax.ShapeDtypeStruct((16, width), BF16),
            jax.ShapeDtypeStruct((2 * block_len, width), BF16),
            jax.ShapeDtypeStruct((2 * block_len, width), F32),
            jax.ShapeDtypeStruct((grid_of.slots, 9 * grid_of.r + 16, grid_of.c), BF16),
        ),
        grid_spec=pltpu.PrefetchScalarGridSpec(
            num_scalar_prefetch=1,
            grid=(2 * split,),
            in_specs=split_specs(2, tile, split, width)
            + split_specs(2, tile, split, width)
            + [
                row_spec,
                whole_spec(cls_row.shape),
                whole_spec(vectors.shape),
                whole_spec(inner_bias.shape),
                pl.BlockSpec(memory_space=pl.ANY),
            ],
            out_specs=(
                kept_spec(tile, split, width),
                other_spec(tile, split, width),
                whole_spec((16, width)),
                row_spec,
                row_spec,
                pl.BlockSpec(memory_space=pl.ANY),
            ),
            scratch_shapes=[
                pltpu.VMEM((width, width), BF16),
                pltpu.VMEM((width, ff), BF16),
                pltpu.VMEM((ff, width), BF16),
                pltpu.VMEM((width, width), F32),
                pltpu.VMEM((width, ff), F32),
                pltpu.VMEM((ff, width), F32),
                pltpu.VMEM((16, ff), F32),
                pltpu.VMEM((tile, ff), BF16),
                pltpu.VMEM((tile, ff), BF16),
                pltpu.VMEM((tile, ff), BF16),
                pltpu.VMEM((grid_of.n, 16, grid_of.c), F32),
                pltpu.SemaphoreType.DMA((grid_of.count(),)),
                pltpu.SemaphoreType.DMA((grid_of.slots,)),
            ],
        ),
        compiler_params=pltpu.CompilerParams(vmem_limit_bytes=60 * 2**20),
        name="middle",
    )(info, *hidden, *cots, context, cls_row, vectors, inner_bias, *weights.packed)


def input_grad_kernel(info, gq_ref, gk_ref, gv_ref, resid_ref, mat_q, mat_k, mat_v, *rest, kept, join):
    if join:
        arrived, grad_ref, joined = rest[0], rest[-2], rest[-1]
        joined[0] = arrived[...].astype(joined.dtype)
    else:
        grad_ref = rest[-1]
    total = resid_ref[...]
    for ref, mat in zip((gq_ref, gk_ref, gv_ref), (mat_q, mat_k, mat_v)):
        total += project_back(ref[...], mat[...])
    if kept:
        grad_ref[0] = total.astype(grad_ref.dtype)
    else:
        grad_ref[...] = total.astype(grad_ref.dtype)


def input_grad(info, grads, resid, mats, out_shape, dtype, kept, join=(), events=()):
    rows, width = resid.shape
    block_len = rows // 2
    tile = min(512, block_len)
    split = block_len // tile
    off = 0 if kept else split
    spec = pl.BlockSpec((tile, width), lambda i, s: (i + off, 0))
    place = kept_spec(tile, split, width) if kept else other_spec(tile, 0, width)
    out = (jax.ShapeDtypeStruct(out_shape, dtype),)
    in_specs = [spec] * 4 + [whole_spec(mat.shape) for mat in mats]
    out_specs = (place,)
    aliases = {}
    if join:
        in_specs += [pl.BlockSpec((tile, width), lambda i, s: (i, 0))] + any_specs(join[:1])
        out += (jax.ShapeDtypeStruct(join[0].shape, join[0].dtype),)
        out_specs += (pl.BlockSpec((1, tile, width), lambda i, s: (1 - s[2], i, 0)),)
        aliases = {len(in_specs): 1}
    return pl.pallas_call(
        functools.partial(input_grad_kernel, kept=kept, join=bool(join)),
        out_shape=out,
        grid_spec=pltpu.PrefetchScalarGridSpec(
            num_scalar_prefetch=1,
            grid=(split,),
            in_specs=in_specs + any_specs(events),
            out_specs=out_specs,
        ),
        input_output_aliases=aliases,
        compiler_params=pltpu.CompilerParams(vmem_limit_bytes=60 * 2**20),
        name="input_grad_kept" if kept else "input_grad_other",
    )(info, *grads, resid, *mats, *join[::-1], *events)


def head_grads_kernel(info, hid_kept, hid_other, *rest, split, grid_of, outs, extra):
    found, rest = rest[:3], rest[3 + extra :]
    sums, (acc, mat_q, mat_k, mat_v, totals, vec_low, sems, vec_sems) = rest[:outs], rest[outs:]
    mats = [mat_q, mat_k, mat_v]
    step = pl.program_id(0)

    @pl.when(step == 0)
    def clear():
        acc[...] = jnp.zeros_like(acc)
        totals[...] = jnp.zeros_like(totals)

    rows = rows_of(hid_kept, hid_other, step, split)
    grads = [ref[...] for ref in found]
    for t, grad in enumerate(grads):
        acc[t] += weight_grad(rows, grad)
    add_rows(totals, 0, grads[0].astype(F32))
    add_rows(totals, 1, grads[2].astype(F32))

    @pl.when(step == pl.num_programs(0) - 1)
    def finish():
        r, c, n = grid_of.r, grid_of.c, grid_of.n
        ((masks, _),) = grid_of.bundles
        stores = grid_of.copies([list(sums)], mats, sems, info, True)
        for t, mat in enumerate(mats):
            mat[...] = acc[t].astype(BF16)
            run_all(stores[t])
        for i in range(n):
            part = jnp.concatenate([totals[0:2, i * c : (i + 1) * c], jnp.zeros((14, c), F32)], 0)
            vec_low[i] = part.astype(BF16)
        tails = []
        each = grid_of.slots // outs
        for slot in range(grid_of.slots):
            j, i = grid_of.place(masks, slot, info)
            place = sums[slot // each].at[slot % each, pl.ds(3 * r, 16), :]
            tails.append(pltpu.make_async_copy(vec_low.at[i], place, vec_sems.at[slot]))
        run_all(tails)
        for group in stores:
            wait_all(group)
        wait_all(tails)


def head_grads(info, hidden, grads, grid_of, outs, events=()):
    block_len, width = hidden[1].shape
    tile = min(512, block_len)
    split = block_len // tile
    rows = pl.BlockSpec((tile, width), lambda i, s: (i, 0))
    block = (grid_of.slots // outs, 3 * grid_of.r + 16, grid_of.c)
    return pl.pallas_call(
        functools.partial(
            head_grads_kernel, split=split, grid_of=grid_of, outs=outs, extra=len(events)
        ),
        out_shape=(jax.ShapeDtypeStruct(block, BF16),) * outs,
        grid_spec=pltpu.PrefetchScalarGridSpec(
            num_scalar_prefetch=1,
            grid=(2 * split,),
            in_specs=split_specs(2, tile, split, width) + [rows] * 3 + any_specs(events),
            out_specs=(pl.BlockSpec(memory_space=pl.ANY),) * outs,
            scratch_shapes=[pltpu.VMEM((3, width, width), F32)]
            + [pltpu.VMEM((width, width), BF16)] * 3
            + [
                pltpu.VMEM((8, width), F32),
                pltpu.VMEM((grid_of.n, 16, grid_of.c), BF16),
                pltpu.SemaphoreType.DMA((grid_of.count(),)),
                pltpu.SemaphoreType.DMA((grid_of.slots,)),
            ],
        ),
        compiler_params=pltpu.CompilerParams(vmem_limit_bytes=60 * 2**20),
        name="head_grads",
    )(info, *hidden, *grads, *events)


def pick_kernel(info, pair_ref, *rest):
    rest[-1][...] = pair_ref[0]


def pick_other(info, pair, events):
    _, block_len, width = pair.shape
    tile = min(512, block_len)
    return pl.pallas_call(
        pick_kernel,
        out_shape=jax.ShapeDtypeStruct((block_len, width), pair.dtype),
        grid_spec=pltpu.PrefetchScalarGridSpec(
            num_scalar_prefetch=1,
            grid=(block_len // tile,),
            in_specs=[pl.BlockSpec((1, tile, width), lambda i, s: (1 - s[2], i, 0))]
            + any_specs(events),
            out_specs=pl.BlockSpec((tile, width), lambda i, s: (i, 0)),
        ),
        compiler_params=pltpu.CompilerParams(vmem_limit_bytes=60 * 2**20),
        name="pick_other",
    )(info, pair, *events)


def pack_kernel(*refs, count):
    out = refs[-1]
    c = out.shape[1]
    at = 0
    for ref in refs[:count]:
        rows, cols = ref.shape
        for start in range(0, cols, c):
            out[at : at + rows, :] = ref[:, start : start + c]
            at += rows


def pack_after(shards, events):
    c = min(s.shape[1] for s in shards)
    rows = sum(s.size for s in shards) // c
    return pl.pallas_call(
        functools.partial(pack_kernel, count=len(shards)),
        out_shape=jax.ShapeDtypeStruct((rows, c), BF16),
        in_specs=[pl.BlockSpec(memory_space=pltpu.VMEM)] * len(shards) + any_specs(events),
        compiler_params=pltpu.CompilerParams(vmem_limit_bytes=60 * 2**20),
        name="pack",
    )(*shards, *events)


def stack_kernel(*refs, count, outs):
    at = 0
    for out in refs[-outs:]:
        rows = out.shape[1]
        for k, ref in enumerate(refs[:count]):
            out[k] = ref[at : at + rows, :]
        at += rows


def stack_rows(blocks, cuts, events):
    c = blocks[0].shape[1]
    return pl.pallas_call(
        functools.partial(stack_kernel, count=len(blocks), outs=len(cuts)),
        out_shape=tuple(jax.ShapeDtypeStruct((len(blocks), rows, c), BF16) for rows in cuts),
        in_specs=[pl.BlockSpec(memory_space=pltpu.VMEM)] * len(blocks) + any_specs(events),
        compiler_params=pltpu.CompilerParams(vmem_limit_bytes=60 * 2**20),
        name="stack_rows",
    )(*blocks, *events)


def join_kernel(*refs, count):
    out = refs[-1]
    each = refs[0].shape[0]
    for k, ref in enumerate(refs[:count]):
        out[k * each : (k + 1) * each] = ref[...]


def join_blocks(parts, events):
    shape = (parts[0].shape[0] * len(parts),) + parts[0].shape[1:]
    return pl.pallas_call(
        functools.partial(join_kernel, count=len(parts)),
        out_shape=jax.ShapeDtypeStruct(shape, BF16),
        in_specs=[pl.BlockSpec(memory_space=pltpu.VMEM)] * len(parts) + any_specs(events),
        compiler_params=pltpu.CompilerParams(vmem_limit_bytes=60 * 2**20),
        name="join_blocks",
    )(*parts, *events)


def add_kernel(*refs, count, extra):
    parts, outs = refs[:count], refs[count + extra :]
    each = outs[0].shape[0]
    for k, out in enumerate(outs):
        here = slice(k * each, (k + 1) * each)
        out[...] = sum(part[here].astype(F32) for part in parts).astype(BF16)


def add_blocks(parts, groups, events):
    shape = (parts[0].shape[0] // groups,) + parts[0].shape[1:]
    return pl.pallas_call(
        functools.partial(add_kernel, count=len(parts), extra=len(events)),
        out_shape=(jax.ShapeDtypeStruct(shape, BF16),) * groups,
        in_specs=[pl.BlockSpec(memory_space=pltpu.VMEM)] * len(parts) + any_specs(events),
        compiler_params=pltpu.CompilerParams(vmem_limit_bytes=60 * 2**20),
        name="add_blocks",
    )(*parts, *events)


def place_kernel(info, base_ref, other_ref, out_ref):
    out_ref[0] = other_ref[...].astype(out_ref.dtype)


def place_other(info, base, other):
    block_len, width = other.shape
    tile = min(512, block_len)
    return pl.pallas_call(
        place_kernel,
        out_shape=jax.ShapeDtypeStruct(base.shape, base.dtype),
        grid_spec=pltpu.PrefetchScalarGridSpec(
            num_scalar_prefetch=1,
            grid=(block_len // tile,),
            in_specs=[
                pl.BlockSpec(memory_space=pl.ANY),
                pl.BlockSpec((tile, width), lambda i, s: (i, 0)),
            ],
            out_specs=pl.BlockSpec((1, tile, width), lambda i, s: (1 - s[2], i, 0)),
        ),
        input_output_aliases={1: 0},
        compiler_params=pltpu.CompilerParams(vmem_limit_bytes=60 * 2**20),
        name="place_other",
    )(info, base, other)


def swap(block, axis, route):
    if all(a == b for a, b in route):
        return block
    return lax.ppermute(block, axis, route)


class Regroup:
    def __init__(self):
        self.n = lax.axis_size("blk")
        self.me = lax.axis_index("blk")
        self.per = self.n // 2
        self.passage = self.me // self.per
        self.part = lax.rem(self.me, 2)
        self.first = [(i, (i % 2) * self.per + i // 2) for i in range(self.n)]
        self.second = [(i, (1 - i % 2) * self.per + i // 2) for i in range(self.n)]
        self.stays = all(a == b for a, b in self.first)

    def pick(self, pair):
        return lax.dynamic_index_in_dim(pair, 1 - self.part, 0, keepdims=False)

    def gather(self, pair, picked):
        other = swap(picked, "blk", self.second)
        if self.stays:
            return (pair, other)
        kept = lax.dynamic_index_in_dim(pair, self.part, 0, keepdims=True)
        return (swap(kept, "blk", self.first), other)

    def kept_index(self):
        return self.part if self.stays else jnp.zeros_like(self.part)

    def all_blocks(self, block):
        if self.n != 2:
            return lax.all_gather(block, "blk", axis=0)
        other = lax.ppermute(block, "blk", [(0, 1), (1, 0)])
        return jnp.where(self.me == 0, jnp.stack([block, other]), jnp.stack([other, block]))

    def send_back(self, other):
        return swap(other, "blk", [(b, a) for a, b in self.second])

    def join(self, info, kept, other):
        if self.stays:
            return place_other(info, kept, other)
        kept = swap(kept[0], "blk", [(b, a) for a, b in self.first])
        other = other.astype(kept.dtype)
        return jnp.where(self.part == 0, jnp.stack([kept, other]), jnp.stack([other, kept]))


def pack(shards):
    c = min(s.shape[1] for s in shards)
    return jnp.concatenate(
        [s[:, at : at + c] for s in shards for at in range(0, s.shape[1], c)], axis=0
    )


def unpack(block, shapes):
    c = block.shape[-1]
    found, at = [], 0
    for rows, cols in shapes:
        parts = []
        for _ in range(cols // c):
            parts.append(block[..., at : at + rows, :])
            at += rows
        found.append(jnp.concatenate(parts, axis=-1) if len(parts) > 1 else parts[0])
    return found


def exchanged(block, mask):
    both = ("batch", "blk")
    places = range(lax.axis_size("batch") * lax.axis_size("blk"))
    return lax.ppermute(block, both, [(i, i ^ mask) for i in places])


def xor_gather(found, masks, stage, events):
    parts = [found] + [exchanged(found, mask) for mask in stage]
    masks = [held ^ mask for mask in [0] + stage for held in masks]
    return join_blocks(parts, events), masks


def xor_masks(stages):
    masks = [0]
    for stage in stages:
        masks = [held ^ mask for held in masks for mask in [0] + stage]
    return masks


def xor_sum(groups, stages, meanwhile):
    for at, stage in enumerate(stages):
        parts = [groups[0]] + [exchanged(g, mask) for mask, g in zip(stage, groups[1:])]
        if at == len(stages) - 1:
            return [part[0] for part in parts]
        events = meanwhile if at == len(stages) - 2 else ()
        groups = add_blocks(parts, len(stages[at + 1]) + 1, events)


class Weights:
    def __init__(self, shards, begin=None):
        self.shapes = [s.shape for s in shards]
        self.m, self.n = lax.axis_size("batch"), lax.axis_size("blk")
        m, n = self.m, self.n
        r, c = min(s[0] for s in self.shapes), min(s[1] for s in self.shapes)
        self.fits = r % 16 == 0 and c % 128 == 0
        powers = m & (m - 1) == 0 and n == 2 and m >= 8
        self.by_pairs = begin is not None and self.fits and powers
        every = list(range(len(shards)))
        if self.by_pairs:
            y, core, x = list(range(1, n)), [n], [2 * n]
            z = list(range(4 * n, m * n, 4 * n))
            near = pack_after(shards, ())
            near = [near] + [exchanged(near, mask) for mask in y]
            cut = sum(s.size for s in shards[:-1]) // c
            cuts = [cut, shards[-1].size // c]
            picked, arrival = begin(near[1:])
            most, least = stack_rows(near, cuts, (picked,))
            flat = lambda part: part.reshape(-1, *part.shape[-2:])
            first = [0] + y
            b, b_masks = xor_gather(flat(least), first, x, ())
            a, a_masks = xor_gather(flat(most), first, z, (b,))
            b, b_masks = xor_gather(b, b_masks, z, ())
            a, a_masks = xor_gather(a, a_masks, x, (arrival, b))
            self.packed, bundles = [], []
            for part, masks, members in ((a, a_masks, every[:-1]), (b, b_masks, every[-1:])):
                for mask in [0] + core:
                    self.packed.append(exchanged(part, mask) if mask else part)
                    bundles.append(([held ^ mask for held in masks], members))
            self.grid_of = Pieces((r, c), (m, n), bundles)
            self.stages = [core, [a ^ b for a in [0] + x for b in [0] + y][1:], z]
            self.sums_of = Pieces((r, c), (m, n), [(xor_masks(self.stages), every)])
            return
        packed = pack_after(shards, ()) if self.fits else pack(shards)
        packed = lax.all_gather(packed, ("batch", "blk"), axis=0)
        if self.fits:
            self.grid_of = Pieces((r, c), (m, n), [(None, every)])
            self.packed = [packed]
        else:
            self.grid_of = Pieces((r * m, c * n), (1, 1), [(None, every)])
            whole = []
            for part in unpack(packed, self.shapes):
                rows, cols = part.shape[1:]
                part = part.reshape(m, n, rows, cols).transpose(0, 2, 1, 3)
                whole.append(part.reshape(m * rows, n * cols))
            self.packed = [pack(whole)[None]]
        self.sums_of = self.grid_of

    def scatter(self, sums, meanwhile=()):
        extra = 16
        if self.by_pairs:
            return finish_sums(xor_sum(sums, self.stages, meanwhile), self.shapes)
        (sums,) = sums
        if not self.fits:
            rows = sums.shape[1] - extra
            wide = [(a * self.m, b * self.n) for a, b in self.shapes]
            parts = []
            for part in unpack(sums[0, :rows], wide):
                a, b = part.shape[0] // self.m, part.shape[1] // self.n
                part = part.reshape(self.m, a, self.n, b).transpose(0, 2, 1, 3)
                parts.append(part.reshape(self.m * self.n, a, b))
            c = min(s[1] for s in self.shapes)
            blocks = jnp.stack([pack([p[d] for p in parts]) for d in range(self.m * self.n)])
            vecs = sums[0, rows:].reshape(extra, self.n, c).transpose(1, 0, 2)
            vecs = jnp.broadcast_to(vecs[None], (self.m, self.n, extra, c))
            sums = jnp.concatenate([blocks, vecs.reshape(self.m * self.n, extra, c)], axis=1)
        height, c = sums.shape[1:]
        own = lax.psum_scatter(
            sums.reshape(-1, c), ("batch", "blk"), scatter_dimension=0, tiled=True
        )
        return finish_sums([own], self.shapes)


def finish_kernel(*refs, count):
    parts, outs = refs[:count], refs[count:]
    at = 0
    for out in outs:
        rows, cols = out.shape
        c = parts[0].shape[1]
        for start in range(0, cols, c):
            here = slice(at, at + rows)
            out[:, start : start + c] = sum(part[here, :].astype(F32) for part in parts)
            at += rows


def finish_sums(parts, shapes):
    height, c = parts[0].shape
    used = sum(a * b for a, b in shapes) // c
    shapes = list(shapes) + [(height - used, c)]
    if used % 16:
        total = sum(part.astype(F32) for part in parts)
        return [*unpack(total[:used], shapes[:-1]), total[used:]]
    return pl.pallas_call(
        functools.partial(finish_kernel, count=len(parts)),
        out_shape=tuple(jax.ShapeDtypeStruct(shape, F32) for shape in shapes),
        compiler_params=pltpu.CompilerParams(vmem_limit_bytes=60 * 2**20),
        name="finish_sums",
    )(*parts)


def on_device(
    hidden_in,
    lengths,
    cot_out,
    cot_cls,
    w_query,
    w_key,
    w_value,
    w_out,
    w_inner,
    w_outer,
    b_query,
    b_value,
    b_out,
    norm1_gain,
    norm1_shift,
    b_inner,
    b_outer,
    norm2_gain,
    norm2_shift,
):
    plan = Regroup()
    groups, block_len, width = hidden_in.shape
    span = groups * block_len
    per = plan.per
    fleets = [[i * per + j for j in range(per)] for i in range(2)]
    first_row = plan.passage * block_len
    owner = lax.rem(plan.me, per) == 0

    length = lax.dynamic_index_in_dim(lengths, plan.passage, 0, keepdims=False)
    info = jnp.stack(
        [
            length,
            first_row,
            plan.kept_index(),
            plan.kept_index(),
            jnp.where(owner, first_row, -1),
            lax.axis_index("batch"),
            plan.me,
        ]
    ).astype(jnp.int32)

    share = width // plan.n
    narrow = jnp.stack(
        [b_query, b_value, b_out, norm1_gain, norm1_shift, b_outer, norm2_gain, norm2_shift]
    )
    parts = [narrow, b_inner.reshape(-1, share)]
    used = narrow.shape[0] + parts[1].shape[0]
    parts.append(jnp.zeros((-used % 16, share), BF16))
    vec_shard = jnp.concatenate(parts, 0)

    hidden = None

    def begin(near):
        nonlocal hidden
        picked = pick_other(info, hidden_in, near)
        hidden = plan.gather(hidden_in, picked)
        return picked, hidden[1]

    heads = Weights([w_query, w_key, w_value], begin if plan.stays else None)
    if hidden is None:
        hidden = plan.gather(hidden_in, plan.pick(hidden_in))
    if heads.by_pairs:
        vec_shard = pack_after([vec_shard], hidden[1:])
    vec_all = plan.all_blocks(vec_shard)
    dense = Weights([w_out, w_inner, w_outer])
    narrow = vec_all[:, :8].transpose(1, 0, 2).reshape(8, width).astype(F32)
    bias_inner = vec_all[:, 8:used].reshape(1, -1).astype(F32)
    bias_heads = jnp.concatenate([narrow[0:1], jnp.zeros_like(narrow[0:1]), narrow[1:2]], 1)

    qkv, *mats = queries_keys_values(
        info, *hidden, heads, bias_heads, cot_out if plan.stays else None
    )
    cots = plan.gather(cot_out, mats.pop() if plan.stays else plan.pick(cot_out))
    at = lambda kind: lambda j: kind * HEADS // 2 + j
    if per == 1:
        sources = [(qkv, at(kind)) for kind in range(3)]
    else:
        kv = lax.all_gather(qkv[:, width:], "blk", axis=0, tiled=True, axis_index_groups=fleets)
        sources = [(qkv, at(0)), (kv, at(0)), (kv, at(1))]
    context_low, probs, sums = attend(info, sources, span)

    own_cls = lax.dynamic_index_in_dim(cot_cls, plan.passage, 0, keepdims=True).astype(F32)
    layer_kept, layer_other, top, grad_context, grad_resid, dense_sums = middle(
        info, hidden, cots, context_low, own_cls, dense, narrow[2:], bias_inner
    )
    part_wo, part_wi, part_wu, dense_vecs = dense.scatter([dense_sums])
    part_bo, part_g1, part_s1, part_bu, part_g2, part_s2 = [dense_vecs[t] for t in range(6)]
    part_bi = dense_vecs[6 : 6 + b_inner.size // share].reshape(-1)
    layer_other = plan.send_back(layer_other)
    tops = plan.all_blocks(top)[::per, 0, :]
    cls_part = lax.dynamic_slice_in_dim(tops, plan.me * share, share, 1)

    back = functools.partial(
        attend_back, info, sources, grad_context, context_low, sums, probs, span
    )
    give = functools.partial(input_grad, info, resid=grad_resid, mats=mats)
    if per == 1:
        most = back([(1, 1), (1, 0), (0, 1)], None)
        other, *layer_rows = give(
            most,
            out_shape=(block_len, width),
            dtype=BF16,
            kept=False,
            join=(layer_kept, layer_other) if plan.stays else (),
            events=(cls_part,),
        )
        layer_rows = layer_rows[0] if layer_rows else plan.join(info, layer_kept, layer_other)
        rest = back([(0, 0)], most, (other, layer_rows))
        other = plan.send_back(other)
    else:
        blocks = span * per // min(1024, span * per)
        grad_q, *grad_kv = back([(k, q) for k in range(blocks) for q in range(2)], None)
        most = [grad_q] + [
            lax.psum_scatter(g, "blk", scatter_dimension=0, tiled=True, axis_index_groups=fleets)
            for g in grad_kv
        ]
        (other,) = give(most, out_shape=(block_len, width), dtype=BF16, kept=False)
        other = plan.send_back(other)
        rest = most
        layer_rows = plan.join(info, layer_kept, layer_other)
    head_sums = head_grads(
        info, hidden, rest, heads.sums_of, 2 if heads.by_pairs else 1, (other,)
    )
    (kept,) = give(rest, out_shape=hidden[0].shape, dtype=F32, kept=True)
    grad_input = plan.join(info, kept, other)
    part_wq, part_wk, part_wv, head_vecs = heads.scatter(
        head_sums, (grad_input, part_wo, dense_vecs)
    )
    part_bq, part_bv = head_vecs[0], head_vecs[1]
    return (
        layer_rows,
        cls_part,
        grad_input,
        part_wq,
        part_wk,
        part_wv,
        part_wo,
        part_wi,
        part_wu,
        part_bq,
        part_bv,
        part_bo,
        part_g1,
        part_s1,
        part_bi,
        part_bu,
        part_g2,
        part_s2,
    )


def solution(mesh):
    rows = P("batch", "blk", None)
    mats = (P("batch", "blk"),) * 6
    vecs = (P("blk"),) * 9
    return jax.shard_map(
        on_device,
        mesh=mesh,
        in_specs=(rows, P("batch"), rows, P("batch", None)) + mats + vecs,
        out_specs=(rows, P("batch", "blk"), rows) + mats + vecs,
        check_vma=False,
    )
```
